32 devices in a mesh: fsdp: 4 (over x, core), seq: 8 (over z, y).
Axes of the slice: x: 2, y: 2, z: 4, core: 2. Of those that a mesh axis runs over, the one named last changes fastest.
Arguments:
- tokens: bfloat16 [6144, 2048], P(('fsdp', 'seq')), may hold values from -40 to 40
- bounds: int32 [4, 2], P('fsdp'), may hold values from 1 to 1535, as said below
- cotangent: bfloat16 [6144, 2048], P(('fsdp', 'seq')), may hold values from -6 to 6
- attn_gain: float32 [2048], replicated, may hold values from 0.25 to 1.75
- query_weight: bfloat16 [2048, 2048], P('fsdp'), may hold values from -0.125 to 0.125
- key_matrix: bfloat16 [2048, 512], P('fsdp'), may hold values from -0.125 to 0.125
- value_matrix: bfloat16 [2048, 512], P('fsdp'), may hold values from -0.125 to 0.125
- query_gain: float32 [64], replicated, may hold values from 1 to 1.6
- key_gain: float32 [64], replicated, may hold values from 1 to 1.6
- out_weight: bfloat16 [2048, 2048], P('fsdp'), may hold values from -2 to 2
- ffn_gain: float32 [2048], replicated, may hold values from 0.25 to 1.75
- gate_weight: bfloat16 [2048, 8192], P(None, 'fsdp'), may hold values from -0.125 to 0.125
- up_weight: bfloat16 [2048, 8192], P(None, 'fsdp'), may hold values from -0.125 to 0.125
- down_weight: bfloat16 [8192, 2048], P('fsdp'), may hold values from -0.0625 to 0.0625
Outputs:
- block_output: bfloat16 [6144, 2048], P(('fsdp', 'seq'))
- input_grad: bfloat16 [6144, 2048], P(('fsdp', 'seq'))
- residual: float32 [6144, 2048], P(('fsdp', 'seq'))
- attn_rms: float32 [6144], P(('fsdp', 'seq'))
- mlp_rms: float32 [6144], P(('fsdp', 'seq'))
- attn_gain_grad: float32 [2048], P(('fsdp', 'seq'))
- query_weight_grad: float32 [2048, 2048], P(('fsdp', 'seq'))
- key_weight_grad: float32 [2048, 512], P(('fsdp', 'seq'))
- value_weight_grad: float32 [2048, 512], P(('fsdp', 'seq'))
- query_gain_grad: float32 [64], replicated
- key_gain_grad: float32 [64], replicated
- out_weight_grad: float32 [2048, 2048], P(('fsdp', 'seq'))
- ffn_gain_grad: float32 [2048], P(('fsdp', 'seq'))
- gate_weight_grad: float32 [2048, 8192], P('seq', 'fsdp')
- up_weight_grad: float32 [2048, 8192], P('seq', 'fsdp')
- down_weight_grad: float32 [8192, 2048], P(('fsdp', 'seq'))
The draws below stay inside these ranges and needn't reach their ends.
Inputs may be any that keep to these rules, and one draw needn't show every extreme that they name: `bounds`: for each sequence b0 < 192 and b1 > 1344, so its second document covers tokens on every index of seq.
All inputs are finite; a program needn't handle non-finite values.
Results may differ from the reference program's by a relative error of at most 0.019.
Values may be sent and summed in bfloat16 or wider, within the bound.
No kernel may reach another device: no remote copies, remote signals or barrier semaphores. Data moves between devices by JAX's collectives and lax.ppermute only.
A program may use at most 512 MiB of HBM per device.

```python
import math
import jax
import jax.numpy as jnp
from jax import lax

MODEL_WIDTH = 2048
QUERY_HEADS = 32
KEY_VALUE_HEADS = 8
HEAD_SIZE = 64
FF = 8192
TOK_DEV = 192
SEQS = 4
SEQLEN = 1536
TOKENS = 6144


def draw_tokens(key, part):
    key = jax.random.fold_in(key, 11)
    keys = jax.random.split(key, 3)
    row_scale = jnp.exp(jax.random.uniform(keys[0], (TOKENS, 1), jnp.float32, -1.1513, 1.1513))
    column_scale = jnp.exp(jax.random.uniform(keys[1], (1, MODEL_WIDTH), jnp.float32, -1.1513, 1.1513))
    base = jax.random.truncated_normal(keys[2], -4.0, 4.0, (TOKENS, MODEL_WIDTH), jnp.float32)
    return jnp.clip(base * row_scale * column_scale, -40.0, 40.0).astype(jnp.bfloat16)


def draw_bounds(key, part):
    key = jax.random.fold_in(key, 5)
    first_key, second_key = jax.random.split(key)
    first_bound = jax.random.randint(first_key, (SEQS,), 0, TOK_DEV - 1)
    second_bound = jax.random.randint(second_key, (SEQS,), 0, TOK_DEV - 1)
    first_bound = first_bound - jnp.min(first_bound) + 1
    second_bound = SEQLEN - 1 - (second_bound - jnp.min(second_bound))
    return jnp.stack([first_bound, second_bound], axis=1).astype(jnp.int32)


def block_scale(rng, dims, pieces, least, top_value):
    gain = 1.0
    for dim, parts in pieces:
        heights = jax.random.uniform(jax.random.fold_in(jax.random.fold_in(rng, 6), dim), (parts,), jnp.float32, least / len(pieces), top_value / len(pieces))
        gain = gain * jnp.repeat(jnp.exp(heights), dims[dim] // parts).reshape((-1,) + (1,) * (len(dims) - 1 - dim))
    return gain


def noise(key, dims, deviation, bound, cuts=(), held_as=jnp.bfloat16):
    drawn = deviation * jax.random.normal(key, dims, jnp.float32)
    if cuts:
        drawn = drawn * block_scale(key, dims, cuts, -0.22, 0.18)
    return jnp.clip(drawn, -bound, bound).astype(held_as)


def setup_inputs(seed: int = 0) -> dict:
    key_list = jax.random.split(jax.random.key(seed), 15)
    return {
        "tokens": draw_tokens(jax.random.fold_in(key_list[14], 71), 0),
        "bounds": draw_bounds(jax.random.fold_in(key_list[14], 71), 0),
        "cotangent": noise(key_list[2], (TOKENS, MODEL_WIDTH), 1.0, 6.0, ((0, 32),)),
        "attn_gain": jnp.clip(1.0 + 0.15 * jax.random.normal(key_list[3], (MODEL_WIDTH,), jnp.float32), 0.25, 1.75),
        "query_weight": noise(key_list[4], (MODEL_WIDTH, QUERY_HEADS * HEAD_SIZE), MODEL_WIDTH ** -0.5, 0.125, ((0, 4),)),
        "key_matrix": noise(key_list[5], (MODEL_WIDTH, KEY_VALUE_HEADS * HEAD_SIZE), MODEL_WIDTH ** -0.5, 0.125, ((0, 4),)),
        "value_matrix": noise(key_list[6], (MODEL_WIDTH, KEY_VALUE_HEADS * HEAD_SIZE), MODEL_WIDTH ** -0.5, 0.125, ((0, 4),)),
        "query_gain": jnp.clip(jnp.exp(jax.random.uniform(key_list[7], (HEAD_SIZE,), jnp.float32, math.log(1.0), math.log(1.6))), 1.0, 1.6),
        "key_gain": jnp.clip(jnp.exp(jax.random.uniform(key_list[8], (HEAD_SIZE,), jnp.float32, math.log(1.0), math.log(1.6))), 1.0, 1.6),
        "out_weight": noise(key_list[9], (QUERY_HEADS * HEAD_SIZE, MODEL_WIDTH), 8 ** -0.5, 2.0, ((0, 4),)),
        "ffn_gain": jnp.clip(1.0 + 0.15 * jax.random.normal(key_list[10], (MODEL_WIDTH,), jnp.float32), 0.25, 1.75),
        "gate_weight": noise(key_list[11], (MODEL_WIDTH, FF), MODEL_WIDTH ** -0.5, 0.125, ((1, 4),)),
        "up_weight": noise(key_list[12], (MODEL_WIDTH, FF), MODEL_WIDTH ** -0.5, 0.125, ((1, 4),)),
        "down_weight": noise(key_list[13], (FF, MODEL_WIDTH), FF ** -0.5, 0.0625, ((0, 4),)),
    }


EPSILON = 1e-05
ROPE_BASE = 1000000.0
MASKED = -1e+30
HIGHEST = lax.Precision.HIGHEST

@jax.custom_vjp
def reduced_input(v):
    return lax.optimization_barrier(v.astype(jnp.bfloat16)).astype(jnp.float32)

@jax.custom_vjp
def reduced_backward(v):
    return v

def low_keep(v):
    return (reduced_input(v), None)

def low_pass(kept, grad):
    return (grad,)

def back_keep(v):
    return (v, None)

def back_low(kept, grad):
    return (reduced_input(grad),)
reduced_input.defvjp(low_keep, low_pass)
reduced_backward.defvjp(back_keep, back_low)

def matrix_product(left, right):
    return jnp.dot(left, right, precision=HIGHEST)

def rms_scale(values):
    return lax.rsqrt(lax.optimization_barrier(jnp.mean(values * values, axis=-1, keepdims=True)) + EPSILON)

def rotate(values, cosine, sine):
    half_dim = values.shape[-1] // 2
    lower_half = values[..., :half_dim]
    upper_half = values[..., half_dim:]
    return jnp.concatenate([lower_half * cosine - upper_half * sine, upper_half * cosine + lower_half * sine], axis=-1)

def doc_layout(bounds, token_length):
    positions = jnp.arange(token_length, dtype=jnp.int32)
    doc_ids = (positions >= bounds[0]).astype(jnp.int32) + (positions >= bounds[1]).astype(jnp.int32)
    starts = jnp.where(positions >= bounds[1], bounds[1], jnp.where(positions >= bounds[0], bounds[0], 0))
    frequency = ROPE_BASE ** (-(jnp.arange(HEAD_SIZE // 2, dtype=jnp.float32) * 2.0 / HEAD_SIZE))
    phases = (positions - starts).astype(jnp.float32)[:, None] * frequency[None, :]
    return (doc_ids, jnp.cos(phases)[:, None, :], jnp.sin(phases)[:, None, :])

def attend(queries, key_per_head, value_per_head, doc_ids):
    token_length = queries.shape[0]
    block_size = min(512, token_length)
    key_index = jnp.arange(token_length, dtype=jnp.int32)

    def one_block(start_row):
        row_queries = lax.dynamic_slice_in_dim(queries, start_row, block_size, 0)
        row_index = start_row + jnp.arange(block_size, dtype=jnp.int32)
        row_docs = lax.dynamic_slice_in_dim(doc_ids, start_row, block_size, 0)
        scores = jnp.einsum('qhd,khd->hqk', row_queries, key_per_head, precision=HIGHEST) * HEAD_SIZE ** (-0.5)
        scores = reduced_backward(scores)
        allowed = (key_index[None, :] <= row_index[:, None]) & (doc_ids[None, :] == row_docs[:, None])
        scores = jnp.where(allowed[None], scores, MASKED)
        row_max = lax.optimization_barrier(jnp.max(scores, axis=-1, keepdims=True))
        weights = jnp.exp(scores - row_max)
        probs = reduced_input(weights / lax.optimization_barrier(jnp.sum(weights, axis=-1, keepdims=True)))
        return jnp.einsum('hqk,khd->qhd', probs, value_per_head, precision=HIGHEST)
    starts = jnp.arange(token_length // block_size, dtype=jnp.int32) * block_size
    return lax.map(jax.checkpoint(one_block), starts).reshape(token_length, QUERY_HEADS, HEAD_SIZE)

def forward(inputs, bounds, attn_gain, query_weight, key_matrix, value_matrix, query_gain, key_gain, out_weight, ffn_gain, gate_weight, up_weight, down_weight):
    token_length = inputs.shape[0]
    doc_ids, cosine, sine = doc_layout(bounds, token_length)
    normalized_input = reduced_input(inputs * rms_scale(inputs) * attn_gain)
    queries = reduced_backward(matrix_product(normalized_input, query_weight)).reshape(token_length, QUERY_HEADS, HEAD_SIZE)
    key_row_matrix = reduced_backward(matrix_product(normalized_input, key_matrix)).reshape(token_length, KEY_VALUE_HEADS, HEAD_SIZE)
    value_row_matrix = reduced_backward(matrix_product(normalized_input, value_matrix)).reshape(token_length, KEY_VALUE_HEADS, HEAD_SIZE)
    queries = reduced_backward(reduced_input(rotate(queries * rms_scale(queries) * query_gain, cosine, sine)))
    key_row_matrix = reduced_input(rotate(key_row_matrix * rms_scale(key_row_matrix) * key_gain, cosine, sine))
    key_per_head = reduced_backward(jnp.repeat(key_row_matrix, QUERY_HEADS // KEY_VALUE_HEADS, axis=1))
    value_per_head = reduced_backward(jnp.repeat(reduced_input(value_row_matrix), QUERY_HEADS // KEY_VALUE_HEADS, axis=1))
    attended = reduced_backward(reduced_input(attend(queries, key_per_head, value_per_head, doc_ids)))
    residual = inputs + reduced_backward(matrix_product(attended.reshape(token_length, QUERY_HEADS * HEAD_SIZE), out_weight))
    inner = reduced_input(residual * rms_scale(residual) * ffn_gain)
    gate_act = reduced_backward(matrix_product(inner, gate_weight))
    up_act = reduced_backward(matrix_product(inner, up_weight))
    hidden = reduced_input(jax.nn.silu(gate_act) * up_act)
    return (residual + reduced_backward(matrix_product(hidden, down_weight)), residual)

def reference(tokens, bounds, cotangent, attn_gain, query_weight, key_matrix, value_matrix, query_gain, key_gain, out_weight, ffn_gain, gate_weight, up_weight, down_weight):
    params = tuple((param.astype(jnp.float32) for param in (attn_gain, query_weight, key_matrix, value_matrix, query_gain, key_gain, out_weight, ffn_gain, gate_weight, up_weight, down_weight)))
    inputs = tokens.astype(jnp.float32).reshape(SEQS, SEQLEN, MODEL_WIDTH)
    cotangents = cotangent.astype(jnp.float32).reshape(SEQS, SEQLEN, MODEL_WIDTH)

    def seq_step(totals, seq_item):
        seq_inputs, seq_bounds, seq_cotangent = seq_item

        def apply_block(values, *weights):
            return forward(values, seq_bounds, *weights)
        (block_out, residual), pullback = jax.vjp(apply_block, seq_inputs, *params)
        gradients = pullback((seq_cotangent, jnp.zeros_like(residual)))
        totals = tuple((left_sum + right_sum for left_sum, right_sum in zip(totals, gradients[1:])))
        first_rms = jnp.sqrt(lax.optimization_barrier(jnp.mean(seq_inputs * seq_inputs, axis=-1)) + EPSILON)
        second_rms = jnp.sqrt(lax.optimization_barrier(jnp.mean(residual * residual, axis=-1)) + EPSILON)
        return (totals, (block_out.astype(jnp.bfloat16), gradients[0].astype(jnp.bfloat16), residual, first_rms, second_rms))
    zero_grads = tuple((jnp.zeros(param.shape, jnp.float32) for param in params))
    totals, per_seq = lax.scan(seq_step, zero_grads, (inputs, bounds, cotangents))
    block_output = per_seq[0].reshape(TOKENS, MODEL_WIDTH)
    input_grad = per_seq[1].reshape(TOKENS, MODEL_WIDTH)
    residual = per_seq[2].reshape(TOKENS, MODEL_WIDTH)
    attn_rms = per_seq[3].reshape(TOKENS)
    mlp_rms = per_seq[4].reshape(TOKENS)
    return (block_output, input_grad, residual, attn_rms, mlp_rms, totals[0], totals[1], totals[2], totals[3], totals[4], totals[5], totals[6], totals[7], totals[8], totals[9], totals[10])
```

```python
import functools

import jax
import jax.numpy as jnp
from jax import lax
from jax.experimental import pallas as pl
from jax.experimental.pallas import tpu as pltpu
from jax.sharding import Mesh, PartitionSpec as P

HEAD_SIZE = 64
QUERY_HEADS = 32
KEY_VALUE_HEADS = 8
EPSILON = 1e-05
ROPE_BASE = 1000000.0
BIG = 30000.0
LANES = 128
BLOCK = 256
VMEM = 56 * 1024 * 1024

F32 = jnp.float32
BF16 = jnp.bfloat16
NT = (((1,), (1,)), ((), ()))
TN = (((0,), (0,)), ((), ()))


def dot(left, right, dims=(((1,), (0,)), ((), ()))):
    return lax.dot_general(left, right, dims, preferred_element_type=F32)


def swap_halves(values):
    half = values.shape[-1] // 2
    return jnp.concatenate([values[:, half:], values[:, :half]], axis=1)


def split_low(column):
    high = column.astype(BF16).astype(F32)
    return high, column - high


def project_kernel(heads, bounds_ref, x_ref, gain_ref, w_ref, head_gain_ref, cos_ref, sin_ref,
                   normed_ref, q_ref, k_ref, v_ref, unit_ref, scale_ref):
    rows = x_ref.shape[0]
    x = x_ref[...].astype(F32)
    scale = lax.rsqrt(jnp.mean(x * x, axis=1, keepdims=True) + EPSILON)
    normed = (x * scale * gain_ref[...]).astype(BF16)
    normed_ref[...] = normed
    pre = dot(normed, w_ref[...])
    cosine, sine = cos_ref[...], sin_ref[...]
    token = pl.program_id(0) * rows + lax.broadcasted_iota(jnp.int32, (rows, HEAD_SIZE), 0)
    doc = (token >= bounds_ref[0]).astype(jnp.int32) + (token >= bounds_ref[1]).astype(jnp.int32)
    lane = lax.broadcasted_iota(jnp.int32, (rows, HEAD_SIZE), 1)
    query_marks = jnp.where(lane == doc, 1.0, 0.0).astype(BF16)
    key_marks = jnp.where(
        lane < 3, jnp.where(lane == doc, 0.0, -BIG), jnp.where(lane < 5, 1.0, 0.0)
    ).astype(BF16)
    value_marks = jnp.where(lane < 2, 1.0, 0.0).astype(BF16)
    scales = jnp.zeros((rows, LANES), F32)
    scale_lane = lax.broadcasted_iota(jnp.int32, (rows, LANES), 1)
    for h in range(heads + 1):
        u = pre[:, h * HEAD_SIZE:(h + 1) * HEAD_SIZE]
        r = lax.rsqrt(jnp.mean(u * u, axis=1, keepdims=True) + EPSILON)
        unit = u * r
        unit_ref[:, h * HEAD_SIZE:(h + 1) * HEAD_SIZE] = unit
        scales = jnp.where(scale_lane == h, r, scales)
        g = unit * head_gain_ref[(1 if h == heads else 0):(2 if h == heads else 1), :HEAD_SIZE]
        rot = (g * cosine + swap_halves(g) * sine).astype(BF16)
        if h < heads:
            q_ref[h * rows:(h + 1) * rows, :HEAD_SIZE] = rot * 0.125
            q_ref[h * rows:(h + 1) * rows, HEAD_SIZE:] = query_marks
        else:
            k_ref[:, :HEAD_SIZE] = rot
            k_ref[:, HEAD_SIZE:] = key_marks
    v_ref[:, :HEAD_SIZE] = pre[:, (heads + 1) * HEAD_SIZE:].astype(BF16)
    v_ref[:, HEAD_SIZE:] = value_marks
    scale_ref[...] = scales


def project(heads, bounds, x, gain, w, head_gain, cosine, sine):
    tokens, width = x.shape
    rows = BLOCK
    cols = w.shape[1]
    row = lambda c: pl.BlockSpec((rows, c), lambda i, b: (i, 0))
    whole = lambda a: pl.BlockSpec(a.shape, lambda i, b: (0, 0))
    return pl.pallas_call(
        functools.partial(project_kernel, heads),
        grid_spec=pltpu.PrefetchScalarGridSpec(
            num_scalar_prefetch=1,
            grid=(tokens // rows,),
            in_specs=[row(width), whole(gain), whole(w), whole(head_gain), row(HEAD_SIZE), row(HEAD_SIZE)],
            out_specs=[
                row(width),
                pl.BlockSpec((heads * rows, LANES), lambda i, b: (i, 0)),
                row(LANES),
                row(LANES),
                row((heads + 1) * HEAD_SIZE),
                row(LANES),
            ],
        ),
        out_shape=[
            jax.ShapeDtypeStruct((tokens, width), BF16),
            jax.ShapeDtypeStruct((heads * tokens, LANES), BF16),
            jax.ShapeDtypeStruct((tokens, LANES), BF16),
            jax.ShapeDtypeStruct((tokens, LANES), BF16),
            jax.ShapeDtypeStruct((tokens, (heads + 1) * HEAD_SIZE), F32),
            jax.ShapeDtypeStruct((tokens, LANES), F32),
        ],
        compiler_params=pltpu.CompilerParams(vmem_limit_bytes=VMEM),
        cost_estimate=pl.CostEstimate(
            flops=2 * tokens * width * cols, bytes_accessed=4 * tokens * width + 2 * width * cols, transcendentals=0
        ),
        name="project",
    )(bounds, x, gain, w, head_gain, cosine, sine)


def attend_kernel(heads, q_ref, k_ref, v_ref, low_ref, out_ref, q2_ref):
    i = pl.program_id(0)
    rows = BLOCK
    q = q_ref[...]

    def step(j, total):
        start = pl.multiple_of(j * rows, rows)
        p = jnp.exp(dot(q, k_ref[pl.ds(start, rows), :], NT)).astype(BF16)
        return total + dot(p, v_ref[pl.ds(start, rows), :])

    total = lax.fori_loop(0, i, step, jnp.zeros((heads * rows, LANES), F32))
    start = pl.multiple_of(i * rows, rows)
    s = dot(q, k_ref[pl.ds(start, rows), :], NT)
    t_local = lax.broadcasted_iota(jnp.int32, s.shape, 0) % rows
    u_local = lax.broadcasted_iota(jnp.int32, s.shape, 1)
    p = jnp.where(u_local <= t_local, jnp.exp(s), 0.0).astype(BF16)
    total = total + dot(p, v_ref[pl.ds(start, rows), :])
    weight = total[:, HEAD_SIZE:HEAD_SIZE + 1]
    out = total[:, :HEAD_SIZE] / weight
    for h in range(heads):
        part = out[h * rows:(h + 1) * rows, :]
        out_ref[:, h * HEAD_SIZE:(h + 1) * HEAD_SIZE] = part
        low_ref[:, h * HEAD_SIZE:(h + 1) * HEAD_SIZE] = part.astype(BF16)
    high, low = split_low(-jnp.log(weight))
    lane = lax.broadcasted_iota(jnp.int32, q.shape, 1)
    q2_ref[...] = jnp.where(
        lane == HEAD_SIZE + 3, high.astype(BF16), jnp.where(lane == HEAD_SIZE + 4, low.astype(BF16), q)
    )


def attend(heads, q, k, v):
    tokens = k.shape[0]
    rows = BLOCK
    return pl.pallas_call(
        functools.partial(attend_kernel, heads),
        grid=(tokens // rows,),
        in_specs=[
            pl.BlockSpec((heads * rows, LANES), lambda i: (i, 0)),
            pl.BlockSpec((tokens, LANES), lambda i: (0, 0)),
            pl.BlockSpec((tokens, LANES), lambda i: (0, 0)),
        ],
        out_specs=[
            pl.BlockSpec((rows, heads * HEAD_SIZE), lambda i: (i, 0)),
            pl.BlockSpec((rows, heads * HEAD_SIZE), lambda i: (i, 0)),
            pl.BlockSpec((heads * rows, LANES), lambda i: (i, 0)),
        ],
        out_shape=[
            jax.ShapeDtypeStruct((tokens, heads * HEAD_SIZE), BF16),
            jax.ShapeDtypeStruct((tokens, heads * HEAD_SIZE), F32),
            jax.ShapeDtypeStruct((heads * tokens, LANES), BF16),
        ],
        compiler_params=pltpu.CompilerParams(vmem_limit_bytes=VMEM),
        cost_estimate=pl.CostEstimate(
            flops=16 * heads * tokens * tokens * LANES // 4, bytes_accessed=8 * tokens * LANES, transcendentals=0
        ),
        name="attend",
    )(q, k, v)


def attend_back_kernel(heads, q_ref, k_ref, v_ref, grad_ref, out_ref, unit_ref, scale_ref, head_gain_ref,
                       cos_ref, sin_ref, dqkv_ref, gains_ref, g_scr, dq_scr, dk_scr, dv_scr):
    rows = BLOCK
    tokens = k_ref.shape[0]
    blocks = tokens // rows
    wide = heads * rows

    def prepare(i, carry):
        start = pl.multiple_of(i * rows, rows)
        lane = lax.broadcasted_iota(jnp.int32, (rows, HEAD_SIZE), 1)
        for h in range(heads):
            cols = slice(h * HEAD_SIZE, (h + 1) * HEAD_SIZE)
            grad = grad_ref[pl.ds(start, rows), cols]
            delta = jnp.sum(grad.astype(F32) * out_ref[pl.ds(start, rows), cols], axis=1, keepdims=True)
            high, low = split_low(-delta)
            marks = jnp.where(lane == 0, high, jnp.where(lane == 1, low, 0.0)).astype(BF16)
            at = pl.ds(pl.multiple_of(i * wide + h * rows, rows), rows)
            g_scr[at, :HEAD_SIZE] = grad
            g_scr[at, HEAD_SIZE:] = marks
        at = pl.ds(pl.multiple_of(i * wide, wide), wide)
        dq_scr[at, :] = jnp.zeros((wide, LANES), F32)
        return carry

    lax.fori_loop(0, blocks, prepare, 0)

    def key_step(j, carry):
        start = pl.multiple_of(j * rows, rows)
        k = k_ref[pl.ds(start, rows), :]
        v = v_ref[pl.ds(start, rows), :]

        def pair(i, diagonal):
            at = pl.ds(pl.multiple_of(i * wide, wide), wide)
            q = q_ref[at, :]
            g = g_scr[at, :]
            p = jnp.exp(dot(k, q, NT))
            if diagonal:
                u_local = lax.broadcasted_iota(jnp.int32, p.shape, 0)
                t_local = lax.broadcasted_iota(jnp.int32, p.shape, 1) % rows
                p = jnp.where(u_local <= t_local, p, 0.0)
            dv = dot(p.astype(BF16), g)
            ds = (p * dot(v, g, NT)).astype(BF16)
            dk = dot(ds, q)
            dq_scr[at, :] += dot(ds, k, TN)
            return dk, dv

        def query_step(i, state):
            dk, dv = pair(i, False)
            return state[0] + dk, state[1] + dv

        dk, dv = lax.fori_loop(j + 1, blocks, query_step, pair(j, True))
        dk_scr[pl.ds(start, rows), :] = dk
        dv_scr[pl.ds(start, rows), :] = dv
        return carry

    lax.fori_loop(0, blocks, key_step, 0)

    def finish(i, carry):
        start = pl.multiple_of(i * rows, rows)
        at = pl.ds(start, rows)
        cosine, sine = cos_ref[at, :], sin_ref[at, :]
        scales = scale_ref[at, :]
        sums = list(carry)
        for h in range(heads + 1):
            cols = slice(h * HEAD_SIZE, (h + 1) * HEAD_SIZE)
            if h < heads:
                d = dq_scr[pl.ds(pl.multiple_of(i * wide + h * rows, rows), rows), :HEAD_SIZE] * 0.125
            else:
                d = dk_scr[at, :HEAD_SIZE]
            which = 0 if h < heads else 1
            e = d * cosine - swap_halves(d) * sine
            unit = unit_ref[at, cols]
            sums[which] = sums[which] + jnp.sum(e * unit, axis=0, keepdims=True)
            w = e * head_gain_ref[which:which + 1, :HEAD_SIZE]
            r = scales[:, h:h + 1]
            dqkv_ref[at, cols] = (r * (w - unit * jnp.mean(w * unit, axis=1, keepdims=True))).astype(BF16)
        dqkv_ref[at, (heads + 1) * HEAD_SIZE:] = dv_scr[at, :HEAD_SIZE].astype(BF16)
        return tuple(sums)

    zero = jnp.zeros((1, HEAD_SIZE), F32)
    q_sum, k_sum = lax.fori_loop(0, blocks, finish, (zero, zero))
    gains_ref[...] = jnp.zeros(gains_ref.shape, F32)
    gains_ref[0:1, :HEAD_SIZE] = q_sum
    gains_ref[0:1, HEAD_SIZE:] = k_sum


def attend_back(heads, q, k, v, grad, out, unit, scale, head_gain, cosine, sine):
    tokens = k.shape[0]
    return pl.pallas_call(
        functools.partial(attend_back_kernel, heads),
        out_shape=[
            jax.ShapeDtypeStruct((tokens, (heads + 2) * HEAD_SIZE), BF16),
            jax.ShapeDtypeStruct((8, LANES), F32),
        ],
        scratch_shapes=[
            pltpu.VMEM((heads * tokens, LANES), BF16),
            pltpu.VMEM((heads * tokens, LANES), F32),
            pltpu.VMEM((tokens, LANES), F32),
            pltpu.VMEM((tokens, LANES), F32),
        ],
        compiler_params=pltpu.CompilerParams(vmem_limit_bytes=VMEM),
        cost_estimate=pl.CostEstimate(
            flops=40 * heads * tokens * tokens * LANES // 4, bytes_accessed=16 * tokens * LANES, transcendentals=0
        ),
        name="attend_back",
    )(q, k, v, grad, out, unit, scale, head_gain, cosine, sine)


def per_device(
    tokens, bounds, cotangent, attn_gain, query_weight, key_matrix, value_matrix,
    query_gain, key_gain, out_weight, ffn_gain, gate_weight, up_weight, down_weight,
):
    fsdp = ("fo", "fi")
    seq = ("so", "si")
    every = fsdp + seq
    group = ("fo", "fi", "si")
    rows, width = tokens.shape
    f_count = lax.axis_size(fsdp)
    s_count = lax.axis_size(seq)
    z_count = lax.axis_size("so")
    f_index = lax.axis_index(fsdp)
    s_index = lax.axis_index(seq)
    z_index = lax.axis_index("so")
    y_index = lax.axis_index("si")
    length = rows * s_count
    heads = QUERY_HEADS // s_count
    copies = max(1, s_count // KEY_VALUE_HEADS)
    kv_cols = HEAD_SIZE
    assert KEY_VALUE_HEADS * copies == s_count
    q_cols = heads * HEAD_SIZE
    cols = q_cols + 2 * kv_cols

    all_cols = jnp.concatenate(
        [
            query_weight.reshape(-1, s_count, q_cols),
            jnp.repeat(key_matrix.reshape(-1, KEY_VALUE_HEADS, kv_cols), copies, axis=1),
            jnp.repeat(value_matrix.reshape(-1, KEY_VALUE_HEADS, kv_cols), copies, axis=1),
        ],
        axis=2,
    )
    own_cols = lax.dynamic_index_in_dim(all_cols, s_index, 1, keepdims=False)
    w_own = lax.all_gather(own_cols, fsdp, axis=0, tiled=True)
    x_full = lax.all_gather(tokens, seq, axis=0, tiled=True)
    c_group = lax.all_gather(cotangent, group, axis=0, tiled=True)
    w_all = lax.all_gather(all_cols.reshape(-1, s_count * cols), fsdp, axis=0, tiled=True)
    out_full = lax.all_gather(out_weight, fsdp, axis=0, tiled=True)

    ids = jnp.arange(length, dtype=jnp.int32)
    b0, b1 = bounds[0, 0], bounds[0, 1]
    starts = jnp.where(ids >= b1, b1, jnp.where(ids >= b0, b0, 0))
    frequency = ROPE_BASE ** (-(jnp.arange(HEAD_SIZE // 2, dtype=F32) * 2.0 / HEAD_SIZE))
    phases = (ids - starts).astype(F32)[:, None] * frequency[None, :]
    cosine, sine = jnp.cos(phases), jnp.sin(phases)
    cos2 = jnp.concatenate([cosine, cosine], axis=1)
    sin2 = jnp.concatenate([-sine, sine], axis=1)
    head_gain = jnp.zeros((8, LANES), F32).at[0, :HEAD_SIZE].set(query_gain).at[1, :HEAD_SIZE].set(key_gain)

    normed, q, k, v, unit, scale = project(
        heads, bounds[0], x_full, attn_gain[None, :], w_own, head_gain, cos2, sin2
    )
    attended_low, attended, q2 = attend(heads, q, k, v)
    heads_out = lax.all_to_all(attended_low, seq, split_axis=0, concat_axis=1, tiled=True)

    inputs = tokens.astype(F32)
    square_one = jnp.mean(inputs * inputs, axis=1, keepdims=True)
    scale_one = lax.rsqrt(square_one + EPSILON)
    residual = inputs + dot(heads_out, out_full)
    square_two = jnp.mean(residual * residual, axis=1, keepdims=True)
    scale_two = lax.rsqrt(square_two + EPSILON)
    inner = (residual * scale_two * ffn_gain).astype(BF16)

    units = gate_weight.shape[1]
    part = units // s_count
    mine = z_count * part
    gate_own = lax.dynamic_index_in_dim(
        gate_weight.reshape(width, z_count, 2, part), y_index, 2, keepdims=False
    ).reshape(width, mine)
    up_own = lax.dynamic_index_in_dim(
        up_weight.reshape(width, z_count, 2, part), y_index, 2, keepdims=False
    ).reshape(width, mine)
    down_own = lax.dynamic_index_in_dim(
        down_weight.reshape(z_count, 2, part, width), y_index, 1, keepdims=False
    ).reshape(mine, width)
    d_hidden = dot(c_group, down_own, NT)
    inner_group = lax.all_gather(inner, group, axis=0, tiled=True)
    gate = dot(inner_group, gate_own)
    up = dot(inner_group, up_own)
    sigma = jax.nn.sigmoid(gate)
    active = gate * sigma
    hidden = (active * up).astype(BF16)
    d_gate = (d_hidden * up * (sigma * (1.0 + gate * (1.0 - sigma)))).astype(BF16)
    d_up = (d_hidden * active).astype(BF16)
    d_inner_part = (dot(d_gate, gate_own, NT) + dot(d_up, up_own, NT)).astype(BF16)
    d_inner = lax.psum_scatter(d_inner_part, group, scatter_dimension=0, tiled=True).astype(F32)
    mlp_part = dot(hidden, down_own).astype(BF16)
    mlp_out = lax.psum_scatter(mlp_part, group, scatter_dimension=0, tiled=True).astype(F32)
    block_output = (residual + mlp_out).astype(BF16)

    down_part = dot(hidden, c_group, TN).astype(BF16)
    gate_part = dot(inner_group, d_gate, TN).astype(BF16)
    up_part = dot(inner_group, d_up, TN).astype(BF16)
    down_grad = lax.psum_scatter(down_part, "so", scatter_dimension=0, tiled=True).astype(F32)

    def owner_rows(partial):
        rows_here = lax.psum_scatter(partial, "so", scatter_dimension=0, tiled=True)
        spread = lax.all_to_all(
            rows_here.reshape(2, width // s_count, mine), "si", split_axis=0, concat_axis=0, tiled=True
        )
        return (
            spread.reshape(2, width // s_count, z_count, part)
            .transpose(1, 2, 0, 3)
            .reshape(width // s_count, units)
            .astype(F32)
        )

    gate_grad = owner_rows(gate_part)
    up_grad = owner_rows(up_part)

    ffn_part = jnp.sum(d_inner * residual * scale_two, axis=0)
    ffn_gain_grad = lax.psum_scatter(ffn_part, every, scatter_dimension=0, tiled=True)
    weighted = d_inner * ffn_gain
    d_residual = cotangent.astype(F32) + scale_two * (
        weighted - residual * scale_two * scale_two * jnp.mean(weighted * residual, axis=1, keepdims=True)
    )
    d_branch = d_residual.astype(BF16)
    d_heads = dot(d_branch, out_full, NT).astype(BF16)
    d_attended = lax.all_to_all(d_heads, seq, split_axis=1, concat_axis=0, tiled=True)

    attended_cols = lax.all_to_all(heads_out, fsdp, split_axis=1, concat_axis=0, tiled=True)
    branch_group = lax.all_gather(d_branch, fsdp, axis=0, tiled=True)
    out_part = dot(attended_cols, branch_group, TN).astype(BF16)
    out_grad = lax.psum_scatter(out_part, seq, scatter_dimension=0, tiled=True).astype(F32)

    d_qkv, gain_parts = attend_back(
        heads, q2, k, v, d_attended, attended, unit, scale, head_gain, cos2, sin2
    )
    gain_sums = lax.psum(gain_parts[0], every)

    proj_part = dot(normed, d_qkv, TN).astype(BF16)
    proj_rows = lax.psum_scatter(proj_part, fsdp, scatter_dimension=0, tiled=True)
    proj_grad = lax.all_to_all(proj_rows, seq, split_axis=0, concat_axis=1, tiled=True).astype(F32)
    own_rows = proj_grad.shape[0]
    by_device = proj_grad.reshape(own_rows, s_count, cols)
    query_grad = by_device[:, :, :q_cols].reshape(own_rows, s_count * q_cols)

    def fold(values):
        return values.reshape(own_rows, KEY_VALUE_HEADS, copies, kv_cols).sum(axis=2).reshape(own_rows, -1)

    key_grad = fold(by_device[:, :, q_cols:q_cols + kv_cols])
    value_grad = fold(by_device[:, :, q_cols + kv_cols:])

    d_tok = lax.all_to_all(d_qkv, seq, split_axis=0, concat_axis=1, tiled=True)
    d_normed = dot(d_tok, w_all, NT)
    attn_part = jnp.sum(d_normed * inputs * scale_one, axis=0)
    attn_gain_grad = lax.psum_scatter(attn_part, every, scatter_dimension=0, tiled=True)
    weighted = d_normed * attn_gain
    input_grad = (
        d_residual
        + scale_one
        * (weighted - inputs * scale_one * scale_one * jnp.mean(weighted * inputs, axis=1, keepdims=True))
    ).astype(BF16)
    attn_rms = jnp.sqrt(square_one + EPSILON)[:, 0]
    mlp_rms = jnp.sqrt(square_two + EPSILON)[:, 0]
    return (
        block_output, input_grad, residual, attn_rms, mlp_rms, attn_gain_grad,
        query_grad, key_grad, value_grad, gain_sums[:HEAD_SIZE], gain_sums[HEAD_SIZE:],
        out_grad, ffn_gain_grad, gate_grad, up_grad, down_grad,
    )


def solution(mesh):
    f_count, s_count = mesh.shape["fsdp"], mesh.shape["seq"]
    fine = Mesh(mesh.devices.reshape(f_count // 2, 2, s_count // 2, 2), ("fo", "fi", "so", "si"))
    f, s = ("fo", "fi"), ("so", "si")
    every = P(f + s, None)
    vector = P(f + s)
    placed = (
        every, P(f, None), every, P(), P(f, None), P(f, None), P(f, None), P(), P(),
        P(f, None), P(), P(None, f), P(None, f), P(f, None),
    )
    return jax.shard_map(
        per_device,
        mesh=fine,
        in_specs=placed,
        out_specs=(
            every, every, every, vector, vector, vector, every, every, every, P(), P(),
            every, vector, P(s, f), P(s, f), every,
        ),
        check_vma=False,
    )
```

```python
import functools

import jax
import jax.numpy as jnp
from jax import lax
from jax.experimental import pallas as pl
from jax.experimental.pallas import tpu as pltpu
from jax.sharding import Mesh, PartitionSpec as P

HEAD_SIZE = 64
QUERY_HEADS = 32
KEY_VALUE_HEADS = 8
EPSILON = 1e-05
ROPE_BASE = 1000000.0
BIG = 30000.0
LANES = 128
BLOCK = 256
VMEM = 60 * 1024 * 1024
COST = pl.CostEstimate(flops=1000, bytes_accessed=1000, transcendentals=0)

F32 = jnp.float32
BF16 = jnp.bfloat16
NT = (((1,), (1,)), ((), ()))
TN = (((0,), (0,)), ((), ()))


def dot(left, right, dims=(((1,), (0,)), ((), ()))):
    return lax.dot_general(left, right, dims, preferred_element_type=F32)


def split_low(values):
    high = values.astype(BF16)
    return high, (values - high.astype(F32)).astype(BF16)


def head_means(values, ones):
    high, low = split_low(values)
    return (dot(high, ones) + dot(low, ones)) * (1.0 / HEAD_SIZE)


def head_ones():
    row = lax.broadcasted_iota(jnp.int32, (LANES, LANES), 0) // HEAD_SIZE
    col = lax.broadcasted_iota(jnp.int32, (LANES, LANES), 1) // HEAD_SIZE
    return jnp.where(row == col, 1.0, 0.0).astype(BF16)


def swap_halves(values):
    lane = lax.broadcasted_iota(jnp.int32, values.shape, 1) % HEAD_SIZE
    half = HEAD_SIZE // 2
    return jnp.where(
        lane < half, pltpu.roll(values, LANES - half, 1), pltpu.roll(values, half, 1)
    )


def project_kernel(heads, count, fresh, index_ref, bounds_ref, *refs):
    x_refs = refs[:count]
    gain_ref, w_ref, head_gain_ref, cos_ref, sin_ref = refs[count:count + 5]
    refs = refs[count + 5 + (0 if fresh else 6):]
    normed_ref, q_ref, k_ref, v_ref, unit_ref, scale_ref, x_scr = refs
    i = pl.program_id(0)
    rows = x_scr.shape[0]
    for r in range(count):
        @pl.when(i == r)
        def _(r=r):
            x_scr[...] = x_refs[r][...]

    x = x_scr[...].astype(F32)
    scale = lax.rsqrt(jnp.mean(x * x, axis=1, keepdims=True) + EPSILON)
    normed = (x * scale * gain_ref[...]).astype(BF16)
    normed_ref[...] = normed
    pre = dot(normed, w_ref[...])
    cosine, sine = cos_ref[...], sin_ref[...]
    shape = (rows, LANES)
    token = index_ref[i] * rows + lax.broadcasted_iota(jnp.int32, shape, 0)
    doc = (token >= bounds_ref[0]).astype(jnp.int32) + (token >= bounds_ref[1]).astype(jnp.int32)
    lane = lax.broadcasted_iota(jnp.int32, shape, 1)
    mark = lane - HEAD_SIZE
    query_marks = jnp.where(mark == doc, 1.0, 0.0)
    key_marks = jnp.where(mark < 3, jnp.where(mark == doc, 0.0, -BIG), jnp.where(mark < 5, 1.0, 0.0))
    value_marks = jnp.where(mark < 2, 1.0, 0.0)
    ones = head_ones()

    def place(values, segment, marks):
        group = values if segment % 2 == 0 else pltpu.roll(values, HEAD_SIZE, 1)
        return jnp.where(lane < HEAD_SIZE, group, marks).astype(BF16)

    for g in range(pre.shape[1] // LANES):
        cols = slice(g * LANES, (g + 1) * LANES)
        u = pre[:, cols]
        r = lax.rsqrt(head_means(u * u, ones) + EPSILON)
        unit = u * r
        unit_ref[:, cols] = unit
        scale_ref[:, cols] = r
        gained = unit * head_gain_ref[0:1, cols]
        rot = (gained * cosine + swap_halves(gained) * sine).astype(BF16).astype(F32)
        for segment in (2 * g, 2 * g + 1):
            if segment < heads:
                q_ref[segment] = place(rot * 0.125, segment, query_marks)
            elif segment == heads:
                k_ref[...] = place(rot, segment, key_marks)
            elif segment == heads + 1:
                v_ref[...] = place(u, segment, value_marks)


def project(heads, blocks, index, bounds, gain, w, head_gain, cosine, sine, length, held=None):
    rows, width = blocks[0].shape
    count = len(blocks)
    cols = w.shape[1]
    row = lambda c: pl.BlockSpec((rows, c), lambda i, n, b: (n[i], 0))
    whole = lambda a: pl.BlockSpec(a.shape, lambda i, n, b: (0, 0))
    fresh = held is None
    held = () if fresh else held
    outs = [
        jax.ShapeDtypeStruct((length, width), BF16),
        jax.ShapeDtypeStruct((heads, length, LANES), BF16),
        jax.ShapeDtypeStruct((length, LANES), BF16),
        jax.ShapeDtypeStruct((length, LANES), BF16),
        jax.ShapeDtypeStruct((length, cols), F32),
        jax.ShapeDtypeStruct((length, cols), F32),
    ]
    tokens = rows * count
    return pl.pallas_call(
        functools.partial(project_kernel, heads, count, fresh),
        grid_spec=pltpu.PrefetchScalarGridSpec(
            num_scalar_prefetch=2,
            grid=(count,),
            in_specs=[whole(b) for b in blocks]
            + [whole(gain), whole(w), whole(head_gain), row(LANES), row(LANES)]
            + [pl.BlockSpec(memory_space=pl.ANY)] * len(held),
            out_specs=[
                row(width),
                pl.BlockSpec((heads, rows, LANES), lambda i, n, b: (0, n[i], 0)),
                row(LANES),
                row(LANES),
                row(cols),
                row(cols),
            ],
            scratch_shapes=[pltpu.VMEM((rows, width), BF16)],
        ),
        out_shape=outs,
        input_output_aliases={2 + count + 5 + n: n for n in range(len(held))},
        compiler_params=pltpu.CompilerParams(vmem_limit_bytes=VMEM),
        cost_estimate=COST,
        name="project",
    )(index, bounds, *blocks, gain, w, head_gain, cosine, sine, *held)


def attend_kernel(heads, q_ref, k_ref, v_ref, low_ref, out_ref, q2_ref):
    i = pl.program_id(0)
    rows = BLOCK
    q = q_ref[...].reshape(heads * rows, LANES)

    def step(j, total):
        start = pl.multiple_of(j * rows, rows)
        p = jnp.exp(dot(q, k_ref[pl.ds(start, rows), :], NT)).astype(BF16)
        return total + dot(p, v_ref[pl.ds(start, rows), :])

    total = lax.fori_loop(0, i, step, jnp.zeros((heads * rows, LANES), F32))
    start = pl.multiple_of(i * rows, rows)
    s = dot(q, k_ref[pl.ds(start, rows), :], NT)
    t_local = lax.broadcasted_iota(jnp.int32, s.shape, 0) % rows
    u_local = lax.broadcasted_iota(jnp.int32, s.shape, 1)
    p = jnp.where(u_local <= t_local, jnp.exp(s), 0.0).astype(BF16)
    total = total + dot(p, v_ref[pl.ds(start, rows), :])
    weight = total[:, HEAD_SIZE:HEAD_SIZE + 1]
    out = total[:, :HEAD_SIZE] / weight
    for h in range(heads):
        part = out[h * rows:(h + 1) * rows, :]
        out_ref[:, h * HEAD_SIZE:(h + 1) * HEAD_SIZE] = part
        low_ref[:, h * HEAD_SIZE:(h + 1) * HEAD_SIZE] = part.astype(BF16)
    high, low = split_low(-jnp.log(weight))
    lane = lax.broadcasted_iota(jnp.int32, q.shape, 1)
    q2 = jnp.where(lane == HEAD_SIZE + 3, high, jnp.where(lane == HEAD_SIZE + 4, low, q))
    q2_ref[...] = q2.reshape(heads, rows, LANES)


def attend(heads, q, k, v):
    tokens = k.shape[0]
    rows = BLOCK
    return pl.pallas_call(
        functools.partial(attend_kernel, heads),
        grid=(tokens // rows,),
        in_specs=[
            pl.BlockSpec((heads, rows, LANES), lambda i: (0, i, 0)),
            pl.BlockSpec((tokens, LANES), lambda i: (0, 0)),
            pl.BlockSpec((tokens, LANES), lambda i: (0, 0)),
        ],
        out_specs=[
            pl.BlockSpec((rows, heads * HEAD_SIZE), lambda i: (i, 0)),
            pl.BlockSpec((rows, heads * HEAD_SIZE), lambda i: (i, 0)),
            pl.BlockSpec((heads, rows, LANES), lambda i: (0, i, 0)),
        ],
        out_shape=[
            jax.ShapeDtypeStruct((tokens, heads * HEAD_SIZE), BF16),
            jax.ShapeDtypeStruct((tokens, heads * HEAD_SIZE), F32),
            jax.ShapeDtypeStruct((heads, tokens, LANES), BF16),
        ],
        compiler_params=pltpu.CompilerParams(vmem_limit_bytes=VMEM),
        cost_estimate=COST,
        name="attend",
    )(q, k, v)


def attend_back_kernel(heads, q_ref, k_ref, v_ref, grad_ref, out_ref, unit_ref, scale_ref, head_gain_ref,
                       cos_ref, sin_ref, dqkv_ref, gains_ref, g_scr, dq_scr, dk_scr, dv_scr):
    rows = BLOCK
    tokens = k_ref.shape[0]
    blocks = tokens // rows
    wide = heads * rows

    def prepare(i, carry):
        at = pl.ds(pl.multiple_of(i * rows, rows), rows)
        lane = lax.broadcasted_iota(jnp.int32, (rows, HEAD_SIZE), 1)
        for h in range(heads):
            cols = slice(h * HEAD_SIZE, (h + 1) * HEAD_SIZE)
            grad = grad_ref[at, cols]
            delta = jnp.sum(grad.astype(F32) * out_ref[at, cols], axis=1, keepdims=True)
            high, low = split_low(-delta)
            g_scr[h, at, :HEAD_SIZE] = grad
            g_scr[h, at, HEAD_SIZE:] = jnp.where(lane == 0, high, jnp.where(lane == 1, low, jnp.zeros_like(low)))
        dq_scr[:, at, :] = jnp.zeros((heads, rows, LANES), F32)
        return carry

    lax.fori_loop(0, blocks, prepare, 0)

    def key_step(j, carry):
        start = pl.multiple_of(j * rows, rows)
        k = k_ref[pl.ds(start, rows), :]
        v = v_ref[pl.ds(start, rows), :]

        def pair(i, diagonal):
            at = pl.ds(pl.multiple_of(i * rows, rows), rows)
            q = q_ref[:, at, :].reshape(wide, LANES)
            g = g_scr[:, at, :].reshape(wide, LANES)
            p = jnp.exp(dot(k, q, NT))
            if diagonal:
                u_local = lax.broadcasted_iota(jnp.int32, p.shape, 0)
                t_local = lax.broadcasted_iota(jnp.int32, p.shape, 1) % rows
                p = jnp.where(u_local <= t_local, p, 0.0)
            dv = dot(p.astype(BF16), g)
            ds = (p * dot(v, g, NT)).astype(BF16)
            dk = dot(ds, q)
            dq_scr[:, at, :] += dot(ds, k, TN).reshape(heads, rows, LANES)
            return dk, dv

        def query_step(i, state):
            dk, dv = pair(i, False)
            return state[0] + dk, state[1] + dv

        dk, dv = lax.fori_loop(j + 1, blocks, query_step, pair(j, True))
        dk_scr[pl.ds(start, rows), :] = dk
        dv_scr[pl.ds(start, rows), :] = dv
        return carry

    lax.fori_loop(0, blocks, key_step, 0)
    groups = unit_ref.shape[1] // LANES
    ones = head_ones()

    def finish(i, carry):
        at = pl.ds(pl.multiple_of(i * rows, rows), rows)
        cosine, sine = cos_ref[at, :], sin_ref[at, :]
        lane = lax.broadcasted_iota(jnp.int32, (rows, LANES), 1)

        def segment_of(s):
            if s < heads:
                return dq_scr[s, at, :] * 0.125
            return (dk_scr if s == heads else dv_scr)[at, :]

        sums = list(carry)
        for g in range(groups):
            cols = slice(g * LANES, (g + 1) * LANES)
            first = segment_of(2 * g)
            last = segment_of(2 * g + 1) if 2 * g + 1 < heads + 2 else first
            d = jnp.where(lane < HEAD_SIZE, first, pltpu.roll(last, HEAD_SIZE, 1))
            e = d * cosine - swap_halves(d) * sine
            unit = unit_ref[at, cols]
            sums[g] = sums[g] + jnp.sum(e * unit, axis=0, keepdims=True)
            w = e * head_gain_ref[0:1, cols]
            normal = scale_ref[at, cols] * (w - unit * head_means(w * unit, ones))
            is_value = lane + g * LANES >= (heads + 1) * HEAD_SIZE
            dqkv_ref[at, cols] = jnp.where(is_value, d, normal).astype(BF16)
        return tuple(sums)

    zero = jnp.zeros((1, LANES), F32)
    sums = lax.fori_loop(0, blocks, finish, (zero,) * groups)
    gains_ref[...] = jnp.zeros(gains_ref.shape, F32)
    for g in range(groups):
        gains_ref[0:1, g * LANES:(g + 1) * LANES] = sums[g]


def attend_back(heads, q, k, v, grad, out, unit, scale, head_gain, cosine, sine):
    tokens = k.shape[0]
    cols = unit.shape[1]
    return pl.pallas_call(
        functools.partial(attend_back_kernel, heads),
        out_shape=[
            jax.ShapeDtypeStruct((tokens, cols), BF16),
            jax.ShapeDtypeStruct((8, cols), F32),
        ],
        scratch_shapes=[
            pltpu.VMEM((heads, tokens, LANES), BF16),
            pltpu.VMEM((heads, tokens, LANES), F32),
            pltpu.VMEM((tokens, LANES), F32),
            pltpu.VMEM((tokens, LANES), F32),
        ],
        compiler_params=pltpu.CompilerParams(vmem_limit_bytes=VMEM),
        cost_estimate=COST,
        name="attend_back",
    )(q, k, v, grad, out, unit, scale, head_gain, cosine, sine)


def feed_kernel(layouts, weight_count, index_ref, *refs):
    tiles = sum(layouts[0])
    sides = []
    for layout in layouts:
        others = refs[tiles:tiles + len(layout)]
        sides.append((refs[:tiles], [(o, t) for o, count in zip(others, layout) for t in range(count)]))
        refs = refs[tiles + len(layout):]
    gate_ref, up_ref, down_ref = refs[:3]
    da_ref, db_ref, ma_ref, mb_ref, hidden_ref, dgu_ref, x_scr, c_scr, gu_scr, down_scr, sem, w_sem = refs[3:]
    i = pl.program_id(0)
    half = x_scr.shape[1] // 2

    def copies(t):
        slot = t % 2
        found = []
        for (own, others), scratch, which in ((sides[0], x_scr, 0), (sides[1], c_scr, 1)):
            other, place = others[t]
            found.append(
                pltpu.make_async_copy(own[t], scratch.at[slot, pl.ds(0, half)], sem.at[slot, which, 0])
            )
            found.append(
                pltpu.make_async_copy(
                    other.at[pl.ds(place * half, half)],
                    scratch.at[slot, pl.ds(half, half)],
                    sem.at[slot, which, 1],
                )
            )
        return found

    mine = hidden_ref.shape[1]
    part = mine // weight_count

    def weight_copies(n):
        at = pl.ds(pl.multiple_of(index_ref[n] * part, part), part)
        return [
            pltpu.make_async_copy(gate_ref.at[:, at], gu_scr.at[:, pl.ds(n * part, part)], w_sem.at[n, 0]),
            pltpu.make_async_copy(up_ref.at[:, at], gu_scr.at[:, pl.ds(mine + n * part, part)], w_sem.at[n, 1]),
            pltpu.make_async_copy(down_ref.at[at], down_scr.at[pl.ds(n * part, part)], w_sem.at[n, 2]),
        ]

    for t in range(tiles):
        @pl.when(i == t)
        def _(t=t):
            if t == 0:
                needed = copies(0) + [copy for n in range(weight_count) for copy in weight_copies(n)]
                for copy in needed:
                    copy.start()
            else:
                needed = copies(t)
            if t + 1 < tiles:
                for copy in copies(t + 1):
                    copy.start()
            for copy in needed:
                copy.wait()

    slot = lax.rem(i, 2)
    both = dot(x_scr[slot], gu_scr[...])
    gate, up = both[:, :mine], both[:, mine:]
    d_hidden = dot(c_scr[slot], down_scr[...], NT)
    sigma = 1.0 / (1.0 + jnp.exp(-gate))
    active = gate * sigma
    hidden = (active * up).astype(BF16)
    hidden_ref[...] = hidden
    dgu_ref[:, :mine] = (d_hidden * up * (sigma * (1.0 + gate * (1.0 - sigma)))).astype(BF16)
    dgu_ref[:, mine:] = (d_hidden * active).astype(BF16)
    d_inner = dot(dgu_ref[...], gu_scr[...], NT)
    mlp = dot(hidden, down_scr[...])
    da_ref[0] = d_inner[:half].astype(BF16)
    db_ref[0] = d_inner[half:].astype(BF16)
    ma_ref[0] = mlp[:half].astype(BF16)
    mb_ref[0] = mlp[half:].astype(BF16)


def feed(x_stage, c_stage, index, weights, part):
    (x_own, x_others), (c_own, c_others) = x_stage, c_stage
    tiles = len(x_own)
    half = x_own[0].shape[0]
    rows = 2 * half
    gate, up, down = weights
    width = gate.shape[0]
    blocks = index.shape[0]
    mine = blocks * part
    halves = pl.BlockSpec((1, half, width), lambda i, n: (i, 0, 0))
    return pl.pallas_call(
        functools.partial(
            feed_kernel, tuple(tuple(o.shape[0] // half for o in others) for others in (x_others, c_others)), blocks
        ),
        grid_spec=pltpu.PrefetchScalarGridSpec(
            num_scalar_prefetch=1,
            grid=(tiles,),
            in_specs=[pl.BlockSpec(memory_space=pl.ANY)] * (2 * tiles + len(x_others) + len(c_others) + 3),
            out_specs=[halves] * 4
            + [
                pl.BlockSpec((rows, mine), lambda i, n: (i, 0)),
                pl.BlockSpec((rows, 2 * mine), lambda i, n: (i, 0)),
            ],
            scratch_shapes=[
                pltpu.VMEM((2, rows, width), BF16),
                pltpu.VMEM((2, rows, width), BF16),
                pltpu.VMEM((width, 2 * mine), BF16),
                pltpu.VMEM((mine, width), BF16),
                pltpu.SemaphoreType.DMA((2, 2, 2)),
                pltpu.SemaphoreType.DMA((blocks, 3)),
            ],
        ),
        out_shape=[jax.ShapeDtypeStruct((tiles, half, width), BF16)] * 4
        + [
            jax.ShapeDtypeStruct((tiles * rows, mine), BF16),
            jax.ShapeDtypeStruct((tiles * rows, 2 * mine), BF16),
        ],
        compiler_params=pltpu.CompilerParams(vmem_limit_bytes=VMEM),
        cost_estimate=COST,
        name="feed",
    )(index, *x_own, *x_others, *c_own, *c_others, gate, up, down)


def stage_arrays(stages):
    arrays, layout = [], []
    for own, others in stages:
        half = own[0].shape[0]
        arrays += list(own) + list(others)
        layout.append((half, len(own), tuple(o.shape[0] // half for o in others)))
    return arrays, tuple(layout)


def stack_rows(refs, layout, scratch):
    at = row = 0
    for half, tiles, others in layout:
        places = [(at + tiles + n, t) for n, count in enumerate(others) for t in range(count)]
        for t, (other, place) in enumerate(places):
            scratch[row:row + half, :] = refs[at + t][...]
            scratch[row + half:row + 2 * half, :] = refs[other][place * half:(place + 1) * half, :]
            row += 2 * half
        at += tiles + len(others)


def gate_grad_kernel(array_count, layout, far, index_ref, *refs):
    arrays, refs = refs[:array_count], refs[array_count:]
    rights, outs, scratch = refs[:len(layout)], refs[len(layout):-1], refs[-1]
    stack_rows(arrays, layout, scratch)
    row = 0
    total = None
    for right in rights:
        size = right.shape[0]
        term = dot(scratch[row:row + size, :], right[...], TN)
        total = term if total is None else total + term
        row += size
    total = total.astype(BF16)
    mine = total.shape[1] // 2
    steps = pl.num_programs(0) // far
    for k in range(far):
        @pl.when(pl.program_id(0) // steps == far - 1 - k)
        def _(k=k):
            outs[k][...] = total[:, :mine]
            outs[far + k][...] = total[:, mine:]


def gate_grad(stages, rights, za, far):
    arrays, layout = stage_arrays(stages)
    width = arrays[0].shape[1]
    units = rights[0].shape[1]
    rows = sum(r.shape[0] for r in rights)
    step = min(256, width // far)
    steps = width // far // step
    block = lambda i, n: (n[0] ^ (far - 1 - i // steps)) * steps + i % steps
    out = lambda k: pl.BlockSpec(
        (step, units // 2), lambda i, n: (jnp.clip(i - (far - 1 - k) * steps, 0, steps - 1), 0)
    )
    return pl.pallas_call(
        functools.partial(gate_grad_kernel, len(arrays), layout, far),
        grid_spec=pltpu.PrefetchScalarGridSpec(
            num_scalar_prefetch=1,
            grid=(width // step,),
            in_specs=[pl.BlockSpec((p.shape[0], step), lambda i, n: (0, block(i, n))) for p in arrays]
            + [pl.BlockSpec(r.shape, lambda i, n: (0, 0)) for r in rights],
            out_specs=[out(k) for k in range(far)] * 2,
            scratch_shapes=[pltpu.VMEM((rows, step), BF16)],
        ),
        out_shape=[jax.ShapeDtypeStruct((width // far, units // 2), BF16)] * (2 * far),
        compiler_params=pltpu.CompilerParams(vmem_limit_bytes=VMEM),
        cost_estimate=COST,
        name="gate_grad",
    )(za.astype(jnp.int32).reshape(1), *arrays, *rights)


def down_grad_kernel(array_count, layout, *refs):
    arrays, refs = refs[:array_count], refs[array_count:]
    lefts, (out_ref, left_scr, scratch) = refs[:len(layout)], refs[len(layout):]

    @pl.when(pl.program_id(0) == 0)
    def _():
        col = 0
        for left in lefts:
            size = left.shape[0]
            left_scr[:, col:col + size] = left[...].T
            col += size

    stack_rows(arrays, layout, scratch)
    out_ref[...] = dot(left_scr[...], scratch[...]).astype(BF16)


def down_grad(lefts, stages):
    arrays, layout = stage_arrays(stages)
    width = arrays[0].shape[1]
    units = lefts[0].shape[1]
    rows = sum(r.shape[0] for r in lefts)
    step = min(256, width)
    return pl.pallas_call(
        functools.partial(down_grad_kernel, len(arrays), layout),
        grid=(width // step,),
        in_specs=[pl.BlockSpec((p.shape[0], step), lambda i: (0, i)) for p in arrays]
        + [pl.BlockSpec(r.shape, lambda i: (0, 0)) for r in lefts],
        out_specs=pl.BlockSpec((units, step), lambda i: (0, i)),
        out_shape=jax.ShapeDtypeStruct((units, width), BF16),
        scratch_shapes=[pltpu.VMEM((units, rows), BF16), pltpu.VMEM((rows, step), BF16)],
        compiler_params=pltpu.CompilerParams(vmem_limit_bytes=VMEM),
        cost_estimate=COST,
        name="down_grad",
    )(*arrays, *lefts)


def place_kernel(index_ref, *refs):
    parts, outs = refs[:-2], refs[-2:]
    for d, ref in enumerate(parts):
        @pl.when(pl.program_id(1) == d)
        def _(ref=ref):
            rows = outs[0].shape[0]
            for n, out_ref in enumerate(outs):
                out_ref[...] = ref[n * rows:(n + 1) * rows, :].astype(F32)


def place(parts, own, part):
    devices = len(parts)
    rows, mine = parts[0].shape[0] // 2, parts[0].shape[1]
    blocks = mine // part
    if part % LANES:
        stack = jnp.stack(parts).reshape(devices, 2, rows, blocks, part)
        stack = jnp.stack([take(stack, own ^ d) for d in range(devices)])
        both = stack.transpose(1, 2, 3, 0, 4).reshape(2, rows, -1).astype(F32)
        return both[0], both[1]
    return pl.pallas_call(
        place_kernel,
        grid_spec=pltpu.PrefetchScalarGridSpec(
            num_scalar_prefetch=1,
            grid=(blocks, devices),
            in_specs=[pl.BlockSpec((2 * rows, part), lambda b, d, n: (0, b))] * devices,
            out_specs=[pl.BlockSpec((rows, part), lambda b, d, n: (0, b * devices + (n[0] ^ d)))] * 2,
        ),
        out_shape=[jax.ShapeDtypeStruct((rows, devices * mine), F32)] * 2,
        compiler_params=pltpu.CompilerParams(vmem_limit_bytes=VMEM),
        cost_estimate=COST,
        name="place",
    )(own.astype(jnp.int32).reshape(1), *parts)


X, Y, Z, C = "fo", "si", "zb", "fi"


def swap(values, axis, offset=1):
    size = lax.axis_size(axis)
    return lax.ppermute(values, axis, [(i, i ^ offset) for i in range(size)])


def swap_cube(values, offset):
    if len(offset) == 1:
        return swap(values, offset[0])
    sizes = [lax.axis_size(a) for a in offset]
    total = 1
    for size in sizes:
        total *= size
    pairs = []
    for i in range(total):
        rest, place = i, []
        for size in reversed(sizes):
            place.append(rest % size ^ 1)
            rest //= size
        j = 0
        for size, p in zip(sizes, reversed(place)):
            j = j * size + p
        pairs.append((i, j))
    return lax.ppermute(values, offset, pairs)


def sync(*values):
    leaves, tree = jax.tree.flatten(values)
    return jax.tree.unflatten(tree, lax.optimization_barrier(leaves))


STAGES = (((),), ((X,), (Y,), (Z,)), ((X, Z), (X, Y), (Z, Y)))


def other_core(arrays):
    return swap(arrays[0] if len(arrays) == 1 else jnp.concatenate(arrays, axis=0), C)


def add_low(left, right):
    return (left.astype(F32) + right.astype(F32)).astype(BF16)


def send_home(stage, here, other):
    total = add_low(here, other)
    return [total[n] if not offset else swap_cube(total[n], offset) for n, offset in enumerate(STAGES[stage])]


def take(partial, block):
    return lax.dynamic_index_in_dim(partial, block, 0, keepdims=False)


def send_far(partial, za):
    return [swap(take(partial, za ^ k), "za", k) for k in range(1, lax.axis_size("za"))]


def add_far(partial, got, za):
    total = take(partial, za).astype(F32)
    for g in got:
        total = total + g.astype(F32)
    return total


def per_device(
    tokens, bounds, cotangent, attn_gain, query_weight, key_matrix, value_matrix,
    query_gain, key_gain, out_weight, ffn_gain, gate_weight, up_weight, down_weight,
):
    fsdp = ("fo", "fi")
    seq = ("za", "zb", "si")
    rows, width = tokens.shape
    f_count = lax.axis_size(fsdp)
    s_count = lax.axis_size(seq)
    far = lax.axis_size("za")
    f_index = lax.axis_index(fsdp)
    s_index = lax.axis_index(seq)
    za, zb, si = lax.axis_index("za"), lax.axis_index("zb"), lax.axis_index("si")
    length = rows * s_count
    heads = QUERY_HEADS // s_count
    copies = max(1, s_count // KEY_VALUE_HEADS)
    assert KEY_VALUE_HEADS * copies == s_count
    q_cols = heads * HEAD_SIZE
    cols = q_cols + 2 * HEAD_SIZE
    padded = -(-cols // LANES) * LANES
    all_q, all_kv = QUERY_HEADS * HEAD_SIZE, KEY_VALUE_HEADS * HEAD_SIZE

    pieces = [
        query_weight.reshape(-1, s_count, q_cols),
        jnp.repeat(key_matrix.reshape(-1, KEY_VALUE_HEADS, HEAD_SIZE), copies, axis=1),
        jnp.repeat(value_matrix.reshape(-1, KEY_VALUE_HEADS, HEAD_SIZE), copies, axis=1),
    ]
    kv_start = (s_index // copies) * HEAD_SIZE
    own_cols = [
        lax.dynamic_slice_in_dim(query_weight, s_index * q_cols, q_cols, 1),
        lax.dynamic_slice_in_dim(key_matrix, kv_start, HEAD_SIZE, 1),
        lax.dynamic_slice_in_dim(value_matrix, kv_start, HEAD_SIZE, 1),
    ]
    if padded > cols:
        pieces.append(jnp.zeros(pieces[0].shape[:2] + (padded - cols,), BF16))
        own_cols.append(jnp.zeros((query_weight.shape[0], padded - cols), BF16))
    w_own = lax.all_gather(jnp.concatenate(own_cols, axis=1), fsdp, axis=0, tiled=True)
    out_full = lax.all_gather(out_weight, fsdp, axis=0, tiled=True)
    w_rows = jnp.concatenate(pieces, axis=2).reshape(-1, s_count * padded)
    w_quarters = lambda n: w_rows[n * (w_rows.shape[0] // 4):(n + 1) * (w_rows.shape[0] // 4)]

    far_list = [(k, swap(tokens, "za", k)) for k in range(1, far)]
    x_y, x_z, c_x = swap(tokens, Y), swap(tokens, Z), swap(cotangent, X)
    ids = jnp.arange(length, dtype=jnp.int32)
    b0, b1 = bounds[0, 0], bounds[0, 1]
    starts = jnp.where(ids >= b1, b1, jnp.where(ids >= b0, b0, 0))
    frequency = ROPE_BASE ** (-(jnp.arange(HEAD_SIZE // 2, dtype=F32) * 2.0 / HEAD_SIZE))
    phases = (ids - starts).astype(F32)[:, None] * frequency[None, :]
    cosine, sine = jnp.cos(phases), jnp.sin(phases)
    cos2 = jnp.concatenate([cosine] * 4, axis=1)
    sin2 = jnp.concatenate([-sine, sine] * 2, axis=1)
    head_gain = jnp.concatenate(
        [query_gain] * heads + [key_gain] + [jnp.ones((padded - cols + HEAD_SIZE,), F32)]
    )[None, :]
    far_list, x_y, x_z, c_x, w_rows, cos2, sin2 = sync([b for _, b in far_list], x_y, x_z, c_x, w_rows, cos2, sin2)

    def some_project(blocks, held):
        index = jnp.stack([((za ^ k) * 2 + (zb ^ dz)) * 2 + (si ^ dy) for (k, dz, dy), _ in blocks])
        return project(
            heads, [b for _, b in blocks], index.astype(jnp.int32), bounds[0], attn_gain[None, :], w_own, head_gain,
            cos2, sin2, length, held,
        )

    far_y = [swap(b, Y) for b in far_list]
    far_z = [swap(b, Z) for b in far_list]
    held = some_project([((0, 0, 0), tokens), ((0, 0, 1), x_y), ((0, 1, 0), x_z)], None)
    far_y, far_z, held, x_y = sync(far_y, far_z, held, x_y)
    x_yz = swap(x_y, Z)
    far_yz = [swap(b, Y) for b in far_z]
    for n, k in enumerate(range(1, far)):
        held = some_project([((k, 0, 0), far_list[n]), ((k, 0, 1), far_y[n]), ((k, 1, 0), far_z[n])], held)
    x_yz, far_yz, held, cot, w_rows = sync(x_yz, far_yz, held, cotangent, w_rows)
    c_y, c_z = swap(cot, Y), swap(cot, Z)
    w_x = [swap(w_quarters(0), X)]
    w_c = swap(w_rows, C)
    held = some_project([((0, 1, 1), x_yz)] + [((k, 1, 1), far_yz[n]) for n, k in enumerate(range(1, far))], held)
    normed, q, k, v, unit, scale = held
    attended_low, attended, q2 = attend(heads, q, k, v)
    c_y, c_z, attended_low, c_x, w_c, w_x = sync(c_y, c_z, attended_low, c_x, w_c, w_x)
    heads_out = lax.all_to_all(attended_low, seq, split_axis=0, concat_axis=1, tiled=True)
    c_xz = swap(c_z, X)
    w_xc = [swap(w_x[0], C)]
    c_one = [c_x, c_y, c_z]
    c_own_other, c_one_other = other_core([cot]), other_core(c_one)
    heads_out, c_xz, c_own_other, c_one_other, w_xc = sync(heads_out, c_xz, c_own_other, c_one_other, w_xc)

    c_two_other = other_core([c_xz])
    own_rows = out_weight.shape[0]
    left = []
    for offset in range(f_count):
        block = lax.dynamic_slice_in_dim(heads_out, (f_index ^ offset) * own_rows, own_rows, 1)
        left.append(swap(block, fsdp, offset) if offset else block)
    inputs = tokens.astype(F32)
    square_one = jnp.mean(inputs * inputs, axis=1, keepdims=True)
    scale_one = lax.rsqrt(square_one + EPSILON)
    residual = inputs + dot(heads_out, out_full)
    square_two = jnp.mean(residual * residual, axis=1, keepdims=True)
    scale_two = lax.rsqrt(square_two + EPSILON)
    inner = (residual * scale_two * ffn_gain).astype(BF16)
    inner, c_two_other, c_y, left = sync(inner, c_two_other, c_y, left)

    units = gate_weight.shape[1]
    part = units // s_count
    mine = far * part
    own_block = zb * 2 + si
    if part % LANES == 0:
        weights = (gate_weight, up_weight, down_weight)
        unit_index = (jnp.arange(far, dtype=jnp.int32) * 4 + own_block).astype(jnp.int32)
        width_of_part = part
    else:
        pick = lambda w: lax.dynamic_index_in_dim(
            w.reshape(width, far, 4, part), own_block, 2, keepdims=False
        ).reshape(width, mine)
        weights = (
            pick(gate_weight),
            pick(up_weight),
            lax.dynamic_index_in_dim(
                down_weight.reshape(far, 4, part, width), own_block, 1, keepdims=False
            ).reshape(mine, width),
        )
        unit_index = jnp.zeros((1,), jnp.int32)
        width_of_part = mine
    run = lambda x_stage, c_stage: feed(x_stage, c_stage, unit_index, weights, width_of_part)
    x, y, z = swap(inner, X), swap(inner, Y), swap(inner, Z)
    x_stages = [([inner], [other_core([inner])])]
    c_stages = [([cot], [c_own_other])]
    fed = [run(x_stages[0], c_stages[0])]
    x, y, z, fed = sync(x, y, z, fed)
    xy, xz, yz = swap(x, Y), swap(z, X), swap(y, Z)
    c_xy, c_yz = swap(c_y, X), swap(c_y, Z)
    x_stages.append(([x, y, z], [other_core([x, y, z])]))
    c_stages.append((c_one, [c_one_other]))
    fed.append(run(x_stages[1], c_stages[1]))
    xy, xz, yz, c_xy, c_yz, fed, x_stages = sync(xy, xz, yz, c_xy, c_yz, fed, x_stages)
    xyz, c_xyz = swap(xz, Y), swap(c_yz, X)
    x_stages.append(([xz, xy, yz], [other_core([xz, xy, yz])]))
    c_stages.append(([c_xz, c_xy, c_yz], [c_two_other, other_core([c_xy, c_yz])]))
    d_home = send_home(0, fed[0][0], swap(fed[0][1], C)) + send_home(1, fed[1][0], swap(fed[1][1], C))
    fed.append(run(x_stages[2], c_stages[2]))
    xyz, c_xyz, d_home, fed, x_stages, c_stages = sync(xyz, c_xyz, d_home, fed, x_stages, c_stages)
    two = add_low(fed[2][0], swap(fed[2][1], C))
    mid = rows // 2
    home = [swap_cube(two[n, :mid], offset) for n, offset in enumerate(STAGES[2])]
    x_stages.append(([xyz], [other_core([xyz])]))
    c_stages.append(([c_xyz], [other_core([c_xyz])]))
    fed.append(run(x_stages[3], c_stages[3]))
    two, home, fed, x_stages, c_stages = sync(two, home, fed, x_stages, c_stages)
    three = add_low(fed[3][0][0], swap(fed[3][1], C)[0])
    last = [swap_cube(two[n, mid:], offset) for n, offset in enumerate(STAGES[2])]
    d_home.append(swap_cube(three, (X, Z, Y)))
    m_other = swap(fed[2][3], C)
    gu = gate_grad(x_stages, [f[5] for f in fed], za, far)
    down_part = down_grad([f[4] for f in fed], c_stages).reshape(far, part, width)
    d_home, last, down_part, gu, fed, w_rows, m_other = sync(d_home, last, down_part, gu, fed, w_rows, m_other)
    d_home += [jnp.concatenate([low, high], axis=0) for low, high in zip(home, last)]
    quarter = width // far // 4

    def owner_block(values, offset):
        return lax.dynamic_slice_in_dim(values, (own_block ^ offset) * quarter, quarter, 0)

    def send_rows(parts, *offsets):
        return [
            swap(jnp.concatenate([owner_block(parts[k], o) for o in offsets], axis=0), "za", k) for k in range(1, far)
        ]

    def to_owners(gates, ups, gate_got, up_got):
        spread = []
        for offset, axes in enumerate(((), (Y,), (Z,), (Z, Y))):
            both = []
            for parts, got in ((gates, gate_got), (ups, up_got)):
                rows_here = owner_block(parts[0], offset).astype(F32)
                for k in range(far - 1):
                    pieces = [t for piece in got for t in jnp.split(piece[k], piece[k].shape[0] // quarter)]
                    rows_here = rows_here + pieces[offset].astype(F32)
                both.append(rows_here.astype(BF16))
            both = jnp.concatenate(both, axis=0)
            spread.append(swap_cube(both, axes) if axes else both)
        return spread

    gate_got = [send_rows(gu[:far], 0)]
    w_x.append(swap(w_quarters(1), X))
    m_other = [swap(fed[0][3], C), swap(fed[1][3], C), m_other, swap(fed[3][3], C)]
    d_inner = sum(a.astype(F32) for a in d_home)
    ffn_part = jnp.sum(d_inner * residual * scale_two, axis=0)
    weighted = d_inner * ffn_gain
    d_residual = cotangent.astype(F32) + scale_two * (
        weighted - residual * scale_two * scale_two * jnp.mean(weighted * residual, axis=1, keepdims=True)
    )
    d_branch = d_residual.astype(BF16)
    d_heads = dot(d_branch, out_full, NT).astype(BF16)
    d_heads, d_branch, gate_got, gu, w_x, m_other, fed = sync(d_heads, d_branch, gate_got, gu, w_x, m_other, fed)
    d_attended = lax.all_to_all(d_heads, seq, split_axis=1, concat_axis=0, tiled=True)
    gate_got.append(send_rows(gu[:far], 1))
    over = swap(d_branch, X)
    right = [d_branch, swap(d_branch, C), over, swap(over, C)]
    m = [add_low(f[2], other) for f, other in zip(fed, m_other)]
    d_attended, right, m, gate_got, gu, w_rows, fed = sync(d_attended, right, m, gate_got, gu, w_rows, fed)
    mixed = [
        jnp.concatenate([owner_block(gu[n + k], o) for n, o in ((0, 2), (0, 3), (far, 0), (far, 1))], axis=0)
        for k in range(1, far)
    ]
    mixed = [swap(t, "za", k + 1) for k, t in enumerate(mixed)]
    w_x.append(swap(w_rows[w_rows.shape[0] // 2:], X))
    m_far = swap(m[3][0], Y)
    out_part = dot(jnp.concatenate(left, axis=0), jnp.concatenate(right, axis=0), TN).astype(BF16)
    out_part = out_part.reshape(far, 2, 2, -1, width)
    pick = lambda values, index, axis: lax.dynamic_index_in_dim(values, index, axis, keepdims=False)
    out_y = swap(pick(out_part, 1 - si, 2), Y)
    d_qkv, gain_parts = attend_back(
        heads, q2, k, v, sync(d_attended, out_part)[0], attended, unit, scale, head_gain, cos2, sin2
    )
    d_qkv, gain_parts, gate_got, mixed, gu, m, m_far, w_x, out_part, out_y = sync(
        d_qkv, gain_parts, gate_got, mixed, gu, m, m_far, w_x, out_part, out_y
    )
    gate_got.append([t[:2 * quarter] for t in mixed])
    up_got = [[t[2 * quarter:] for t in mixed]]
    d_tok = lax.all_to_all(d_qkv, seq, split_axis=0, concat_axis=1, tiled=True)
    proj_part = dot(normed, d_qkv, TN).astype(BF16).reshape(2, 2, width // 4, padded)
    fi, fo = lax.axis_index(C), lax.axis_index(X)
    proj_core = add_low(pick(proj_part, fi, 1), swap(pick(proj_part, 1 - fi, 1), C))
    proj_x = swap(take(proj_core, 1 - fo), X)
    w_xc.append(swap(jnp.concatenate(w_x[1:], axis=0), C))
    m_x = swap(m[2][1], X)
    out_part = add_low(pick(out_part, si, 2), out_y)
    m_xz = add_low(m[2][0], m_far)
    d_tok, up_got, gate_got, gu, proj_core, proj_x, w_xc, out_part, m, m_x, m_xz, gain_parts, down_part = sync(
        d_tok, up_got, gate_got, gu, proj_core, proj_x, w_xc, out_part, m, m_x, m_xz, gain_parts, down_part
    )
    up_got.append(send_rows(gu[far:], 2, 3))
    m_z = [swap(m_xz, X), swap(m[2][2], Y)]
    out_z = swap(pick(out_part, 1 - zb, 1), Z)
    blocks = [w_rows, w_c, jnp.concatenate(w_x, axis=0), jnp.concatenate(w_xc, axis=0)]
    by_offset = jnp.stack([dot(d_tok, w, NT) for w in blocks])
    d_normed = jnp.concatenate([take(by_offset, f_index ^ n) for n in range(f_count)], axis=1)
    weighted = d_normed * attn_gain
    input_grad = (
        d_residual
        + scale_one
        * (weighted - inputs * scale_one * scale_one * jnp.mean(weighted * inputs, axis=1, keepdims=True))
    ).astype(BF16)
    proj_rows = add_low(take(proj_core, fo), proj_x)
    m_one = [m[1][0], add_low(m[1][1], m_x)]
    m_z, up_got, gate_got, input_grad, gu, proj_rows, m, m_one, out_z, out_part, gain_parts, down_part = sync(
        m_z, up_got, gate_got, input_grad, gu, proj_rows, m, m_one, out_z, out_part, gain_parts, down_part
    )
    proj = lax.all_to_all(proj_rows, seq, split_axis=0, concat_axis=1, tiled=True)
    down_half = part // 2
    down_got = [send_far(down_part[:, :down_half], za)]
    spread = to_owners(gu[:far], gu[far:], gate_got, up_got)
    m_one.append((m[1][2].astype(F32) + m_z[0].astype(F32) + m_z[1].astype(F32)).astype(BF16))
    out_part = add_low(pick(out_part, zb, 1), out_z)
    gain_row = gain_parts[0]
    pack = jnp.concatenate(
        [
            ffn_part,
            gain_row[:q_cols].reshape(heads, HEAD_SIZE).sum(axis=0),
            gain_row[q_cols:q_cols + HEAD_SIZE],
        ]
    ).reshape(-1, LANES)
    for axis in ("fi", "fo", "si", "zb", "za"):
        offset = 1
        while offset < lax.axis_size(axis):
            pack = pack + swap(pack, axis, offset)
            offset *= 2
    pack = pack.reshape(-1)
    proj, spread, m, m_one, out_part, down_part, down_got, pack = sync(
        proj, spread, m, m_one, out_part, down_part, down_got, pack
    )
    out_got = send_far(out_part, za)
    down_got.append(send_far(down_part[:, down_half:], za))
    m_last = [swap(m_one[0], X), swap(m_one[1], Y), swap(m_one[2], Z)]
    gate_up = place(spread, own_block, part)
    gate_mine, up_mine = gate_up
    down_mine = jnp.concatenate(
        [add_far(down_part[:, :down_half], down_got[0], za), add_far(down_part[:, down_half:], down_got[1], za)], axis=0
    )
    mlp_out = m[0][0].astype(F32) + sum(a.astype(F32) for a in m_last)
    block_output = (residual + mlp_out).astype(BF16)
    out_mine = add_far(out_part, out_got, za)
    proj = proj.astype(F32)
    count = proj.shape[0]
    by_device = proj.reshape(count, s_count, padded)

    def fold(values):
        return values.reshape(count, KEY_VALUE_HEADS, copies, HEAD_SIZE).sum(axis=2).reshape(count, -1)

    query_mine = by_device[:, :, :q_cols].reshape(count, QUERY_HEADS * HEAD_SIZE)
    key_mine = fold(by_device[:, :, q_cols:q_cols + HEAD_SIZE])
    value_mine = fold(by_device[:, :, q_cols + HEAD_SIZE:cols])

    my_w = lax.dynamic_slice_in_dim(w_rows, s_index * count, count, 0).astype(F32)
    my_gain = lax.dynamic_slice_in_dim(attn_gain, (f_index * s_count + s_index) * count, count, 0)
    attn_gain_mine = jnp.sum(my_w * proj, axis=1) / my_gain
    ffn_gain_mine = lax.dynamic_slice_in_dim(pack, (f_index * s_count + s_index) * count, count, 0)
    attn_rms = jnp.sqrt(square_one + EPSILON)[:, 0]
    mlp_rms = jnp.sqrt(square_two + EPSILON)[:, 0]
    return (
        block_output, input_grad, residual, attn_rms, mlp_rms, attn_gain_mine,
        query_mine, key_mine, value_mine, pack[width:width + HEAD_SIZE], pack[width + HEAD_SIZE:],
        out_mine, ffn_gain_mine, gate_mine, up_mine, down_mine,
    )


def solution(mesh):
    f_count, s_count = mesh.shape["fsdp"], mesh.shape["seq"]
    fine = Mesh(
        mesh.devices.reshape(f_count // 2, 2, s_count // 4, 2, 2), ("fo", "fi", "za", "zb", "si")
    )
    f, s = ("fo", "fi"), ("za", "zb", "si")
    every = P(f + s, None)
    vector = P(f + s)
    placed = (
        every, P(f, None), every, P(), P(f, None), P(f, None), P(f, None), P(), P(),
        P(f, None), P(), P(None, f), P(None, f), P(f, None),
    )
    return jax.shard_map(
        per_device,
        mesh=fine,
        in_specs=placed,
        out_specs=(
            every, every, every, vector, vector, vector, every, every, every, P(), P(),
            every, vector, P(s, f), P(s, f), every,
        ),
        check_vma=False,
    )
```

```python
import functools

import jax
import jax.numpy as jnp
from jax import lax
from jax.experimental import pallas as pl
from jax.experimental.pallas import tpu as pltpu
from jax.sharding import Mesh, PartitionSpec as P

HEAD_SIZE = 64
QUERY_HEADS = 32
KEY_VALUE_HEADS = 8
EPSILON = 1e-05
ROPE_BASE = 1000000.0
BIG = 30000.0
LANES = 128
BLOCK = 256
UNROLLED = 2048
VMEM = 60 * 1024 * 1024
COST = pl.CostEstimate(flops=1000, bytes_accessed=1000, transcendentals=0)

F32 = jnp.float32
BF16 = jnp.bfloat16
NT = (((1,), (1,)), ((), ()))
TN = (((0,), (0,)), ((), ()))


def dot(left, right, dims=(((1,), (0,)), ((), ()))):
    return lax.dot_general(left, right, dims, preferred_element_type=F32)


def split_low(values):
    high = values.astype(BF16)
    return high, (values - high.astype(F32)).astype(BF16)


def head_means(values, ones):
    high, low = split_low(values)
    return (dot(high, ones) + dot(low, ones)) * (1.0 / HEAD_SIZE)


def head_ones():
    row = lax.broadcasted_iota(jnp.int32, (LANES, LANES), 0) // HEAD_SIZE
    col = lax.broadcasted_iota(jnp.int32, (LANES, LANES), 1) // HEAD_SIZE
    return jnp.where(row == col, 1.0, 0.0).astype(BF16)


def swap_halves(values):
    lane = lax.broadcasted_iota(jnp.int32, values.shape, 1) % HEAD_SIZE
    half = HEAD_SIZE // 2
    return jnp.where(
        lane < half, pltpu.roll(values, LANES - half, 1), pltpu.roll(values, half, 1)
    )


def project_kernel(heads, count, fresh, index_ref, bounds_ref, *refs):
    x_refs = refs[:count]
    gain_ref, w_ref, head_gain_ref, cos_ref, sin_ref = refs[count:count + 5]
    refs = refs[count + 5 + (0 if fresh else 6):]
    normed_ref, q_ref, k_ref, v_ref, unit_ref, scale_ref, x_scr = refs
    i = pl.program_id(0)
    rows = x_scr.shape[0]
    for r in range(count):
        @pl.when(i == r)
        def _(r=r):
            x_scr[...] = x_refs[r][...]

    x = x_scr[...].astype(F32)
    scale = lax.rsqrt(jnp.mean(x * x, axis=1, keepdims=True) + EPSILON)
    normed = (x * scale * gain_ref[...]).astype(BF16)
    normed_ref[...] = normed
    pre = dot(normed, w_ref[...])
    cosine, sine = cos_ref[...], sin_ref[...]
    shape = (rows, LANES)
    token = index_ref[i] * rows + lax.broadcasted_iota(jnp.int32, shape, 0)
    doc = (token >= bounds_ref[0]).astype(jnp.int32) + (token >= bounds_ref[1]).astype(jnp.int32)
    lane = lax.broadcasted_iota(jnp.int32, shape, 1)
    mark = lane - HEAD_SIZE
    query_marks = jnp.where(mark == doc, 1.0, 0.0)
    key_marks = jnp.where(mark < 3, jnp.where(mark == doc, 0.0, -BIG), jnp.where(mark < 5, 1.0, 0.0))
    value_marks = jnp.where(mark < 2, 1.0, 0.0)
    ones = head_ones()

    def place(values, segment, marks):
        group = values if segment % 2 == 0 else pltpu.roll(values, HEAD_SIZE, 1)
        return jnp.where(lane < HEAD_SIZE, group, marks).astype(BF16)

    for g in range(pre.shape[1] // LANES):
        cols = slice(g * LANES, (g + 1) * LANES)
        u = pre[:, cols]
        r = lax.rsqrt(head_means(u * u, ones) + EPSILON)
        unit = u * r
        unit_ref[:, cols] = unit
        scale_ref[:, cols] = r
        gained = unit * head_gain_ref[0:1, cols]
        rot = (gained * cosine + swap_halves(gained) * sine).astype(BF16).astype(F32)
        for segment in (2 * g, 2 * g + 1):
            if segment < heads:
                q_ref[segment] = place(rot * 0.125, segment, query_marks)
            elif segment == heads:
                k_ref[...] = place(rot, segment, key_marks)
            elif segment == heads + 1:
                v_ref[...] = place(u, segment, value_marks)


def project(heads, blocks, index, bounds, gain, w, head_gain, cosine, sine, length, held=None):
    rows, width = blocks[0].shape
    count = len(blocks)
    cols = w.shape[1]
    row = lambda c: pl.BlockSpec((rows, c), lambda i, n, b: (n[i], 0))
    whole = lambda a: pl.BlockSpec(a.shape, lambda i, n, b: (0, 0))
    fresh = held is None
    held = () if fresh else held
    outs = [
        jax.ShapeDtypeStruct((length, width), BF16),
        jax.ShapeDtypeStruct((heads, length, LANES), BF16),
        jax.ShapeDtypeStruct((length, LANES), BF16),
        jax.ShapeDtypeStruct((length, LANES), BF16),
        jax.ShapeDtypeStruct((length, cols), F32),
        jax.ShapeDtypeStruct((length, cols), F32),
    ]
    tokens = rows * count
    return pl.pallas_call(
        functools.partial(project_kernel, heads, count, fresh),
        grid_spec=pltpu.PrefetchScalarGridSpec(
            num_scalar_prefetch=2,
            grid=(count,),
            in_specs=[whole(b) for b in blocks]
            + [whole(gain), whole(w), whole(head_gain), row(LANES), row(LANES)]
            + [pl.BlockSpec(memory_space=pl.ANY)] * len(held),
            out_specs=[
                row(width),
                pl.BlockSpec((heads, rows, LANES), lambda i, n, b: (0, n[i], 0)),
                row(LANES),
                row(LANES),
                row(cols),
                row(cols),
            ],
            scratch_shapes=[pltpu.VMEM((rows, width), BF16)],
        ),
        out_shape=outs,
        input_output_aliases={2 + count + 5 + n: n for n in range(len(held))},
        compiler_params=pltpu.CompilerParams(vmem_limit_bytes=VMEM),
        cost_estimate=COST,
        name="project",
    )(index, bounds, *blocks, gain, w, head_gain, cosine, sine, *held)


def attend_kernel(heads, q_ref, k_ref, v_ref, low_ref, out_ref, q2_ref):
    i = pl.program_id(0)
    rows = BLOCK
    q = q_ref[...].reshape(heads * rows, LANES)

    def step(j, total):
        start = pl.multiple_of(j * rows, rows)
        p = jnp.exp(dot(q, k_ref[pl.ds(start, rows), :], NT)).astype(BF16)
        return total + dot(p, v_ref[pl.ds(start, rows), :])

    total = lax.fori_loop(0, i, step, jnp.zeros((heads * rows, LANES), F32))
    start = pl.multiple_of(i * rows, rows)
    s = dot(q, k_ref[pl.ds(start, rows), :], NT)
    t_local = lax.broadcasted_iota(jnp.int32, s.shape, 0) % rows
    u_local = lax.broadcasted_iota(jnp.int32, s.shape, 1)
    p = jnp.where(u_local <= t_local, jnp.exp(s), 0.0).astype(BF16)
    total = total + dot(p, v_ref[pl.ds(start, rows), :])
    weight = total[:, HEAD_SIZE:HEAD_SIZE + 1]
    out = total[:, :HEAD_SIZE] / weight
    for h in range(heads):
        part = out[h * rows:(h + 1) * rows, :]
        out_ref[:, h * HEAD_SIZE:(h + 1) * HEAD_SIZE] = part
        low_ref[:, h * HEAD_SIZE:(h + 1) * HEAD_SIZE] = part.astype(BF16)
    high, low = split_low(-jnp.log(weight))
    lane = lax.broadcasted_iota(jnp.int32, q.shape, 1)
    q2 = jnp.where(lane == HEAD_SIZE + 3, high, jnp.where(lane == HEAD_SIZE + 4, low, q))
    q2_ref[...] = q2.reshape(heads, rows, LANES)


def attend_unrolled_kernel(heads, rows, q_ref, k_ref, v_ref, low_ref, out_ref, q2_ref):
    stretch = q_ref.shape[1]

    def block(first, at):
        q = q_ref[:, at:at + rows, :].reshape(heads * rows, LANES)
        s = dot(q, k_ref[first:first + rows, :], NT)
        t_local = lax.broadcasted_iota(jnp.int32, s.shape, 0) % rows
        u_local = lax.broadcasted_iota(jnp.int32, s.shape, 1)
        p = jnp.where(u_local <= t_local, jnp.exp(s), 0.0).astype(BF16)
        total = dot(p, v_ref[first:first + rows, :])
        if first:
            p = jnp.exp(dot(q, k_ref[:first, :], NT)).astype(BF16)
            total = total + dot(p, v_ref[:first, :])
        weight = total[:, HEAD_SIZE:HEAD_SIZE + 1]
        out = total[:, :HEAD_SIZE] / weight
        for h in range(heads):
            part = out[h * rows:(h + 1) * rows, :]
            out_ref[at:at + rows, h * HEAD_SIZE:(h + 1) * HEAD_SIZE] = part
            low_ref[at:at + rows, h * HEAD_SIZE:(h + 1) * HEAD_SIZE] = part.astype(BF16)
        high, low = split_low(-jnp.log(weight))
        lane = lax.broadcasted_iota(jnp.int32, q.shape, 1)
        q2 = jnp.where(lane == HEAD_SIZE + 3, high, jnp.where(lane == HEAD_SIZE + 4, low, q))
        q2_ref[:, at:at + rows, :] = q2.reshape(heads, rows, LANES)

    for step in range(k_ref.shape[0] // stretch):
        @pl.when(pl.program_id(0) == step)
        def _(step=step):
            for at in range(0, stretch, rows):
                block(step * stretch + at, at)


def attend(heads, q, k, v):
    tokens = k.shape[0]
    if tokens <= UNROLLED and tokens % (2 * BLOCK) == 0:
        kernel, rows = functools.partial(attend_unrolled_kernel, heads, BLOCK // 2), 2 * BLOCK
    else:
        kernel, rows = functools.partial(attend_kernel, heads), BLOCK
    return pl.pallas_call(
        kernel,
        grid=(tokens // rows,),
        in_specs=[
            pl.BlockSpec((heads, rows, LANES), lambda i: (0, i, 0)),
            pl.BlockSpec((tokens, LANES), lambda i: (0, 0)),
            pl.BlockSpec((tokens, LANES), lambda i: (0, 0)),
        ],
        out_specs=[
            pl.BlockSpec((rows, heads * HEAD_SIZE), lambda i: (i, 0)),
            pl.BlockSpec((rows, heads * HEAD_SIZE), lambda i: (i, 0)),
            pl.BlockSpec((heads, rows, LANES), lambda i: (0, i, 0)),
        ],
        out_shape=[
            jax.ShapeDtypeStruct((tokens, heads * HEAD_SIZE), BF16),
            jax.ShapeDtypeStruct((tokens, heads * HEAD_SIZE), F32),
            jax.ShapeDtypeStruct((heads, tokens, LANES), BF16),
        ],
        compiler_params=pltpu.CompilerParams(vmem_limit_bytes=VMEM),
        cost_estimate=COST,
        name="attend",
    )(q, k, v)


def attend_back_kernel(heads, q_ref, k_ref, v_ref, grad_ref, out_ref, unit_hbm, scale_hbm, head_gain_ref,
                       cos_hbm, sin_hbm, dqkv_ref, gains_ref, g_scr, dq_scr, dk_scr, dv_scr,
                       unit_ref, scale_ref, cos_ref, sin_ref, sems):
    rows = BLOCK
    tokens = k_ref.shape[0]
    blocks = tokens // rows
    wide = heads * rows
    late = [
        pltpu.make_async_copy(source, target, sems.at[n])
        for n, (source, target) in enumerate(
            ((unit_hbm, unit_ref), (scale_hbm, scale_ref), (cos_hbm, cos_ref), (sin_hbm, sin_ref))
        )
    ]
    for copy in late:
        copy.start()

    def prepare(i, carry):
        at = pl.ds(pl.multiple_of(i * rows, rows), rows)
        lane = lax.broadcasted_iota(jnp.int32, (rows, HEAD_SIZE), 1)
        for h in range(heads):
            cols = slice(h * HEAD_SIZE, (h + 1) * HEAD_SIZE)
            grad = grad_ref[at, cols]
            delta = jnp.sum(grad.astype(F32) * out_ref[at, cols], axis=1, keepdims=True)
            high, low = split_low(-delta)
            g_scr[h, at, :HEAD_SIZE] = grad
            g_scr[h, at, HEAD_SIZE:] = jnp.where(lane == 0, high, jnp.where(lane == 1, low, jnp.zeros_like(low)))
        dq_scr[:, at, :] = jnp.zeros((heads, rows, LANES), F32)
        return carry

    lax.fori_loop(0, blocks, prepare, 0)

    def pair(j, i, diagonal):
        at = pl.ds(i * rows, rows)
        k = k_ref[pl.ds(j * rows, rows), :]
        q = q_ref[:, at, :].reshape(wide, LANES)
        g = g_scr[:, at, :].reshape(wide, LANES)
        p = jnp.exp(dot(k, q, NT))
        if diagonal:
            u_local = lax.broadcasted_iota(jnp.int32, p.shape, 0)
            t_local = lax.broadcasted_iota(jnp.int32, p.shape, 1) % rows
            p = jnp.where(u_local <= t_local, p, 0.0)
        dv = dot(p.astype(BF16), g)
        ds = (p * dot(v_ref[pl.ds(j * rows, rows), :], g, NT)).astype(BF16)
        dk = dot(ds, q)
        dq_scr[:, at, :] += dot(ds, k, TN).reshape(heads, rows, LANES)
        return dk, dv

    def key_step(j, carry):
        def query_step(i, state):
            dk, dv = pair(j, i, False)
            return state[0] + dk, state[1] + dv

        state = pair(j, j, True)
        if tokens <= UNROLLED:
            for i in range(j + 1, blocks):
                state = query_step(i, state)
        else:
            state = lax.fori_loop(j + 1, blocks, query_step, state)
        dk_scr[pl.ds(j * rows, rows), :] = state[0]
        dv_scr[pl.ds(j * rows, rows), :] = state[1]
        return carry

    if tokens <= UNROLLED:
        for j in range(blocks):
            key_step(j, 0)
    else:
        lax.fori_loop(0, blocks, key_step, 0)
    for copy in late:
        copy.wait()
    groups = unit_ref.shape[1] // LANES
    ones = head_ones()

    def finish(i, carry):
        at = pl.ds(pl.multiple_of(i * rows, rows), rows)
        cosine, sine = cos_ref[at, :], sin_ref[at, :]
        lane = lax.broadcasted_iota(jnp.int32, (rows, LANES), 1)

        def segment_of(s):
            if s < heads:
                return dq_scr[s, at, :] * 0.125
            return (dk_scr if s == heads else dv_scr)[at, :]

        sums = list(carry)
        for g in range(groups):
            cols = slice(g * LANES, (g + 1) * LANES)
            first = segment_of(2 * g)
            last = segment_of(2 * g + 1) if 2 * g + 1 < heads + 2 else first
            d = jnp.where(lane < HEAD_SIZE, first, pltpu.roll(last, HEAD_SIZE, 1))
            e = d * cosine - swap_halves(d) * sine
            unit = unit_ref[at, cols]
            sums[g] = sums[g] + jnp.sum(e * unit, axis=0, keepdims=True)
            w = e * head_gain_ref[0:1, cols]
            normal = scale_ref[at, cols] * (w - unit * head_means(w * unit, ones))
            is_value = lane + g * LANES >= (heads + 1) * HEAD_SIZE
            dqkv_ref[at, cols] = jnp.where(is_value, d, normal).astype(BF16)
        return tuple(sums)

    zero = jnp.zeros((1, LANES), F32)
    sums = lax.fori_loop(0, blocks, finish, (zero,) * groups)
    gains_ref[...] = jnp.zeros(gains_ref.shape, F32)
    for g in range(groups):
        gains_ref[0:1, g * LANES:(g + 1) * LANES] = sums[g]


def attend_back(heads, q, k, v, grad, out, unit, scale, head_gain, cosine, sine):
    tokens = k.shape[0]
    cols = unit.shape[1]
    vmem, late = pl.BlockSpec(memory_space=pltpu.VMEM), pl.BlockSpec(memory_space=pl.ANY)
    return pl.pallas_call(
        functools.partial(attend_back_kernel, heads),
        in_specs=[vmem] * 5 + [late] * 2 + [vmem] + [late] * 2,
        out_specs=[vmem] * 2,
        out_shape=[
            jax.ShapeDtypeStruct((tokens, cols), BF16),
            jax.ShapeDtypeStruct((8, cols), F32),
        ],
        scratch_shapes=[
            pltpu.VMEM((heads, tokens, LANES), BF16),
            pltpu.VMEM((heads, tokens, LANES), F32),
            pltpu.VMEM((tokens, LANES), F32),
            pltpu.VMEM((tokens, LANES), F32),
            pltpu.VMEM((tokens, cols), F32),
            pltpu.VMEM((tokens, cols), F32),
            pltpu.VMEM((tokens, LANES), F32),
            pltpu.VMEM((tokens, LANES), F32),
            pltpu.SemaphoreType.DMA((4,)),
        ],
        compiler_params=pltpu.CompilerParams(vmem_limit_bytes=VMEM),
        cost_estimate=COST,
        name="attend_back",
    )(q, k, v, grad, out, unit, scale, head_gain, cosine, sine)


def feed_kernel(layouts, weight_count, index_ref, *refs):
    tiles = sum(layouts[0][1])
    sides = []
    for pieces, layout in layouts:
        own = []
        for count in pieces:
            own.append(refs[:count])
            refs = refs[count:]
        others = refs[:len(layout)]
        sides.append((own, [(o, t) for o, count in zip(others, layout) for t in range(count)]))
        refs = refs[len(layout):]
    gate_ref, up_ref, down_ref = refs[:3]
    da_ref, db_ref, ma_ref, mb_ref, hidden_ref, dgu_ref, x_scr, c_scr, gu_scr, down_scr, sem, w_sem = refs[3:]
    i = pl.program_id(0)
    half = x_scr.shape[1] // 2

    def copies(t):
        slot = t % 2
        found = []
        for (own, others), scratch, which in ((sides[0], x_scr, 0), (sides[1], c_scr, 1)):
            other, place = others[t]
            size = half // len(own[t])
            for n, piece in enumerate(own[t]):
                found.append(
                    pltpu.make_async_copy(piece, scratch.at[slot, pl.ds(n * size, size)], sem.at[slot, which, n + 1])
                )
            found.append(
                pltpu.make_async_copy(
                    other.at[pl.ds(place * half, half)],
                    scratch.at[slot, pl.ds(half, half)],
                    sem.at[slot, which, 0],
                )
            )
        return found

    mine = hidden_ref.shape[1]
    part = mine // weight_count

    def weight_copies(n):
        at = pl.ds(pl.multiple_of(index_ref[n] * part, part), part)
        return [
            pltpu.make_async_copy(gate_ref.at[:, at], gu_scr.at[:, pl.ds(n * part, part)], w_sem.at[n, 0]),
            pltpu.make_async_copy(up_ref.at[:, at], gu_scr.at[:, pl.ds(mine + n * part, part)], w_sem.at[n, 1]),
            pltpu.make_async_copy(down_ref.at[at], down_scr.at[pl.ds(n * part, part)], w_sem.at[n, 2]),
        ]

    for t in range(tiles):
        @pl.when(i == t)
        def _(t=t):
            if t == 0:
                needed = copies(0) + [copy for n in range(weight_count) for copy in weight_copies(n)]
                for copy in needed:
                    copy.start()
            else:
                needed = copies(t)
            if t + 1 < tiles:
                for copy in copies(t + 1):
                    copy.start()
            for copy in needed:
                copy.wait()

    slot = lax.rem(i, 2)
    both = dot(x_scr[slot], gu_scr[...])
    gate, up = both[:, :mine], both[:, mine:]
    d_hidden = dot(c_scr[slot], down_scr[...], NT)
    sigma = 1.0 / (1.0 + jnp.exp(-gate))
    active = gate * sigma
    hidden = (active * up).astype(BF16)
    hidden_ref[...] = hidden
    dgu_ref[:, :mine] = (d_hidden * up * (sigma * (1.0 + gate * (1.0 - sigma)))).astype(BF16)
    dgu_ref[:, mine:] = (d_hidden * active).astype(BF16)
    d_inner = dot(dgu_ref[...], gu_scr[...], NT)
    mlp = dot(hidden, down_scr[...])
    da_ref[0] = d_inner[:half].astype(BF16)
    db_ref[0] = d_inner[half:].astype(BF16)
    ma_ref[0] = mlp[:half].astype(BF16)
    mb_ref[0] = mlp[half:].astype(BF16)


def feed(x_stage, c_stage, index, weights, part):
    (x_own, x_others), (c_own, c_others) = x_stage, c_stage
    tiles = len(x_own)
    half = x_own[0][0].shape[0] * len(x_own[0])
    layouts = tuple(
        (tuple(len(t) for t in own), tuple(o.shape[0] // half for o in others))
        for own, others in ((x_own, x_others), (c_own, c_others))
    )
    arrays = [a for own, others in ((x_own, x_others), (c_own, c_others)) for a in sum(own, []) + list(others)]
    rows = 2 * half
    gate, up, down = weights
    width = gate.shape[0]
    blocks = index.shape[0]
    mine = blocks * part
    halves = pl.BlockSpec((1, half, width), lambda i, n: (i, 0, 0))
    return pl.pallas_call(
        functools.partial(feed_kernel, layouts, blocks),
        grid_spec=pltpu.PrefetchScalarGridSpec(
            num_scalar_prefetch=1,
            grid=(tiles,),
            in_specs=[pl.BlockSpec(memory_space=pl.ANY)] * (len(arrays) + 3),
            out_specs=[halves] * 4
            + [
                pl.BlockSpec((rows, mine), lambda i, n: (i, 0)),
                pl.BlockSpec((rows, 2 * mine), lambda i, n: (i, 0)),
            ],
            scratch_shapes=[
                pltpu.VMEM((2, rows, width), BF16),
                pltpu.VMEM((2, rows, width), BF16),
                pltpu.VMEM((width, 2 * mine), BF16),
                pltpu.VMEM((mine, width), BF16),
                pltpu.SemaphoreType.DMA((2, 2, 3)),
                pltpu.SemaphoreType.DMA((blocks, 3)),
            ],
        ),
        out_shape=[jax.ShapeDtypeStruct((tiles, half, width), BF16)] * 4
        + [
            jax.ShapeDtypeStruct((tiles * rows, mine), BF16),
            jax.ShapeDtypeStruct((tiles * rows, 2 * mine), BF16),
        ],
        compiler_params=pltpu.CompilerParams(vmem_limit_bytes=VMEM),
        cost_estimate=COST,
        name="feed",
    )(index, *arrays, gate, up, down)


def stage_arrays(stages):
    arrays, layout = [], []
    for own, others in stages:
        half = own[0][0].shape[0] * len(own[0])
        arrays += sum(own, []) + list(others)
        layout.append((half, tuple(len(t) for t in own), tuple(o.shape[0] // half for o in others)))
    return arrays, tuple(layout)


def stack_rows(refs, layout, scratch):
    at = row = 0
    for half, tiles, others in layout:
        places = [(at + sum(tiles) + n, t) for n, count in enumerate(others) for t in range(count)]
        for pieces, (other, place) in zip(tiles, places):
            size = half // pieces
            for n in range(pieces):
                scratch[row + n * size:row + (n + 1) * size, :] = refs[at + n][...]
            at += pieces
            scratch[row + half:row + 2 * half, :] = refs[other][place * half:(place + 1) * half, :]
            row += 2 * half
        at += len(others)


def gate_grad_kernel(array_count, layout, *refs):
    arrays, refs = refs[:array_count], refs[array_count:]
    rights, (gate_ref, up_ref, scratch) = refs[:len(layout)], refs[len(layout):]
    stack_rows(arrays, layout, scratch)
    row = 0
    total = None
    for right in rights:
        size = right.shape[0]
        term = dot(scratch[row:row + size, :], right[...], TN)
        total = term if total is None else total + term
        row += size
    total = total.astype(BF16)
    mine = total.shape[1] // 2
    gate_ref[...] = total[:, :mine]
    up_ref[...] = total[:, mine:]


def gate_grad(stages, rights):
    arrays, layout = stage_arrays(stages)
    width = arrays[0].shape[1]
    units = rights[0].shape[1]
    rows = sum(r.shape[0] for r in rights)
    step = min(256, width)
    return pl.pallas_call(
        functools.partial(gate_grad_kernel, len(arrays), layout),
        grid=(width // step,),
        in_specs=[pl.BlockSpec((p.shape[0], step), lambda i: (0, i)) for p in arrays]
        + [pl.BlockSpec(r.shape, lambda i: (0, 0)) for r in rights],
        out_specs=[pl.BlockSpec((step, units // 2), lambda i: (i, 0))] * 2,
        out_shape=[jax.ShapeDtypeStruct((width, units // 2), BF16)] * 2,
        scratch_shapes=[pltpu.VMEM((rows, step), BF16)],
        compiler_params=pltpu.CompilerParams(vmem_limit_bytes=VMEM),
        cost_estimate=COST,
        name="gate_grad",
    )(*arrays, *rights)


def down_grad_kernel(array_count, layout, *refs):
    arrays, refs = refs[:array_count], refs[array_count:]
    lefts, (out_ref, left_scr, scratch) = refs[:len(layout)], refs[len(layout):]

    @pl.when(pl.program_id(0) == 0)
    def _():
        col = 0
        for left in lefts:
            size = left.shape[0]
            left_scr[:, col:col + size] = left[...].T
            col += size

    stack_rows(arrays, layout, scratch)
    out_ref[...] = dot(left_scr[...], scratch[...]).astype(BF16)


def down_grad(lefts, stages):
    arrays, layout = stage_arrays(stages)
    width = arrays[0].shape[1]
    units = lefts[0].shape[1]
    rows = sum(r.shape[0] for r in lefts)
    step = min(256, width)
    return pl.pallas_call(
        functools.partial(down_grad_kernel, len(arrays), layout),
        grid=(width // step,),
        in_specs=[pl.BlockSpec((p.shape[0], step), lambda i: (0, i)) for p in arrays]
        + [pl.BlockSpec(r.shape, lambda i: (0, 0)) for r in lefts],
        out_specs=pl.BlockSpec((units, step), lambda i: (0, i)),
        out_shape=jax.ShapeDtypeStruct((units, width), BF16),
        scratch_shapes=[pltpu.VMEM((units, rows), BF16), pltpu.VMEM((rows, step), BF16)],
        compiler_params=pltpu.CompilerParams(vmem_limit_bytes=VMEM),
        cost_estimate=COST,
        name="down_grad",
    )(*arrays, *lefts)


def place_kernel(index_ref, *refs):
    parts, outs = refs[:-2], refs[-2:]
    for d, ref in enumerate(parts):
        @pl.when(pl.program_id(1) == d)
        def _(ref=ref):
            rows = outs[0].shape[0]
            for n, out_ref in enumerate(outs):
                out_ref[...] = ref[n * rows:(n + 1) * rows, :].astype(F32)


def place(parts, own, part):
    devices = len(parts)
    rows, mine = parts[0].shape[0] // 2, parts[0].shape[1]
    blocks = mine // part
    if part % LANES:
        stack = jnp.stack(parts).reshape(devices, 2, rows, blocks, part)
        stack = jnp.stack([take(stack, own ^ d) for d in range(devices)])
        both = stack.transpose(1, 2, 3, 0, 4).reshape(2, rows, -1).astype(F32)
        return both[0], both[1]
    return pl.pallas_call(
        place_kernel,
        grid_spec=pltpu.PrefetchScalarGridSpec(
            num_scalar_prefetch=1,
            grid=(blocks, devices),
            in_specs=[pl.BlockSpec((2 * rows, part), lambda b, d, n: (0, b))] * devices,
            out_specs=[pl.BlockSpec((rows, part), lambda b, d, n: (0, b * devices + (n[0] ^ d)))] * 2,
        ),
        out_shape=[jax.ShapeDtypeStruct((rows, devices * mine), F32)] * 2,
        compiler_params=pltpu.CompilerParams(vmem_limit_bytes=VMEM),
        cost_estimate=COST,
        name="place",
    )(own.astype(jnp.int32).reshape(1), *parts)


X, Y, Z, C = "fo", "si", "zb", "fi"


def swap(values, axis, offset=1):
    size = lax.axis_size(axis)
    return lax.ppermute(values, axis, [(i, i ^ offset) for i in range(size)])


def swap_cube(values, offset):
    if len(offset) == 1:
        return swap(values, offset[0])
    sizes = [lax.axis_size(a) for a in offset]
    total = 1
    for size in sizes:
        total *= size
    pairs = []
    for i in range(total):
        rest, place = i, []
        for size in reversed(sizes):
            place.append(rest % size ^ 1)
            rest //= size
        j = 0
        for size, p in zip(sizes, reversed(place)):
            j = j * size + p
        pairs.append((i, j))
    return lax.ppermute(values, offset, pairs)


def sync(*values):
    leaves, tree = jax.tree.flatten(values)
    return jax.tree.unflatten(tree, lax.optimization_barrier(leaves))


STAGES = (((),), ((X,), (Y,), (Z,)), ((X, Z), (X, Y), (Z, Y), (X, Z, Y)))


def other_core(arrays):
    return swap(arrays[0] if len(arrays) == 1 else jnp.concatenate(arrays, axis=0), C)


def add_low(left, right):
    return (left.astype(F32) + right.astype(F32)).astype(BF16)


def send_home(stage, here, other):
    total = add_low(here, other)
    return [total[n] if not offset else swap_cube(total[n], offset) for n, offset in enumerate(STAGES[stage])]


def take(partial, block):
    return lax.dynamic_index_in_dim(partial, block, 0, keepdims=False)


def send_far(partial, za):
    return [swap(take(partial, za ^ k), "za", k) for k in range(1, lax.axis_size("za"))]


def add_far(partial, got, za):
    total = take(partial, za).astype(F32)
    for g in got:
        total = total + g.astype(F32)
    return total


def per_device(
    tokens, bounds, cotangent, attn_gain, query_weight, key_matrix, value_matrix,
    query_gain, key_gain, out_weight, ffn_gain, gate_weight, up_weight, down_weight,
):
    fsdp = ("fo", "fi")
    seq = ("za", "zb", "si")
    rows, width = tokens.shape
    f_count = lax.axis_size(fsdp)
    s_count = lax.axis_size(seq)
    far = lax.axis_size("za")
    f_index = lax.axis_index(fsdp)
    s_index = lax.axis_index(seq)
    za, zb, si = lax.axis_index("za"), lax.axis_index("zb"), lax.axis_index("si")
    length = rows * s_count
    heads = QUERY_HEADS // s_count
    copies = max(1, s_count // KEY_VALUE_HEADS)
    assert KEY_VALUE_HEADS * copies == s_count
    q_cols = heads * HEAD_SIZE
    cols = q_cols + 2 * HEAD_SIZE
    padded = -(-cols // LANES) * LANES
    all_q, all_kv = QUERY_HEADS * HEAD_SIZE, KEY_VALUE_HEADS * HEAD_SIZE

    pieces = [
        query_weight.reshape(-1, s_count, q_cols),
        jnp.repeat(key_matrix.reshape(-1, KEY_VALUE_HEADS, HEAD_SIZE), copies, axis=1),
        jnp.repeat(value_matrix.reshape(-1, KEY_VALUE_HEADS, HEAD_SIZE), copies, axis=1),
    ]
    kv_start = (s_index // copies) * HEAD_SIZE
    own_cols = [
        lax.dynamic_slice_in_dim(query_weight, s_index * q_cols, q_cols, 1),
        lax.dynamic_slice_in_dim(key_matrix, kv_start, HEAD_SIZE, 1),
        lax.dynamic_slice_in_dim(value_matrix, kv_start, HEAD_SIZE, 1),
    ]
    if padded > cols:
        pieces.append(jnp.zeros(pieces[0].shape[:2] + (padded - cols,), BF16))
        own_cols.append(jnp.zeros((query_weight.shape[0], padded - cols), BF16))
    w_own = lax.all_gather(jnp.concatenate(own_cols, axis=1), fsdp, axis=0, tiled=True)
    out_full = lax.all_gather(out_weight, fsdp, axis=0, tiled=True)
    w_rows = jnp.concatenate(pieces, axis=2).reshape(-1, s_count * padded)
    w_quarter = w_rows.shape[0] // 4
    w_parts = [w_rows[:w_quarter], w_rows[w_quarter:2 * w_quarter], w_rows[2 * w_quarter:]]

    far_list = [(k, swap(tokens, "za", k)) for k in range(1, far)]
    x_y, x_z, c_x = swap(tokens, Y), swap(tokens, Z), swap(cotangent, X)
    ids = jnp.arange(length, dtype=jnp.int32)
    b0, b1 = bounds[0, 0], bounds[0, 1]
    starts = jnp.where(ids >= b1, b1, jnp.where(ids >= b0, b0, 0))
    frequency = ROPE_BASE ** (-(jnp.arange(HEAD_SIZE // 2, dtype=F32) * 2.0 / HEAD_SIZE))
    phases = (ids - starts).astype(F32)[:, None] * frequency[None, :]
    cosine, sine = jnp.cos(phases), jnp.sin(phases)
    cos2 = jnp.concatenate([cosine] * 4, axis=1)
    sin2 = jnp.concatenate([-sine, sine] * 2, axis=1)
    head_gain = jnp.concatenate(
        [query_gain] * heads + [key_gain] + [jnp.ones((padded - cols + HEAD_SIZE,), F32)]
    )[None, :]
    far_list, x_y, x_z, c_x, w_rows, w_parts, cos2, sin2 = sync(
        [b for _, b in far_list], x_y, x_z, c_x, w_rows, w_parts, cos2, sin2
    )

    def some_project(blocks, held):
        index = jnp.stack([((za ^ k) * 2 + (zb ^ dz)) * 2 + (si ^ dy) for (k, dz, dy), _ in blocks])
        return project(
            heads, [b for _, b in blocks], index.astype(jnp.int32), bounds[0], attn_gain[None, :], w_own, head_gain,
            cos2, sin2, length, held,
        )

    far_y = [swap(b, Y) for b in far_list]
    far_z = [swap(b, Z) for b in far_list]
    held = some_project([((0, 0, 0), tokens), ((0, 0, 1), x_y), ((0, 1, 0), x_z)], None)
    far_y, far_z, held, x_y = sync(far_y, far_z, held, x_y)
    x_yz = swap(x_y, Z)
    far_yz = [swap(b, Y) for b in far_z]
    for n, k in enumerate(range(1, far)):
        held = some_project([((k, 0, 0), far_list[n]), ((k, 0, 1), far_y[n]), ((k, 1, 0), far_z[n])], held)
    w_c = swap(w_rows, C)
    c_own_other = other_core([cotangent])
    x_yz, far_yz, held, w_c, c_own_other, cot, c_x, w_parts = sync(
        x_yz, far_yz, held, w_c, c_own_other, cotangent, c_x, w_parts
    )
    c_y, c_z = swap(cot, Y), swap(cot, Z)
    w_x = [swap(w_parts[0], X)]
    mid = rows // 2
    c_xy, c_xz = [swap(c_x[:mid], Y)], [swap(c_x[:mid], Z)]
    held = some_project([((0, 1, 1), x_yz)] + [((k, 1, 1), far_yz[n]) for n, k in enumerate(range(1, far))], held)
    normed, q, k, v, unit, scale = held
    attended_low, attended, q2 = attend(heads, q, k, v)
    c_y, c_z, attended_low, c_x, c_xy, c_xz, w_x = sync(c_y, c_z, attended_low, c_x, c_xy, c_xz, w_x)
    heads_out = lax.all_to_all(attended_low, seq, split_axis=0, concat_axis=1, tiled=True)
    c_xyz = [swap(c_xy[0], Z)]
    c_xy.append(swap(c_y[mid:], X))
    c_xz.append(swap(c_z[mid:], X))
    c_yz = swap(c_z, Y)
    c_one = [c_x, c_y, c_z]
    c_one_other = other_core(c_one)
    c_xyz.append(swap(c_xz[1], Y))
    heads_out, c_xz, c_xy, c_yz, c_xyz, c_one_other = sync(heads_out, c_xz, c_xy, c_yz, c_xyz, c_one_other)
    c_two = [c_xz, c_xy, [c_yz], c_xyz]

    inputs = tokens.astype(F32)
    square_one = jnp.mean(inputs * inputs, axis=1, keepdims=True)
    scale_one = lax.rsqrt(square_one + EPSILON)
    residual = inputs + dot(heads_out, out_full)
    square_two = jnp.mean(residual * residual, axis=1, keepdims=True)
    scale_two = lax.rsqrt(square_two + EPSILON)
    inner = (residual * scale_two * ffn_gain).astype(BF16)
    (inner,) = sync(inner)

    units = gate_weight.shape[1]
    part = units // s_count
    mine = far * part
    own_block = zb * 2 + si
    if part % LANES == 0:
        weights = (gate_weight, up_weight, down_weight)
        unit_index = (jnp.arange(far, dtype=jnp.int32) * 4 + own_block).astype(jnp.int32)
        width_of_part = part
    else:
        pick = lambda w: lax.dynamic_index_in_dim(
            w.reshape(width, far, 4, part), own_block, 2, keepdims=False
        ).reshape(width, mine)
        weights = (
            pick(gate_weight),
            pick(up_weight),
            lax.dynamic_index_in_dim(
                down_weight.reshape(far, 4, part, width), own_block, 1, keepdims=False
            ).reshape(mine, width),
        )
        unit_index = jnp.zeros((1,), jnp.int32)
        width_of_part = mine
    run = lambda x_stage, c_stage: feed(x_stage, c_stage, unit_index, weights, width_of_part)
    x, y, z = swap(inner, X), swap(inner, Y), swap(inner, Z)
    x_stages = [([[inner]], [other_core([inner])])]
    c_stages = [([[cot]], [c_own_other])]
    fed = [run(x_stages[0], c_stages[0])]
    x, y, z, fed, inner, c_two = sync(x, y, z, fed, inner, c_two)
    xy, xz, yz = swap(x, Y), swap(z, X), swap(y, Z)
    xyz = swap_cube(inner, (X, Z, Y))
    x_stages.append(([[x], [y], [z]], [other_core([x, y, z])]))
    c_stages.append(([[c] for c in c_one], [c_one_other]))
    c_two_other = other_core(sum(c_two, []))
    fed.append(run(x_stages[1], c_stages[1]))
    xy, xz, yz, xyz, fed, x_stages, w_parts, c_two, c_two_other = sync(
        xy, xz, yz, xyz, fed, x_stages, w_parts, c_two, c_two_other
    )
    x_stages.append(([[xz], [xy], [yz], [xyz]], [other_core([xz, xy, yz, xyz])]))
    c_stages.append((c_two, [c_two_other]))
    d_home = send_home(0, fed[0][0], swap(fed[0][1], C)) + send_home(1, fed[1][0], swap(fed[1][1], C))
    w_x.append(swap(w_parts[1], X))
    fed.append(run(x_stages[2], c_stages[2]))
    d_home, fed, x_stages, w_x = sync(d_home, fed, x_stages, w_x)
    far_xz, far_xy, far_yz, far_xyz = add_low(fed[2][0], swap(fed[2][1], C))
    hops = [swap(far_xyz, Y), swap(far_xy, X), swap(far_yz, Z)]
    down_part = down_grad([f[4] for f in fed], c_stages)
    far_xz, hops, d_home, down_part, fed = sync(far_xz, hops, d_home, down_part, fed)
    d_home += [swap_cube(add_low(far_xz, hops[0]), (X, Z)), swap(add_low(hops[1], hops[2]), Y)]
    m_other = [swap(f[3], C) for f in fed[:2]]
    gate_part, up_part = gate_grad(x_stages, [f[5] for f in fed])
    d_home, down_part, gate_part, up_part, fed, m_other, heads_out = sync(
        d_home, down_part, gate_part, up_part, fed, m_other, heads_out
    )
    gate_far = lax.psum_scatter(gate_part, "za", scatter_dimension=0, tiled=True)
    up_far = lax.psum_scatter(up_part, "za", scatter_dimension=0, tiled=True)
    down_far = lax.psum_scatter(down_part, "za", scatter_dimension=0, tiled=True)
    quarter = width // far // 4

    def owner_block(values, offset):
        return lax.dynamic_slice_in_dim(values, (own_block ^ offset) * quarter, quarter, 0)

    def to_owners(gates, ups):
        spread = []
        for offset, axes in enumerate(((), (Y,), (Z,), (Z, Y))):
            both = jnp.concatenate([owner_block(gates, offset), owner_block(ups, offset)], axis=0)
            spread.append(swap_cube(both, axes) if axes else both)
        return spread

    m_other.append(swap(fed[2][3], C))
    own_rows = out_weight.shape[0]
    left = []
    for offset in range(f_count):
        block = lax.dynamic_slice_in_dim(heads_out, (f_index ^ offset) * own_rows, own_rows, 1)
        left.append(swap(block, fsdp, offset) if offset else block)
    d_inner = sum(a.astype(F32) for a in d_home)
    ffn_part = jnp.sum(d_inner * residual * scale_two, axis=0)
    weighted = d_inner * ffn_gain
    d_residual = cotangent.astype(F32) + scale_two * (
        weighted - residual * scale_two * scale_two * jnp.mean(weighted * residual, axis=1, keepdims=True)
    )
    d_branch = d_residual.astype(BF16)
    d_heads = dot(d_branch, out_full, NT).astype(BF16)
    d_heads, d_branch, m_other, fed, left = sync(d_heads, d_branch, m_other, fed, left)
    d_attended = lax.all_to_all(d_heads, seq, split_axis=1, concat_axis=0, tiled=True)
    over = swap(d_branch, X)
    right = [d_branch, swap(d_branch, C), over, swap(over, C)]
    m = [add_low(f[2], other) for f, other in zip(fed[:2], m_other)]
    m.append([add_low(fed[2][2][n], m_other[2][n]) for n in range(4)])
    m_far = swap(m[2][3], Y)
    d_attended, right, m, m_far, w_parts, w_x = sync(d_attended, right, m, m_far, w_parts, w_x)
    w_x.append(swap(w_parts[2], X))
    w_xc = [swap(jnp.concatenate(w_x[:2], axis=0), C)]
    out_part = dot(jnp.concatenate(left, axis=0), jnp.concatenate(right, axis=0), TN).astype(BF16)
    out_part = out_part.reshape(far, 2, 2, -1, width)
    pick = lambda values, index, axis: lax.dynamic_index_in_dim(values, index, axis, keepdims=False)
    out_y = swap(pick(out_part, 1 - si, 2), Y)
    d_qkv, gain_parts = attend_back(
        heads, q2, k, v, sync(d_attended, out_part)[0], attended, unit, scale, head_gain, cos2, sin2
    )
    d_qkv, gain_parts, m, m_far, w_x, w_xc, out_part, out_y = sync(
        d_qkv, gain_parts, m, m_far, w_x, w_xc, out_part, out_y
    )
    d_tok = lax.all_to_all(d_qkv, seq, split_axis=0, concat_axis=1, tiled=True)
    proj_part = dot(normed, d_qkv, TN).astype(BF16).reshape(2, 2, width // 4, padded)
    fi, fo = lax.axis_index(C), lax.axis_index(X)
    proj_core = add_low(pick(proj_part, fi, 1), swap(pick(proj_part, 1 - fi, 1), C))
    proj_x = swap(take(proj_core, 1 - fo), X)
    w_xc.append(swap(w_x[2], C))
    m_x, m_yz = swap(m[2][1], X), swap(m[2][2], Y)
    out_part = add_low(pick(out_part, si, 2), out_y)
    m_xz = add_low(m[2][0], m_far)
    d_tok, proj_core, proj_x, w_xc, out_part, m, m_x, m_yz, m_xz, gain_parts, gate_far, up_far = sync(
        d_tok, proj_core, proj_x, w_xc, out_part, m, m_x, m_yz, m_xz, gain_parts, gate_far, up_far
    )
    m_z = [swap(m_xz, X), m_yz]
    spread = to_owners(gate_far, up_far)
    blocks = [w_rows, w_c, jnp.concatenate(w_x, axis=0), jnp.concatenate(w_xc, axis=0)]
    by_offset = jnp.stack([dot(d_tok, w, NT) for w in blocks])
    d_normed = jnp.concatenate([take(by_offset, f_index ^ n) for n in range(f_count)], axis=1)
    weighted = d_normed * attn_gain
    input_grad = (
        d_residual
        + scale_one
        * (weighted - inputs * scale_one * scale_one * jnp.mean(weighted * inputs, axis=1, keepdims=True))
    ).astype(BF16)
    proj_rows = add_low(take(proj_core, fo), proj_x)
    m_one = [m[1][0], add_low(m[1][1], m_x)]
    m_z, spread, input_grad, proj_rows, m, m_one, out_part, gain_parts = sync(
        m_z, spread, input_grad, proj_rows, m, m_one, out_part, gain_parts
    )
    proj = lax.all_to_all(proj_rows, seq, split_axis=0, concat_axis=1, tiled=True)
    m_last = [swap(m_one[0], X), swap(m_one[1], Y)]
    m_one.append((m[1][2].astype(F32) + m_z[0].astype(F32) + m_z[1].astype(F32)).astype(BF16))
    out_z = swap(pick(out_part, 1 - zb, 1), Z)
    gain_row = gain_parts[0]
    pack = jnp.concatenate(
        [
            ffn_part,
            gain_row[:q_cols].reshape(heads, HEAD_SIZE).sum(axis=0),
            gain_row[q_cols:q_cols + HEAD_SIZE],
        ]
    ).reshape(-1, LANES)
    for axis in ("fi", "fo", "si", "zb", "za"):
        offset = 1
        while offset < lax.axis_size(axis):
            pack = pack + swap(pack, axis, offset)
            offset *= 2
    pack = pack.reshape(-1)
    gate_mine, up_mine = place(spread, own_block, part)
    proj, gate_mine, up_mine, m, m_one, m_last, out_part, out_z, down_far, pack = sync(
        proj, gate_mine, up_mine, m, m_one, m_last, out_part, out_z, down_far, pack
    )
    out_part = add_low(pick(out_part, zb, 1), out_z)
    out_got = send_far(out_part, za)
    m_last.append(swap(m_one[2], Z))
    down_mine = down_far.astype(F32)
    mlp_out = m[0][0].astype(F32) + sum(a.astype(F32) for a in m_last)
    block_output = (residual + mlp_out).astype(BF16)
    out_mine = add_far(out_part, out_got, za)
    proj = proj.astype(F32)
    count = proj.shape[0]
    by_device = proj.reshape(count, s_count, padded)

    def fold(values):
        return values.reshape(count, KEY_VALUE_HEADS, copies, HEAD_SIZE).sum(axis=2).reshape(count, -1)

    query_mine = by_device[:, :, :q_cols].reshape(count, QUERY_HEADS * HEAD_SIZE)
    key_mine = fold(by_device[:, :, q_cols:q_cols + HEAD_SIZE])
    value_mine = fold(by_device[:, :, q_cols + HEAD_SIZE:cols])

    my_w = lax.dynamic_slice_in_dim(w_rows, s_index * count, count, 0).astype(F32)
    my_gain = lax.dynamic_slice_in_dim(attn_gain, (f_index * s_count + s_index) * count, count, 0)
    attn_gain_mine = jnp.sum(my_w * proj, axis=1) / my_gain
    ffn_gain_mine = lax.dynamic_slice_in_dim(pack, (f_index * s_count + s_index) * count, count, 0)
    attn_rms = jnp.sqrt(square_one + EPSILON)[:, 0]
    mlp_rms = jnp.sqrt(square_two + EPSILON)[:, 0]
    return (
        block_output, input_grad, residual, attn_rms, mlp_rms, attn_gain_mine,
        query_mine, key_mine, value_mine, pack[width:width + HEAD_SIZE], pack[width + HEAD_SIZE:],
        out_mine, ffn_gain_mine, gate_mine, up_mine, down_mine,
    )


def solution(mesh):
    f_count, s_count = mesh.shape["fsdp"], mesh.shape["seq"]
    fine = Mesh(
        mesh.devices.reshape(f_count // 2, 2, s_count // 4, 2, 2), ("fo", "fi", "za", "zb", "si")
    )
    f, s = ("fo", "fi"), ("za", "zb", "si")
    every = P(f + s, None)
    vector = P(f + s)
    placed = (
        every, P(f, None), every, P(), P(f, None), P(f, None), P(f, None), P(), P(),
        P(f, None), P(), P(None, f), P(None, f), P(f, None),
    )
    return jax.shard_map(
        per_device,
        mesh=fine,
        in_specs=placed,
        out_specs=(
            every, every, every, vector, vector, vector, every, every, every, P(), P(),
            every, vector, P(s, f), P(s, f), every,
        ),
        check_vma=False,
    )
```

```python
import functools

import jax
import jax.numpy as jnp
from jax import lax
from jax.experimental import pallas as pl
from jax.experimental.pallas import tpu as pltpu
from jax.sharding import Mesh, PartitionSpec as P

HEAD_SIZE = 64
QUERY_HEADS = 32
KEY_VALUE_HEADS = 8
EPSILON = 1e-05
ROPE_BASE = 1000000.0
BIG = 30000.0
LANES = 128
BLOCK = 256
UNROLLED = 2048
VMEM = 60 * 1024 * 1024
COST = pl.CostEstimate(flops=1000, bytes_accessed=1000, transcendentals=0)

F32 = jnp.float32
BF16 = jnp.bfloat16
NT = (((1,), (1,)), ((), ()))
TN = (((0,), (0,)), ((), ()))


def dot(left, right, dims=(((1,), (0,)), ((), ()))):
    return lax.dot_general(left, right, dims, preferred_element_type=F32)


def split_low(values):
    high = values.astype(BF16)
    return high, (values - high.astype(F32)).astype(BF16)


def head_means(values, ones):
    high, low = split_low(values)
    return (dot(high, ones) + dot(low, ones)) * (1.0 / HEAD_SIZE)


def head_ones():
    row = lax.broadcasted_iota(jnp.int32, (LANES, LANES), 0) // HEAD_SIZE
    col = lax.broadcasted_iota(jnp.int32, (LANES, LANES), 1) // HEAD_SIZE
    return jnp.where(row == col, 1.0, 0.0).astype(BF16)


def swap_halves(values):
    lane = lax.broadcasted_iota(jnp.int32, values.shape, 1) % HEAD_SIZE
    half = HEAD_SIZE // 2
    return jnp.where(
        lane < half, pltpu.roll(values, LANES - half, 1), pltpu.roll(values, half, 1)
    )


def project_kernel(heads, count, fresh, index_ref, bounds_ref, *refs):
    x_refs = refs[:count]
    gain_ref, w_ref, head_gain_ref, cos_ref, sin_ref = refs[count:count + 5]
    refs = refs[count + 5 + (0 if fresh else 6):]
    normed_ref, q_ref, k_ref, v_ref, unit_ref, scale_ref, x_scr = refs
    i = pl.program_id(0)
    rows = x_scr.shape[0]
    for r in range(count):
        @pl.when(i == r)
        def _(r=r):
            x_scr[...] = x_refs[r][...]

    x = x_scr[...].astype(F32)
    scale = lax.rsqrt(jnp.mean(x * x, axis=1, keepdims=True) + EPSILON)
    normed = (x * scale * gain_ref[...]).astype(BF16)
    normed_ref[...] = normed
    pre = dot(normed, w_ref[...])
    cosine, sine = cos_ref[...], sin_ref[...]
    shape = (rows, LANES)
    token = index_ref[i] * rows + lax.broadcasted_iota(jnp.int32, shape, 0)
    doc = (token >= bounds_ref[0]).astype(jnp.int32) + (token >= bounds_ref[1]).astype(jnp.int32)
    lane = lax.broadcasted_iota(jnp.int32, shape, 1)
    mark = lane - HEAD_SIZE
    query_marks = jnp.where(mark == doc, 1.0, 0.0)
    key_marks = jnp.where(mark < 3, jnp.where(mark == doc, 0.0, -BIG), jnp.where(mark < 5, 1.0, 0.0))
    value_marks = jnp.where(mark < 2, 1.0, 0.0)
    ones = head_ones()

    def place(values, segment, marks):
        group = values if segment % 2 == 0 else pltpu.roll(values, HEAD_SIZE, 1)
        return jnp.where(lane < HEAD_SIZE, group, marks).astype(BF16)

    for g in range(pre.shape[1] // LANES):
        cols = slice(g * LANES, (g + 1) * LANES)
        u = pre[:, cols]
        r = lax.rsqrt(head_means(u * u, ones) + EPSILON)
        unit = u * r
        unit_ref[:, cols] = unit
        scale_ref[:, cols] = r
        gained = unit * head_gain_ref[0:1, cols]
        rot = (gained * cosine + swap_halves(gained) * sine).astype(BF16).astype(F32)
        for segment in (2 * g, 2 * g + 1):
            if segment < heads:
                q_ref[segment] = place(rot * 0.125, segment, query_marks)
            elif segment == heads:
                k_ref[...] = place(rot, segment, key_marks)
            elif segment == heads + 1:
                v_ref[...] = place(u, segment, value_marks)


def project(heads, blocks, index, bounds, gain, w, head_gain, cosine, sine, length, held=None):
    rows, width = blocks[0].shape
    count = len(blocks)
    cols = w.shape[1]
    row = lambda c: pl.BlockSpec((rows, c), lambda i, n, b: (n[i], 0))
    whole = lambda a: pl.BlockSpec(a.shape, lambda i, n, b: (0, 0))
    fresh = held is None
    held = () if fresh else held
    outs = [
        jax.ShapeDtypeStruct((length, width), BF16),
        jax.ShapeDtypeStruct((heads, length, LANES), BF16),
        jax.ShapeDtypeStruct((length, LANES), BF16),
        jax.ShapeDtypeStruct((length, LANES), BF16),
        jax.ShapeDtypeStruct((length, cols), F32),
        jax.ShapeDtypeStruct((length, cols), F32),
    ]
    tokens = rows * count
    return pl.pallas_call(
        functools.partial(project_kernel, heads, count, fresh),
        grid_spec=pltpu.PrefetchScalarGridSpec(
            num_scalar_prefetch=2,
            grid=(count,),
            in_specs=[whole(b) for b in blocks]
            + [whole(gain), whole(w), whole(head_gain), row(LANES), row(LANES)]
            + [pl.BlockSpec(memory_space=pl.ANY)] * len(held),
            out_specs=[
                row(width),
                pl.BlockSpec((heads, rows, LANES), lambda i, n, b: (0, n[i], 0)),
                row(LANES),
                row(LANES),
                row(cols),
                row(cols),
            ],
            scratch_shapes=[pltpu.VMEM((rows, width), BF16)],
        ),
        out_shape=outs,
        input_output_aliases={2 + count + 5 + n: n for n in range(len(held))},
        compiler_params=pltpu.CompilerParams(vmem_limit_bytes=VMEM),
        cost_estimate=COST,
        name="project",
    )(index, bounds, *blocks, gain, w, head_gain, cosine, sine, *held)


def attend_kernel(heads, q_ref, k_ref, v_ref, low_ref, out_ref, q2_ref):
    i = pl.program_id(0)
    rows = BLOCK
    q = q_ref[...].reshape(heads * rows, LANES)

    def step(j, total):
        start = pl.multiple_of(j * rows, rows)
        p = jnp.exp(dot(q, k_ref[pl.ds(start, rows), :], NT)).astype(BF16)
        return total + dot(p, v_ref[pl.ds(start, rows), :])

    total = lax.fori_loop(0, i, step, jnp.zeros((heads * rows, LANES), F32))
    start = pl.multiple_of(i * rows, rows)
    s = dot(q, k_ref[pl.ds(start, rows), :], NT)
    t_local = lax.broadcasted_iota(jnp.int32, s.shape, 0) % rows
    u_local = lax.broadcasted_iota(jnp.int32, s.shape, 1)
    p = jnp.where(u_local <= t_local, jnp.exp(s), 0.0).astype(BF16)
    total = total + dot(p, v_ref[pl.ds(start, rows), :])
    weight = total[:, HEAD_SIZE:HEAD_SIZE + 1]
    out = total[:, :HEAD_SIZE] / weight
    for h in range(heads):
        part = out[h * rows:(h + 1) * rows, :]
        out_ref[:, h * HEAD_SIZE:(h + 1) * HEAD_SIZE] = part
        low_ref[:, h * HEAD_SIZE:(h + 1) * HEAD_SIZE] = part.astype(BF16)
    high, low = split_low(-jnp.log(weight))
    lane = lax.broadcasted_iota(jnp.int32, q.shape, 1)
    q2 = jnp.where(lane == HEAD_SIZE + 3, high, jnp.where(lane == HEAD_SIZE + 4, low, q))
    q2_ref[...] = q2.reshape(heads, rows, LANES)


def attend_unrolled_kernel(heads, rows, q_ref, k_ref, v_ref, low_ref, out_ref, q2_ref):
    stretch = q_ref.shape[1]

    def block(first, at):
        q = q_ref[:, at:at + rows, :].reshape(heads * rows, LANES)
        s = dot(q, k_ref[first:first + rows, :], NT)
        t_local = lax.broadcasted_iota(jnp.int32, s.shape, 0) % rows
        u_local = lax.broadcasted_iota(jnp.int32, s.shape, 1)
        p = jnp.where(u_local <= t_local, jnp.exp(s), 0.0).astype(BF16)
        total = dot(p, v_ref[first:first + rows, :])
        if first:
            p = jnp.exp(dot(q, k_ref[:first, :], NT)).astype(BF16)
            total = total + dot(p, v_ref[:first, :])
        weight = total[:, HEAD_SIZE:HEAD_SIZE + 1]
        out = total[:, :HEAD_SIZE] / weight
        for h in range(heads):
            part = out[h * rows:(h + 1) * rows, :]
            out_ref[at:at + rows, h * HEAD_SIZE:(h + 1) * HEAD_SIZE] = part
            low_ref[at:at + rows, h * HEAD_SIZE:(h + 1) * HEAD_SIZE] = part.astype(BF16)
        high, low = split_low(-jnp.log(weight))
        lane = lax.broadcasted_iota(jnp.int32, q.shape, 1)
        q2 = jnp.where(lane == HEAD_SIZE + 3, high, jnp.where(lane == HEAD_SIZE + 4, low, q))
        q2_ref[:, at:at + rows, :] = q2.reshape(heads, rows, LANES)

    for step in range(k_ref.shape[0] // stretch):
        @pl.when(pl.program_id(0) == step)
        def _(step=step):
            for at in range(0, stretch, rows):
                block(step * stretch + at, at)


def attend(heads, q, k, v):
    tokens = k.shape[0]
    if tokens <= UNROLLED and tokens % (2 * BLOCK) == 0:
        kernel, rows = functools.partial(attend_unrolled_kernel, heads, BLOCK // 2), 2 * BLOCK
    else:
        kernel, rows = functools.partial(attend_kernel, heads), BLOCK
    return pl.pallas_call(
        kernel,
        grid=(tokens // rows,),
        in_specs=[
            pl.BlockSpec((heads, rows, LANES), lambda i: (0, i, 0)),
            pl.BlockSpec((tokens, LANES), lambda i: (0, 0)),
            pl.BlockSpec((tokens, LANES), lambda i: (0, 0)),
        ],
        out_specs=[
            pl.BlockSpec((rows, heads * HEAD_SIZE), lambda i: (i, 0)),
            pl.BlockSpec((rows, heads * HEAD_SIZE), lambda i: (i, 0)),
            pl.BlockSpec((heads, rows, LANES), lambda i: (0, i, 0)),
        ],
        out_shape=[
            jax.ShapeDtypeStruct((tokens, heads * HEAD_SIZE), BF16),
            jax.ShapeDtypeStruct((tokens, heads * HEAD_SIZE), F32),
            jax.ShapeDtypeStruct((heads, tokens, LANES), BF16),
        ],
        compiler_params=pltpu.CompilerParams(vmem_limit_bytes=VMEM),
        cost_estimate=COST,
        name="attend",
    )(q, k, v)


def attend_back_kernel(heads, q_ref, k_ref, v_ref, grad_ref, out_ref, unit_hbm, scale_hbm, head_gain_ref,
                       cos_hbm, sin_hbm, dqkv_ref, gains_ref, g_scr, dq_scr, dk_scr, dv_scr,
                       unit_ref, scale_ref, cos_ref, sin_ref, sems):
    rows = BLOCK
    tokens = k_ref.shape[0]
    blocks = tokens // rows
    wide = heads * rows
    late = [
        pltpu.make_async_copy(source, target, sems.at[n])
        for n, (source, target) in enumerate(
            ((unit_hbm, unit_ref), (scale_hbm, scale_ref), (cos_hbm, cos_ref), (sin_hbm, sin_ref))
        )
    ]
    for copy in late:
        copy.start()

    def prepare(i, carry):
        at = pl.ds(pl.multiple_of(i * rows, rows), rows)
        lane = lax.broadcasted_iota(jnp.int32, (rows, HEAD_SIZE), 1)
        for h in range(heads):
            cols = slice(h * HEAD_SIZE, (h + 1) * HEAD_SIZE)
            grad = grad_ref[at, cols]
            delta = jnp.sum(grad.astype(F32) * out_ref[at, cols], axis=1, keepdims=True)
            high, low = split_low(-delta)
            g_scr[h, at, :HEAD_SIZE] = grad
            g_scr[h, at, HEAD_SIZE:] = jnp.where(lane == 0, high, jnp.where(lane == 1, low, jnp.zeros_like(low)))
        dq_scr[:, at, :] = jnp.zeros((heads, rows, LANES), F32)
        return carry

    lax.fori_loop(0, blocks, prepare, 0)

    def pair(j, i, diagonal):
        at = pl.ds(i * rows, rows)
        k = k_ref[pl.ds(j * rows, rows), :]
        q = q_ref[:, at, :].reshape(wide, LANES)
        g = g_scr[:, at, :].reshape(wide, LANES)
        p = jnp.exp(dot(k, q, NT))
        if diagonal:
            u_local = lax.broadcasted_iota(jnp.int32, p.shape, 0)
            t_local = lax.broadcasted_iota(jnp.int32, p.shape, 1) % rows
            p = jnp.where(u_local <= t_local, p, 0.0)
        dv = dot(p.astype(BF16), g)
        ds = (p * dot(v_ref[pl.ds(j * rows, rows), :], g, NT)).astype(BF16)
        dk = dot(ds, q)
        dq_scr[:, at, :] += dot(ds, k, TN).reshape(heads, rows, LANES)
        return dk, dv

    def key_step(j, carry):
        def query_step(i, state):
            dk, dv = pair(j, i, False)
            return state[0] + dk, state[1] + dv

        state = pair(j, j, True)
        if tokens <= UNROLLED:
            for i in range(j + 1, blocks):
                state = query_step(i, state)
        else:
            state = lax.fori_loop(j + 1, blocks, query_step, state)
        dk_scr[pl.ds(j * rows, rows), :] = state[0]
        dv_scr[pl.ds(j * rows, rows), :] = state[1]
        return carry

    if tokens <= UNROLLED:
        for j in range(blocks):
            key_step(j, 0)
    else:
        lax.fori_loop(0, blocks, key_step, 0)
    for copy in late:
        copy.wait()
    groups = unit_ref.shape[1] // LANES
    ones = head_ones()

    def finish(i, carry):
        at = pl.ds(pl.multiple_of(i * rows, rows), rows)
        cosine, sine = cos_ref[at, :], sin_ref[at, :]
        lane = lax.broadcasted_iota(jnp.int32, (rows, LANES), 1)

        def segment_of(s):
            if s < heads:
                return dq_scr[s, at, :] * 0.125
            return (dk_scr if s == heads else dv_scr)[at, :]

        sums = list(carry)
        for g in range(groups):
            cols = slice(g * LANES, (g + 1) * LANES)
            first = segment_of(2 * g)
            last = segment_of(2 * g + 1) if 2 * g + 1 < heads + 2 else first
            d = jnp.where(lane < HEAD_SIZE, first, pltpu.roll(last, HEAD_SIZE, 1))
            e = d * cosine - swap_halves(d) * sine
            unit = unit_ref[at, cols]
            sums[g] = sums[g] + jnp.sum(e * unit, axis=0, keepdims=True)
            w = e * head_gain_ref[0:1, cols]
            normal = scale_ref[at, cols] * (w - unit * head_means(w * unit, ones))
            is_value = lane + g * LANES >= (heads + 1) * HEAD_SIZE
            dqkv_ref[at, cols] = jnp.where(is_value, d, normal).astype(BF16)
        return tuple(sums)

    zero = jnp.zeros((1, LANES), F32)
    sums = lax.fori_loop(0, blocks, finish, (zero,) * groups)
    gains_ref[...] = jnp.zeros(gains_ref.shape, F32)
    for g in range(groups):
        gains_ref[0:1, g * LANES:(g + 1) * LANES] = sums[g]


def attend_back(heads, q, k, v, grad, out, unit, scale, head_gain, cosine, sine):
    tokens = k.shape[0]
    cols = unit.shape[1]
    vmem, late = pl.BlockSpec(memory_space=pltpu.VMEM), pl.BlockSpec(memory_space=pl.ANY)
    return pl.pallas_call(
        functools.partial(attend_back_kernel, heads),
        in_specs=[vmem] * 5 + [late] * 2 + [vmem] + [late] * 2,
        out_specs=[vmem] * 2,
        out_shape=[
            jax.ShapeDtypeStruct((tokens, cols), BF16),
            jax.ShapeDtypeStruct((8, cols), F32),
        ],
        scratch_shapes=[
            pltpu.VMEM((heads, tokens, LANES), BF16),
            pltpu.VMEM((heads, tokens, LANES), F32),
            pltpu.VMEM((tokens, LANES), F32),
            pltpu.VMEM((tokens, LANES), F32),
            pltpu.VMEM((tokens, cols), F32),
            pltpu.VMEM((tokens, cols), F32),
            pltpu.VMEM((tokens, LANES), F32),
            pltpu.VMEM((tokens, LANES), F32),
            pltpu.SemaphoreType.DMA((4,)),
        ],
        compiler_params=pltpu.CompilerParams(vmem_limit_bytes=VMEM),
        cost_estimate=COST,
        name="attend_back",
    )(q, k, v, grad, out, unit, scale, head_gain, cosine, sine)


def cut(arrays, sizes, half):
    tiles = [[] for _ in range(sum(sizes) // half)]
    row = 0
    for array, size in zip(arrays, sizes):
        start = 0
        while start < size:
            count = min(size - start, half - row % half)
            tiles[row // half].append((array, start, count))
            start += count
            row += count
    return tiles


def feed_kernel(layouts, weight_count, index_ref, *refs):
    tiles = len(layouts[0][0])
    half = refs[-6].shape[1] // 2
    sides = []
    for pieces, layout in layouts:
        own = []
        for count in pieces:
            own.append(refs[:count])
            refs = refs[count:]
        sides.append((own, cut(refs[:len(layout)], layout, half)))
        refs = refs[len(layout):]
    gate_ref, up_ref, down_ref = refs[:3]
    da_ref, db_ref, ma_ref, mb_ref, hidden_ref, dgu_ref, x_scr, c_scr, gu_scr, down_scr, sem, w_sem = refs[3:]
    i = pl.program_id(0)
    half = x_scr.shape[1] // 2

    def copies(t):
        slot = t % 2
        found = []
        for (own, others), scratch, which in ((sides[0], x_scr, 0), (sides[1], c_scr, 1)):
            size = half // len(own[t])
            for n, piece in enumerate(own[t]):
                found.append(
                    pltpu.make_async_copy(piece, scratch.at[slot, pl.ds(n * size, size)], sem.at[slot, which, n])
                )
            row = half
            for n, (other, start, size) in enumerate(others[t]):
                found.append(
                    pltpu.make_async_copy(
                        other.at[pl.ds(start, size)],
                        scratch.at[slot, pl.ds(row, size)],
                        sem.at[slot, which, n + 2],
                    )
                )
                row += size
        return found

    mine = hidden_ref.shape[1]
    part = mine // weight_count

    def weight_copies(n):
        at = pl.ds(pl.multiple_of(index_ref[n] * part, part), part)
        return [
            pltpu.make_async_copy(gate_ref.at[:, at], gu_scr.at[:, pl.ds(n * part, part)], w_sem.at[n, 0]),
            pltpu.make_async_copy(up_ref.at[:, at], gu_scr.at[:, pl.ds(mine + n * part, part)], w_sem.at[n, 1]),
            pltpu.make_async_copy(down_ref.at[at], down_scr.at[pl.ds(n * part, part)], w_sem.at[n, 2]),
        ]

    for t in range(tiles):
        @pl.when(i == t)
        def _(t=t):
            if t == 0:
                needed = copies(0) + [copy for n in range(weight_count) for copy in weight_copies(n)]
                for copy in needed:
                    copy.start()
            else:
                needed = copies(t)
            if t + 1 < tiles:
                for copy in copies(t + 1):
                    copy.start()
            for copy in needed:
                copy.wait()

    slot = lax.rem(i, 2)
    both = dot(x_scr[slot], gu_scr[...])
    gate, up = both[:, :mine], both[:, mine:]
    d_hidden = dot(c_scr[slot], down_scr[...], NT)
    sigma = 1.0 / (1.0 + jnp.exp(-gate))
    active = gate * sigma
    hidden = (active * up).astype(BF16)
    hidden_ref[...] = hidden
    dgu_ref[:, :mine] = (d_hidden * up * (sigma * (1.0 + gate * (1.0 - sigma)))).astype(BF16)
    dgu_ref[:, mine:] = (d_hidden * active).astype(BF16)
    d_inner = dot(dgu_ref[...], gu_scr[...], NT)
    mlp = dot(hidden, down_scr[...])
    da_ref[0] = d_inner[:half].astype(BF16)
    db_ref[0] = d_inner[half:].astype(BF16)
    ma_ref[0] = mlp[:half].astype(BF16)
    mb_ref[0] = mlp[half:].astype(BF16)


def feed(x_stage, c_stage, index, weights, part):
    (x_own, x_others), (c_own, c_others) = x_stage, c_stage
    tiles = len(x_own)
    half = x_own[0][0].shape[0] * len(x_own[0])
    layouts = tuple(
        (tuple(len(t) for t in own), tuple(o.shape[0] for o in others))
        for own, others in ((x_own, x_others), (c_own, c_others))
    )
    arrays = [a for own, others in ((x_own, x_others), (c_own, c_others)) for a in sum(own, []) + list(others)]
    rows = 2 * half
    gate, up, down = weights
    width = gate.shape[0]
    blocks = index.shape[0]
    mine = blocks * part
    halves = pl.BlockSpec((1, half, width), lambda i, n: (i, 0, 0))
    return pl.pallas_call(
        functools.partial(feed_kernel, layouts, blocks),
        grid_spec=pltpu.PrefetchScalarGridSpec(
            num_scalar_prefetch=1,
            grid=(tiles,),
            in_specs=[pl.BlockSpec(memory_space=pl.ANY)] * (len(arrays) + 3),
            out_specs=[halves] * 4
            + [
                pl.BlockSpec((rows, mine), lambda i, n: (i, 0)),
                pl.BlockSpec((rows, 2 * mine), lambda i, n: (i, 0)),
            ],
            scratch_shapes=[
                pltpu.VMEM((2, rows, width), BF16),
                pltpu.VMEM((2, rows, width), BF16),
                pltpu.VMEM((width, 2 * mine), BF16),
                pltpu.VMEM((mine, width), BF16),
                pltpu.SemaphoreType.DMA((2, 2, 4)),
                pltpu.SemaphoreType.DMA((blocks, 3)),
            ],
        ),
        out_shape=[jax.ShapeDtypeStruct((tiles, half, width), BF16)] * 4
        + [
            jax.ShapeDtypeStruct((tiles * rows, mine), BF16),
            jax.ShapeDtypeStruct((tiles * rows, 2 * mine), BF16),
        ],
        compiler_params=pltpu.CompilerParams(vmem_limit_bytes=VMEM),
        cost_estimate=COST,
        name="feed",
    )(index, *arrays, gate, up, down)


def stage_arrays(stages):
    arrays, layout = [], []
    for own, others in stages:
        half = own[0][0].shape[0] * len(own[0])
        arrays += sum(own, []) + list(others)
        layout.append((half, tuple(len(t) for t in own), tuple(o.shape[0] for o in others)))
    return arrays, tuple(layout)


def stack_rows(refs, layout, scratch):
    at = row = 0
    for half, tiles, others in layout:
        first = at + sum(tiles)
        for pieces, across in zip(tiles, cut(refs[first:first + len(others)], others, half)):
            size = half // pieces
            for n in range(pieces):
                scratch[row:row + size, :] = refs[at + n][...]
                row += size
            at += pieces
            for other, start, size in across:
                scratch[row:row + size, :] = other[start:start + size, :]
                row += size
        at += len(others)


def gate_grad_kernel(array_count, layout, *refs):
    arrays, refs = refs[:array_count], refs[array_count:]
    rights, (out_ref, scratch) = refs[:len(layout)], refs[len(layout):]
    stack_rows(arrays, layout, scratch)
    row = 0
    total = None
    for right in rights:
        size = right.shape[0]
        term = dot(scratch[row:row + size, :], right[...], TN)
        total = term if total is None else total + term
        row += size
    out_ref[...] = total.astype(BF16)


def gate_grad(stages, rights):
    arrays, layout = stage_arrays(stages)
    width = arrays[0].shape[1]
    units = rights[0].shape[1]
    rows = sum(r.shape[0] for r in rights)
    step = min(256, width)
    return pl.pallas_call(
        functools.partial(gate_grad_kernel, len(arrays), layout),
        grid=(width // step,),
        in_specs=[pl.BlockSpec((p.shape[0], step), lambda i: (0, i)) for p in arrays]
        + [pl.BlockSpec(r.shape, lambda i: (0, 0)) for r in rights],
        out_specs=pl.BlockSpec((step, units), lambda i: (i, 0)),
        out_shape=jax.ShapeDtypeStruct((width, units), BF16),
        scratch_shapes=[pltpu.VMEM((rows, step), BF16)],
        compiler_params=pltpu.CompilerParams(vmem_limit_bytes=VMEM),
        cost_estimate=COST,
        name="gate_grad",
    )(*arrays, *rights)


def down_grad_kernel(array_count, layout, *refs):
    arrays, refs = refs[:array_count], refs[array_count:]
    lefts, (out_ref, left_scr, scratch) = refs[:len(layout)], refs[len(layout):]

    @pl.when(pl.program_id(0) == 0)
    def _():
        col = 0
        for left in lefts:
            size = left.shape[0]
            left_scr[:, col:col + size] = left[...].T
            col += size

    stack_rows(arrays, layout, scratch)
    out_ref[...] = dot(left_scr[...], scratch[...]).astype(BF16)


def down_grad(lefts, stages):
    arrays, layout = stage_arrays(stages)
    width = arrays[0].shape[1]
    units = lefts[0].shape[1]
    rows = sum(r.shape[0] for r in lefts)
    step = min(256, width)
    return pl.pallas_call(
        functools.partial(down_grad_kernel, len(arrays), layout),
        grid=(width // step,),
        in_specs=[pl.BlockSpec((p.shape[0], step), lambda i: (0, i)) for p in arrays]
        + [pl.BlockSpec(r.shape, lambda i: (0, 0)) for r in lefts],
        out_specs=pl.BlockSpec((units, step), lambda i: (0, i)),
        out_shape=jax.ShapeDtypeStruct((units, width), BF16),
        scratch_shapes=[pltpu.VMEM((units, rows), BF16), pltpu.VMEM((rows, step), BF16)],
        compiler_params=pltpu.CompilerParams(vmem_limit_bytes=VMEM),
        cost_estimate=COST,
        name="down_grad",
    )(*arrays, *lefts)


def place_kernel(index_ref, *refs):
    parts, outs = refs[:-2], refs[-2:]
    devices = len(parts) // 2
    for d in range(devices):
        @pl.when(pl.program_id(1) == d)
        def _(d=d):
            outs[0][...] = parts[d][...].astype(F32)
            outs[1][...] = parts[devices + d][...].astype(F32)


def place(parts, own, part):
    devices = len(parts)
    rows, mine = parts[0].shape[0], parts[0].shape[1] // 2
    blocks = mine // part
    if part % LANES:
        stack = jnp.stack(parts).reshape(devices, rows, 2, blocks, part)
        stack = jnp.stack([take(stack, own ^ d) for d in range(devices)])
        both = stack.transpose(2, 1, 3, 0, 4).reshape(2, rows, -1).astype(F32)
        return both[0], both[1]
    first = pl.BlockSpec((rows, part), lambda b, d, n: (0, b))
    second = pl.BlockSpec((rows, part), lambda b, d, n: (0, blocks + b))
    return pl.pallas_call(
        place_kernel,
        grid_spec=pltpu.PrefetchScalarGridSpec(
            num_scalar_prefetch=1,
            grid=(blocks, devices),
            in_specs=[first] * devices + [second] * devices,
            out_specs=[pl.BlockSpec((rows, part), lambda b, d, n: (0, b * devices + (n[0] ^ d)))] * 2,
        ),
        out_shape=[jax.ShapeDtypeStruct((rows, devices * mine), F32)] * 2,
        compiler_params=pltpu.CompilerParams(vmem_limit_bytes=VMEM),
        cost_estimate=COST,
        name="place",
    )(own.astype(jnp.int32).reshape(1), *parts, *parts)


X, Y, Z, C = "fo", "si", "zb", "fi"


def swap(values, axis, offset=1):
    size = lax.axis_size(axis)
    return lax.ppermute(values, axis, [(i, i ^ offset) for i in range(size)])


def swap_cube(values, offset):
    if len(offset) == 1:
        return swap(values, offset[0])
    sizes = [lax.axis_size(a) for a in offset]
    total = 1
    for size in sizes:
        total *= size
    pairs = []
    for i in range(total):
        rest, place = i, []
        for size in reversed(sizes):
            place.append(rest % size ^ 1)
            rest //= size
        j = 0
        for size, p in zip(sizes, reversed(place)):
            j = j * size + p
        pairs.append((i, j))
    return lax.ppermute(values, offset, pairs)


def sync(*values):
    leaves, tree = jax.tree.flatten(values)
    return jax.tree.unflatten(tree, lax.optimization_barrier(leaves))


STAGES = (((),), ((X,), (Y,), (Z,)), ((X, Z), (X, Y), (Z, Y), (X, Z, Y)))


def other_core(arrays):
    return swap(arrays[0] if len(arrays) == 1 else jnp.concatenate(arrays, axis=0), C)


def add_low(left, right):
    return (left.astype(F32) + right.astype(F32)).astype(BF16)


def send_home(stage, here, other):
    total = add_low(here, other)
    return [total[n] if not offset else swap_cube(total[n], offset) for n, offset in enumerate(STAGES[stage])]


def take(partial, block):
    return lax.dynamic_index_in_dim(partial, block, 0, keepdims=False)


def send_far(partial, za):
    return [swap(take(partial, za ^ k), "za", k) for k in range(1, lax.axis_size("za"))]


def add_far(partial, got, za):
    total = take(partial, za).astype(F32)
    for g in got:
        total = total + g.astype(F32)
    return total


def per_device(
    tokens, bounds, cotangent, attn_gain, query_weight, key_matrix, value_matrix,
    query_gain, key_gain, out_weight, ffn_gain, gate_weight, up_weight, down_weight,
):
    fsdp = ("fo", "fi")
    seq = ("za", "zb", "si")
    rows, width = tokens.shape
    f_count = lax.axis_size(fsdp)
    s_count = lax.axis_size(seq)
    far = lax.axis_size("za")
    f_index = lax.axis_index(fsdp)
    s_index = lax.axis_index(seq)
    za, zb, si = lax.axis_index("za"), lax.axis_index("zb"), lax.axis_index("si")
    length = rows * s_count
    heads = QUERY_HEADS // s_count
    copies = max(1, s_count // KEY_VALUE_HEADS)
    assert KEY_VALUE_HEADS * copies == s_count
    q_cols = heads * HEAD_SIZE
    cols = q_cols + 2 * HEAD_SIZE
    padded = -(-cols // LANES) * LANES
    all_q, all_kv = QUERY_HEADS * HEAD_SIZE, KEY_VALUE_HEADS * HEAD_SIZE

    pieces = [
        query_weight.reshape(-1, s_count, q_cols),
        jnp.repeat(key_matrix.reshape(-1, KEY_VALUE_HEADS, HEAD_SIZE), copies, axis=1),
        jnp.repeat(value_matrix.reshape(-1, KEY_VALUE_HEADS, HEAD_SIZE), copies, axis=1),
    ]
    kv_start = (s_index // copies) * HEAD_SIZE
    own_cols = [
        lax.dynamic_slice_in_dim(query_weight, s_index * q_cols, q_cols, 1),
        lax.dynamic_slice_in_dim(key_matrix, kv_start, HEAD_SIZE, 1),
        lax.dynamic_slice_in_dim(value_matrix, kv_start, HEAD_SIZE, 1),
    ]
    if padded > cols:
        pieces.append(jnp.zeros(pieces[0].shape[:2] + (padded - cols,), BF16))
        own_cols.append(jnp.zeros((query_weight.shape[0], padded - cols), BF16))
    w_own = lax.all_gather(jnp.concatenate(own_cols, axis=1), fsdp, axis=0, tiled=True)
    out_full = lax.all_gather(out_weight, fsdp, axis=0, tiled=True)
    w_rows = jnp.concatenate(pieces, axis=2).reshape(-1, s_count * padded)
    w_quarter = w_rows.shape[0] // 4
    w_parts = [w_rows[:w_quarter], w_rows[w_quarter:2 * w_quarter], w_rows[2 * w_quarter:]]

    far_list = [(k, swap(tokens, "za", k)) for k in range(1, far)]
    x_y, x_z, c_x = swap(tokens, Y), swap(tokens, Z), swap(cotangent, X)
    ids = jnp.arange(length, dtype=jnp.int32)
    b0, b1 = bounds[0, 0], bounds[0, 1]
    starts = jnp.where(ids >= b1, b1, jnp.where(ids >= b0, b0, 0))
    frequency = ROPE_BASE ** (-(jnp.arange(HEAD_SIZE // 2, dtype=F32) * 2.0 / HEAD_SIZE))
    phases = (ids - starts).astype(F32)[:, None] * frequency[None, :]
    cosine, sine = jnp.cos(phases), jnp.sin(phases)
    cos2 = jnp.concatenate([cosine] * 4, axis=1)
    sin2 = jnp.concatenate([-sine, sine] * 2, axis=1)
    head_gain = jnp.concatenate(
        [query_gain] * heads + [key_gain] + [jnp.ones((padded - cols + HEAD_SIZE,), F32)]
    )[None, :]
    far_list, x_y, x_z, c_x, w_rows, w_parts, cos2, sin2 = sync(
        [b for _, b in far_list], x_y, x_z, c_x, w_rows, w_parts, cos2, sin2
    )

    def some_project(blocks, held):
        index = jnp.stack([((za ^ k) * 2 + (zb ^ dz)) * 2 + (si ^ dy) for (k, dz, dy), _ in blocks])
        return project(
            heads, [b for _, b in blocks], index.astype(jnp.int32), bounds[0], attn_gain[None, :], w_own, head_gain,
            cos2, sin2, length, held,
        )

    far_y = [swap(b, Y) for b in far_list]
    far_z = [swap(b, Z) for b in far_list]
    held = some_project([((0, 0, 0), tokens), ((0, 0, 1), x_y), ((0, 1, 0), x_z)], None)
    far_y, far_z, held, x_y = sync(far_y, far_z, held, x_y)
    x_yz = swap(x_y, Z)
    far_yz = [swap(b, Y) for b in far_z]
    for n, k in enumerate(range(1, far)):
        held = some_project([((k, 0, 0), far_list[n]), ((k, 0, 1), far_y[n]), ((k, 1, 0), far_z[n])], held)
    w_c = swap(w_rows, C)
    c_own_other = other_core([cotangent])
    x_yz, far_yz, held, w_c, c_own_other, cot, c_x, w_parts = sync(
        x_yz, far_yz, held, w_c, c_own_other, cotangent, c_x, w_parts
    )
    c_y, c_z = swap(cot, Y), swap(cot, Z)
    w_x = [swap(w_parts[0], X)]
    mid = rows // 2
    c_xy, c_xz = [swap(c_x[:mid], Y)], [swap(c_x[:mid], Z)]
    held = some_project([((0, 1, 1), x_yz)] + [((k, 1, 1), far_yz[n]) for n, k in enumerate(range(1, far))], held)
    normed, q, k, v, unit, scale = held
    attended_low, attended, q2 = attend(heads, q, k, v)
    c_y, c_z, attended_low, c_x, c_xy, c_xz, w_x = sync(c_y, c_z, attended_low, c_x, c_xy, c_xz, w_x)
    heads_out = lax.all_to_all(attended_low, seq, split_axis=0, concat_axis=1, tiled=True)
    c_xyz = [swap(c_xy[0], Z)]
    c_xy.append(swap(c_y[mid:], X))
    c_xz.append(swap(c_z[mid:], X))
    c_yz = swap(c_z, Y)
    c_one = [c_x, c_y, c_z]
    c_one_other = other_core(c_one)
    heads_out, c_xz, c_xy, c_yz, c_xyz, c_one_other = sync(heads_out, c_xz, c_xy, c_yz, c_xyz, c_one_other)

    inputs = tokens.astype(F32)
    square_one = jnp.mean(inputs * inputs, axis=1, keepdims=True)
    scale_one = lax.rsqrt(square_one + EPSILON)
    residual = inputs + dot(heads_out, out_full)
    square_two = jnp.mean(residual * residual, axis=1, keepdims=True)
    scale_two = lax.rsqrt(square_two + EPSILON)
    inner = (residual * scale_two * ffn_gain).astype(BF16)
    c_xyz.append(swap(c_yz[mid:], X))
    c_two_other = [swap(c, C) for c in c_xz + c_xy]
    inner, c_xyz, c_two_other, c_yz = sync(inner, c_xyz, c_two_other, c_yz)

    units = gate_weight.shape[1]
    part = units // s_count
    mine = far * part
    own_block = zb * 2 + si
    if part % LANES == 0:
        weights = (gate_weight, up_weight, down_weight)
        unit_index = (jnp.arange(far, dtype=jnp.int32) * 4 + own_block).astype(jnp.int32)
        width_of_part = part
    else:
        pick = lambda w: lax.dynamic_index_in_dim(
            w.reshape(width, far, 4, part), own_block, 2, keepdims=False
        ).reshape(width, mine)
        weights = (
            pick(gate_weight),
            pick(up_weight),
            lax.dynamic_index_in_dim(
                down_weight.reshape(far, 4, part, width), own_block, 1, keepdims=False
            ).reshape(mine, width),
        )
        unit_index = jnp.zeros((1,), jnp.int32)
        width_of_part = mine
    run = lambda x_stage, c_stage: feed(x_stage, c_stage, unit_index, weights, width_of_part)
    x, y, z = swap(inner, X), swap(inner, Y), swap(inner, Z)
    c_two_other.append(swap(c_yz, C))
    x_stages = [([[inner]], [other_core([inner])])]
    c_stages = [([[cot]], [c_own_other])]
    fed = [run(x_stages[0], c_stages[0])]
    x, y, z, fed, inner, c_xyz, c_two_other = sync(x, y, z, fed, inner, c_xyz, c_two_other)
    c_two = [c_xz, c_xy, [c_yz], c_xyz]
    xy, xz, yz = swap(x, Y), swap(z, X), swap(y, Z)
    xyz = swap_cube(inner, (X, Z, Y))
    x_stages.append(([[x], [y], [z]], [other_core([x, y, z])]))
    c_stages.append(([[c] for c in c_one], [c_one_other]))
    c_two_other += [swap(c, C) for c in c_xyz]
    fed.append(run(x_stages[1], c_stages[1]))
    xy, xz, yz, xyz, fed, x_stages, w_parts, c_two, c_two_other = sync(
        xy, xz, yz, xyz, fed, x_stages, w_parts, c_two, c_two_other
    )
    x_stages.append(([[xz], [xy], [yz], [xyz]], [other_core([xz, xy, yz, xyz])]))
    c_stages.append((c_two, c_two_other))
    d_home = send_home(0, fed[0][0], swap(fed[0][1], C)) + send_home(1, fed[1][0], swap(fed[1][1], C))
    w_x.append(swap(w_parts[1], X))
    fed.append(run(x_stages[2], c_stages[2]))
    d_home, fed, x_stages, w_x = sync(d_home, fed, x_stages, w_x)
    far_xz, far_xy, far_yz, far_xyz = add_low(fed[2][0], swap(fed[2][1], C))
    hops = [swap(far_xyz, Y), swap(far_xy, X), swap(far_yz, Z)]
    down_part = down_grad([f[4] for f in fed], c_stages)
    far_xz, hops, d_home, down_part, fed = sync(far_xz, hops, d_home, down_part, fed)
    d_home += [swap_cube(add_low(far_xz, hops[0]), (X, Z)), swap(add_low(hops[1], hops[2]), Y)]
    m_other = [swap(f[3], C) for f in fed[:2]]
    gu_part = gate_grad(x_stages, [f[5] for f in fed])
    d_home, down_part, gu_part, fed, m_other, heads_out = sync(
        d_home, down_part, gu_part, fed, m_other, heads_out
    )
    gu_far = lax.psum_scatter(gu_part, "za", scatter_dimension=0, tiled=True)
    down_far = lax.psum_scatter(down_part, "za", scatter_dimension=0, tiled=True)
    quarter = width // far // 4

    def to_owners(values):
        spread = []
        for offset, axes in enumerate(((), (Y,), (Z,), (Z, Y))):
            block = lax.dynamic_slice_in_dim(values, (own_block ^ offset) * quarter, quarter, 0)
            spread.append(swap_cube(block, axes) if axes else block)
        return spread

    m_other.append(swap(fed[2][3], C))
    own_rows = out_weight.shape[0]
    left = []
    for offset in range(f_count):
        block = lax.dynamic_slice_in_dim(heads_out, (f_index ^ offset) * own_rows, own_rows, 1)
        left.append(swap(block, fsdp, offset) if offset else block)
    d_inner = sum(a.astype(F32) for a in d_home)
    ffn_part = jnp.sum(d_inner * residual * scale_two, axis=0)
    weighted = d_inner * ffn_gain
    d_residual = cotangent.astype(F32) + scale_two * (
        weighted - residual * scale_two * scale_two * jnp.mean(weighted * residual, axis=1, keepdims=True)
    )
    d_branch = d_residual.astype(BF16)
    d_heads = dot(d_branch, out_full, NT).astype(BF16)
    d_heads, d_branch, m_other, fed, left = sync(d_heads, d_branch, m_other, fed, left)
    d_attended = lax.all_to_all(d_heads, seq, split_axis=1, concat_axis=0, tiled=True)
    over = swap(d_branch, X)
    right = [d_branch, swap(d_branch, C), over, swap(over, C)]
    m = [add_low(f[2], other) for f, other in zip(fed[:2], m_other)]
    m.append([add_low(fed[2][2][n], m_other[2][n]) for n in range(4)])
    m_far = swap(m[2][3], Y)
    d_attended, right, m, m_far, w_parts, w_x = sync(d_attended, right, m, m_far, w_parts, w_x)
    w_x.append(swap(w_parts[2], X))
    w_xc = [swap(jnp.concatenate(w_x[:2], axis=0), C)]
    out_part = dot(jnp.concatenate(left, axis=0), jnp.concatenate(right, axis=0), TN).astype(BF16)
    out_part = out_part.reshape(far, 2, 2, -1, width)
    pick = lambda values, index, axis: lax.dynamic_index_in_dim(values, index, axis, keepdims=False)
    out_y = swap(pick(out_part, 1 - si, 2), Y)
    d_qkv, gain_parts = attend_back(
        heads, q2, k, v, sync(d_attended, out_part)[0], attended, unit, scale, head_gain, cos2, sin2
    )
    d_qkv, gain_parts, m, m_far, w_x, w_xc, out_part, out_y = sync(
        d_qkv, gain_parts, m, m_far, w_x, w_xc, out_part, out_y
    )
    d_tok = lax.all_to_all(d_qkv, seq, split_axis=0, concat_axis=1, tiled=True)
    proj_part = dot(normed, d_qkv, TN).astype(BF16).reshape(2, 2, width // 4, padded)
    fi, fo = lax.axis_index(C), lax.axis_index(X)
    proj_core = add_low(pick(proj_part, fi, 1), swap(pick(proj_part, 1 - fi, 1), C))
    proj_x = swap(take(proj_core, 1 - fo), X)
    w_xc.append(swap(w_x[2], C))
    m_x, m_yz = swap(m[2][1], X), swap(m[2][2], Y)
    out_part = add_low(pick(out_part, si, 2), out_y)
    m_xz = add_low(m[2][0], m_far)
    d_tok, proj_core, proj_x, w_xc, out_part, m, m_x, m_yz, m_xz, gain_parts, gu_far = sync(
        d_tok, proj_core, proj_x, w_xc, out_part, m, m_x, m_yz, m_xz, gain_parts, gu_far
    )
    m_z = [swap(m_xz, X), m_yz]
    spread = to_owners(gu_far)
    blocks = [w_rows, w_c, jnp.concatenate(w_x, axis=0), jnp.concatenate(w_xc, axis=0)]
    by_offset = jnp.stack([dot(d_tok, w, NT) for w in blocks])
    d_normed = jnp.concatenate([take(by_offset, f_index ^ n) for n in range(f_count)], axis=1)
    weighted = d_normed * attn_gain
    input_grad = (
        d_residual
        + scale_one
        * (weighted - inputs * scale_one * scale_one * jnp.mean(weighted * inputs, axis=1, keepdims=True))
    ).astype(BF16)
    proj_rows = add_low(take(proj_core, fo), proj_x)
    m_one = [m[1][0], add_low(m[1][1], m_x)]
    m_z, spread, input_grad, proj_rows, m, m_one, out_part, gain_parts = sync(
        m_z, spread, input_grad, proj_rows, m, m_one, out_part, gain_parts
    )
    proj = lax.all_to_all(proj_rows, seq, split_axis=0, concat_axis=1, tiled=True)
    m_last = [swap(m_one[0], X), swap(m_one[1], Y)]
    m_one.append((m[1][2].astype(F32) + m_z[0].astype(F32) + m_z[1].astype(F32)).astype(BF16))
    out_z = swap(pick(out_part, 1 - zb, 1), Z)
    gain_row = gain_parts[0]
    pack = jnp.concatenate(
        [
            ffn_part,
            gain_row[:q_cols].reshape(heads, HEAD_SIZE).sum(axis=0),
            gain_row[q_cols:q_cols + HEAD_SIZE],
        ]
    ).reshape(-1, LANES)
    for axis in ("fi", "fo", "si", "zb", "za"):
        offset = 1
        while offset < lax.axis_size(axis):
            pack = pack + swap(pack, axis, offset)
            offset *= 2
    pack = pack.reshape(-1)
    gate_mine, up_mine = place(spread, own_block, part)
    proj, gate_mine, up_mine, m, m_one, m_last, out_part, out_z, down_far, pack = sync(
        proj, gate_mine, up_mine, m, m_one, m_last, out_part, out_z, down_far, pack
    )
    out_part = add_low(pick(out_part, zb, 1), out_z)
    out_got = send_far(out_part, za)
    m_last.append(swap(m_one[2], Z))
    down_mine = down_far.astype(F32)
    mlp_out = m[0][0].astype(F32) + sum(a.astype(F32) for a in m_last)
    block_output = (residual + mlp_out).astype(BF16)
    out_mine = add_far(out_part, out_got, za)
    proj = proj.astype(F32)
    count = proj.shape[0]
    by_device = proj.reshape(count, s_count, padded)

    def fold(values):
        return values.reshape(count, KEY_VALUE_HEADS, copies, HEAD_SIZE).sum(axis=2).reshape(count, -1)

    query_mine = by_device[:, :, :q_cols].reshape(count, QUERY_HEADS * HEAD_SIZE)
    key_mine = fold(by_device[:, :, q_cols:q_cols + HEAD_SIZE])
    value_mine = fold(by_device[:, :, q_cols + HEAD_SIZE:cols])

    my_w = lax.dynamic_slice_in_dim(w_rows, s_index * count, count, 0).astype(F32)
    my_gain = lax.dynamic_slice_in_dim(attn_gain, (f_index * s_count + s_index) * count, count, 0)
    attn_gain_mine = jnp.sum(my_w * proj, axis=1) / my_gain
    ffn_gain_mine = lax.dynamic_slice_in_dim(pack, (f_index * s_count + s_index) * count, count, 0)
    attn_rms = jnp.sqrt(square_one + EPSILON)[:, 0]
    mlp_rms = jnp.sqrt(square_two + EPSILON)[:, 0]
    return (
        block_output, input_grad, residual, attn_rms, mlp_rms, attn_gain_mine,
        query_mine, key_mine, value_mine, pack[width:width + HEAD_SIZE], pack[width + HEAD_SIZE:],
        out_mine, ffn_gain_mine, gate_mine, up_mine, down_mine,
    )


def solution(mesh):
    f_count, s_count = mesh.shape["fsdp"], mesh.shape["seq"]
    fine = Mesh(
        mesh.devices.reshape(f_count // 2, 2, s_count // 4, 2, 2), ("fo", "fi", "za", "zb", "si")
    )
    f, s = ("fo", "fi"), ("za", "zb", "si")
    every = P(f + s, None)
    vector = P(f + s)
    placed = (
        every, P(f, None), every, P(), P(f, None), P(f, None), P(f, None), P(), P(),
        P(f, None), P(), P(None, f), P(None, f), P(f, None),
    )
    return jax.shard_map(
        per_device,
        mesh=fine,
        in_specs=placed,
        out_specs=(
            every, every, every, vector, vector, vector, every, every, every, P(), P(),
            every, vector, P(s, f), P(s, f), every,
        ),
        check_vma=False,
    )
```

```python
import functools

import jax
import jax.numpy as jnp
from jax import lax
from jax.experimental import pallas as pl
from jax.experimental.pallas import tpu as pltpu
from jax.sharding import Mesh, PartitionSpec as P

HEAD_SIZE = 64
QUERY_HEADS = 32
KEY_VALUE_HEADS = 8
EPSILON = 1e-05
ROPE_BASE = 1000000.0
BIG = 30000.0
LANES = 128
BLOCK = 256
UNROLLED = 2048
VMEM = 60 * 1024 * 1024
COST = pl.CostEstimate(flops=1000, bytes_accessed=1000, transcendentals=0)

F32 = jnp.float32
BF16 = jnp.bfloat16
NT = (((1,), (1,)), ((), ()))
TN = (((0,), (0,)), ((), ()))


def dot(left, right, dims=(((1,), (0,)), ((), ()))):
    return lax.dot_general(left, right, dims, preferred_element_type=F32)


def split_low(values):
    high = values.astype(BF16)
    return high, (values - high.astype(F32)).astype(BF16)


def head_means(values, ones):
    high, low = split_low(values)
    return (dot(high, ones) + dot(low, ones)) * (1.0 / HEAD_SIZE)


def head_ones():
    row = lax.broadcasted_iota(jnp.int32, (LANES, LANES), 0) // HEAD_SIZE
    col = lax.broadcasted_iota(jnp.int32, (LANES, LANES), 1) // HEAD_SIZE
    return jnp.where(row == col, 1.0, 0.0).astype(BF16)


def swap_halves(values):
    lane = lax.broadcasted_iota(jnp.int32, values.shape, 1) % HEAD_SIZE
    half = HEAD_SIZE // 2
    return jnp.where(
        lane < half, pltpu.roll(values, LANES - half, 1), pltpu.roll(values, half, 1)
    )


def project_kernel(heads, count, fresh, index_ref, bounds_ref, *refs):
    x_refs = refs[:count]
    gain_ref, w_ref, head_gain_ref, cos_ref, sin_ref = refs[count:count + 5]
    refs = refs[count + 5 + (0 if fresh else 6):]
    normed_ref, q_ref, k_ref, v_ref, unit_ref, scale_ref, x_scr = refs
    i = pl.program_id(0)
    rows = x_scr.shape[0]
    for r in range(count):
        @pl.when(i == r)
        def _(r=r):
            x_scr[...] = x_refs[r][...]

    x = x_scr[...].astype(F32)
    scale = lax.rsqrt(jnp.mean(x * x, axis=1, keepdims=True) + EPSILON)
    normed = (x * scale * gain_ref[...]).astype(BF16)
    normed_ref[...] = normed
    pre = dot(normed, w_ref[...])
    cosine, sine = cos_ref[...], sin_ref[...]
    shape = (rows, LANES)
    token = index_ref[i] * rows + lax.broadcasted_iota(jnp.int32, shape, 0)
    doc = (token >= bounds_ref[0]).astype(jnp.int32) + (token >= bounds_ref[1]).astype(jnp.int32)
    lane = lax.broadcasted_iota(jnp.int32, shape, 1)
    mark = lane - HEAD_SIZE
    query_marks = jnp.where(mark == doc, 1.0, 0.0)
    key_marks = jnp.where(mark < 3, jnp.where(mark == doc, 0.0, -BIG), jnp.where(mark < 5, 1.0, 0.0))
    value_marks = jnp.where(mark < 2, 1.0, 0.0)
    ones = head_ones()

    def place(values, segment, marks):
        group = values if segment % 2 == 0 else pltpu.roll(values, HEAD_SIZE, 1)
        return jnp.where(lane < HEAD_SIZE, group, marks).astype(BF16)

    for g in range(pre.shape[1] // LANES):
        cols = slice(g * LANES, (g + 1) * LANES)
        u = pre[:, cols]
        r = lax.rsqrt(head_means(u * u, ones) + EPSILON)
        unit = u * r
        unit_ref[:, cols] = unit
        scale_ref[:, cols] = r
        gained = unit * head_gain_ref[0:1, cols]
        rot = (gained * cosine + swap_halves(gained) * sine).astype(BF16).astype(F32)
        for segment in (2 * g, 2 * g + 1):
            if segment < heads:
                q_ref[segment] = place(rot * 0.125, segment, query_marks)
            elif segment == heads:
                k_ref[...] = place(rot, segment, key_marks)
            elif segment == heads + 1:
                v_ref[...] = place(u, segment, value_marks)


def project(heads, blocks, index, bounds, gain, w, head_gain, cosine, sine, length, held=None):
    rows, width = blocks[0].shape
    count = len(blocks)
    cols = w.shape[1]
    row = lambda c: pl.BlockSpec((rows, c), lambda i, n, b: (n[i], 0))
    whole = lambda a: pl.BlockSpec(a.shape, lambda i, n, b: (0, 0))
    fresh = held is None
    held = () if fresh else held
    outs = [
        jax.ShapeDtypeStruct((length, width), BF16),
        jax.ShapeDtypeStruct((heads, length, LANES), BF16),
        jax.ShapeDtypeStruct((length, LANES), BF16),
        jax.ShapeDtypeStruct((length, LANES), BF16),
        jax.ShapeDtypeStruct((length, cols), F32),
        jax.ShapeDtypeStruct((length, cols), F32),
    ]
    tokens = rows * count
    return pl.pallas_call(
        functools.partial(project_kernel, heads, count, fresh),
        grid_spec=pltpu.PrefetchScalarGridSpec(
            num_scalar_prefetch=2,
            grid=(count,),
            in_specs=[whole(b) for b in blocks]
            + [whole(gain), whole(w), whole(head_gain), row(LANES), row(LANES)]
            + [pl.BlockSpec(memory_space=pl.ANY)] * len(held),
            out_specs=[
                row(width),
                pl.BlockSpec((heads, rows, LANES), lambda i, n, b: (0, n[i], 0)),
                row(LANES),
                row(LANES),
                row(cols),
                row(cols),
            ],
            scratch_shapes=[pltpu.VMEM((rows, width), BF16)],
        ),
        out_shape=outs,
        input_output_aliases={2 + count + 5 + n: n for n in range(len(held))},
        compiler_params=pltpu.CompilerParams(vmem_limit_bytes=VMEM),
        cost_estimate=COST,
        name="project",
    )(index, bounds, *blocks, gain, w, head_gain, cosine, sine, *held)


def attend_kernel(heads, q_ref, k_ref, v_ref, low_ref, out_ref, q2_ref):
    i = pl.program_id(0)
    rows = BLOCK
    q = q_ref[...].reshape(heads * rows, LANES)

    def step(j, total):
        start = pl.multiple_of(j * rows, rows)
        p = jnp.exp(dot(q, k_ref[pl.ds(start, rows), :], NT)).astype(BF16)
        return total + dot(p, v_ref[pl.ds(start, rows), :])

    total = lax.fori_loop(0, i, step, jnp.zeros((heads * rows, LANES), F32))
    start = pl.multiple_of(i * rows, rows)
    s = dot(q, k_ref[pl.ds(start, rows), :], NT)
    t_local = lax.broadcasted_iota(jnp.int32, s.shape, 0) % rows
    u_local = lax.broadcasted_iota(jnp.int32, s.shape, 1)
    p = jnp.where(u_local <= t_local, jnp.exp(s), 0.0).astype(BF16)
    total = total + dot(p, v_ref[pl.ds(start, rows), :])
    weight = total[:, HEAD_SIZE:HEAD_SIZE + 1]
    out = total[:, :HEAD_SIZE] / weight
    for h in range(heads):
        part = out[h * rows:(h + 1) * rows, :]
        out_ref[:, h * HEAD_SIZE:(h + 1) * HEAD_SIZE] = part
        low_ref[:, h * HEAD_SIZE:(h + 1) * HEAD_SIZE] = part.astype(BF16)
    high, low = split_low(-jnp.log(weight))
    lane = lax.broadcasted_iota(jnp.int32, q.shape, 1)
    q2 = jnp.where(lane == HEAD_SIZE + 3, high, jnp.where(lane == HEAD_SIZE + 4, low, q))
    q2_ref[...] = q2.reshape(heads, rows, LANES)


def attend_unrolled_kernel(heads, rows, q_ref, k_ref, v_ref, low_ref, out_ref, q2_ref):
    stretch = q_ref.shape[1]

    def block(first, at):
        q = q_ref[:, at:at + rows, :].reshape(heads * rows, LANES)
        s = dot(q, k_ref[first:first + rows, :], NT)
        t_local = lax.broadcasted_iota(jnp.int32, s.shape, 0) % rows
        u_local = lax.broadcasted_iota(jnp.int32, s.shape, 1)
        p = jnp.where(u_local <= t_local, jnp.exp(s), 0.0).astype(BF16)
        total = dot(p, v_ref[first:first + rows, :])
        if first:
            p = jnp.exp(dot(q, k_ref[:first, :], NT)).astype(BF16)
            total = total + dot(p, v_ref[:first, :])
        weight = total[:, HEAD_SIZE:HEAD_SIZE + 1]
        out = total[:, :HEAD_SIZE] / weight
        for h in range(heads):
            part = out[h * rows:(h + 1) * rows, :]
            out_ref[at:at + rows, h * HEAD_SIZE:(h + 1) * HEAD_SIZE] = part
            low_ref[at:at + rows, h * HEAD_SIZE:(h + 1) * HEAD_SIZE] = part.astype(BF16)
        high, low = split_low(-jnp.log(weight))
        lane = lax.broadcasted_iota(jnp.int32, q.shape, 1)
        q2 = jnp.where(lane == HEAD_SIZE + 3, high, jnp.where(lane == HEAD_SIZE + 4, low, q))
        q2_ref[:, at:at + rows, :] = q2.reshape(heads, rows, LANES)

    for step in range(k_ref.shape[0] // stretch):
        @pl.when(pl.program_id(0) == step)
        def _(step=step):
            for at in range(0, stretch, rows):
                block(step * stretch + at, at)


def attend(heads, q, k, v):
    tokens = k.shape[0]
    if tokens <= UNROLLED and tokens % (2 * BLOCK) == 0:
        kernel, rows = functools.partial(attend_unrolled_kernel, heads, BLOCK // 2), 2 * BLOCK
    else:
        kernel, rows = functools.partial(attend_kernel, heads), BLOCK
    return pl.pallas_call(
        kernel,
        grid=(tokens // rows,),
        in_specs=[
            pl.BlockSpec((heads, rows, LANES), lambda i: (0, i, 0)),
            pl.BlockSpec((tokens, LANES), lambda i: (0, 0)),
            pl.BlockSpec((tokens, LANES), lambda i: (0, 0)),
        ],
        out_specs=[
            pl.BlockSpec((rows, heads * HEAD_SIZE), lambda i: (i, 0)),
            pl.BlockSpec((rows, heads * HEAD_SIZE), lambda i: (i, 0)),
            pl.BlockSpec((heads, rows, LANES), lambda i: (0, i, 0)),
        ],
        out_shape=[
            jax.ShapeDtypeStruct((tokens, heads * HEAD_SIZE), BF16),
            jax.ShapeDtypeStruct((tokens, heads * HEAD_SIZE), F32),
            jax.ShapeDtypeStruct((heads, tokens, LANES), BF16),
        ],
        compiler_params=pltpu.CompilerParams(vmem_limit_bytes=VMEM),
        cost_estimate=COST,
        name="attend",
    )(q, k, v)


def attend_back_kernel(heads, q_ref, k_ref, v_ref, grad_ref, out_ref, unit_hbm, scale_hbm, head_gain_ref,
                       cos_hbm, sin_hbm, dqkv_ref, gains_ref, g_scr, dq_scr, dk_scr, dv_scr,
                       unit_ref, scale_ref, cos_ref, sin_ref, sems):
    rows = BLOCK
    tokens = k_ref.shape[0]
    blocks = tokens // rows
    wide = heads * rows
    late = [
        pltpu.make_async_copy(source, target, sems.at[n])
        for n, (source, target) in enumerate(
            ((unit_hbm, unit_ref), (scale_hbm, scale_ref), (cos_hbm, cos_ref), (sin_hbm, sin_ref))
        )
    ]
    for copy in late:
        copy.start()

    def prepare(i, carry):
        at = pl.ds(pl.multiple_of(i * rows, rows), rows)
        lane = lax.broadcasted_iota(jnp.int32, (rows, HEAD_SIZE), 1)
        for h in range(heads):
            cols = slice(h * HEAD_SIZE, (h + 1) * HEAD_SIZE)
            grad = grad_ref[at, cols]
            delta = jnp.sum(grad.astype(F32) * out_ref[at, cols], axis=1, keepdims=True)
            high, low = split_low(-delta)
            g_scr[h, at, :HEAD_SIZE] = grad
            g_scr[h, at, HEAD_SIZE:] = jnp.where(lane == 0, high, jnp.where(lane == 1, low, jnp.zeros_like(low)))
        dq_scr[:, at, :] = jnp.zeros((heads, rows, LANES), F32)
        return carry

    lax.fori_loop(0, blocks, prepare, 0)

    def pair(j, i, diagonal):
        at = pl.ds(i * rows, rows)
        k = k_ref[pl.ds(j * rows, rows), :]
        q = q_ref[:, at, :].reshape(wide, LANES)
        g = g_scr[:, at, :].reshape(wide, LANES)
        p = jnp.exp(dot(k, q, NT))
        if diagonal:
            u_local = lax.broadcasted_iota(jnp.int32, p.shape, 0)
            t_local = lax.broadcasted_iota(jnp.int32, p.shape, 1) % rows
            p = jnp.where(u_local <= t_local, p, 0.0)
        dv = dot(p.astype(BF16), g)
        ds = (p * dot(v_ref[pl.ds(j * rows, rows), :], g, NT)).astype(BF16)
        dk = dot(ds, q)
        dq_scr[:, at, :] += dot(ds, k, TN).reshape(heads, rows, LANES)
        return dk, dv

    def key_step(j, carry):
        def query_step(i, state):
            dk, dv = pair(j, i, False)
            return state[0] + dk, state[1] + dv

        state = pair(j, j, True)
        if tokens <= UNROLLED:
            for i in range(j + 1, blocks):
                state = query_step(i, state)
        else:
            state = lax.fori_loop(j + 1, blocks, query_step, state)
        dk_scr[pl.ds(j * rows, rows), :] = state[0]
        dv_scr[pl.ds(j * rows, rows), :] = state[1]
        return carry

    if tokens <= UNROLLED:
        for j in range(blocks):
            key_step(j, 0)
    else:
        lax.fori_loop(0, blocks, key_step, 0)
    for copy in late:
        copy.wait()
    groups = unit_ref.shape[1] // LANES
    ones = head_ones()

    def finish(i, carry):
        at = pl.ds(pl.multiple_of(i * rows, rows), rows)
        cosine, sine = cos_ref[at, :], sin_ref[at, :]
        lane = lax.broadcasted_iota(jnp.int32, (rows, LANES), 1)

        def segment_of(s):
            if s < heads:
                return dq_scr[s, at, :] * 0.125
            return (dk_scr if s == heads else dv_scr)[at, :]

        sums = list(carry)
        for g in range(groups):
            cols = slice(g * LANES, (g + 1) * LANES)
            first = segment_of(2 * g)
            last = segment_of(2 * g + 1) if 2 * g + 1 < heads + 2 else first
            d = jnp.where(lane < HEAD_SIZE, first, pltpu.roll(last, HEAD_SIZE, 1))
            e = d * cosine - swap_halves(d) * sine
            unit = unit_ref[at, cols]
            sums[g] = sums[g] + jnp.sum(e * unit, axis=0, keepdims=True)
            w = e * head_gain_ref[0:1, cols]
            normal = scale_ref[at, cols] * (w - unit * head_means(w * unit, ones))
            is_value = lane + g * LANES >= (heads + 1) * HEAD_SIZE
            dqkv_ref[at, cols] = jnp.where(is_value, d, normal).astype(BF16)
        return tuple(sums)

    zero = jnp.zeros((1, LANES), F32)
    sums = lax.fori_loop(0, blocks, finish, (zero,) * groups)
    gains_ref[...] = jnp.zeros(gains_ref.shape, F32)
    for g in range(groups):
        gains_ref[0:1, g * LANES:(g + 1) * LANES] = sums[g]


def attend_back(heads, q, k, v, grad, out, unit, scale, head_gain, cosine, sine):
    tokens = k.shape[0]
    cols = unit.shape[1]
    vmem, late = pl.BlockSpec(memory_space=pltpu.VMEM), pl.BlockSpec(memory_space=pl.ANY)
    return pl.pallas_call(
        functools.partial(attend_back_kernel, heads),
        in_specs=[vmem] * 5 + [late] * 2 + [vmem] + [late] * 2,
        out_specs=[vmem] * 2,
        out_shape=[
            jax.ShapeDtypeStruct((tokens, cols), BF16),
            jax.ShapeDtypeStruct((8, cols), F32),
        ],
        scratch_shapes=[
            pltpu.VMEM((heads, tokens, LANES), BF16),
            pltpu.VMEM((heads, tokens, LANES), F32),
            pltpu.VMEM((tokens, LANES), F32),
            pltpu.VMEM((tokens, LANES), F32),
            pltpu.VMEM((tokens, cols), F32),
            pltpu.VMEM((tokens, cols), F32),
            pltpu.VMEM((tokens, LANES), F32),
            pltpu.VMEM((tokens, LANES), F32),
            pltpu.SemaphoreType.DMA((4,)),
        ],
        compiler_params=pltpu.CompilerParams(vmem_limit_bytes=VMEM),
        cost_estimate=COST,
        name="attend_back",
    )(q, k, v, grad, out, unit, scale, head_gain, cosine, sine)


def cut(arrays, sizes, half):
    tiles = [[] for _ in range(sum(sizes) // half)]
    row = 0
    for array, size in zip(arrays, sizes):
        start = 0
        while start < size:
            count = min(size - start, half - row % half)
            tiles[row // half].append((array, start, count))
            start += count
            row += count
    return tiles


def feed_kernel(layouts, weight_count, index_ref, *refs):
    tiles = len(layouts[0][0])
    half = refs[-6].shape[1] // 2
    sides = []
    for pieces, layout in layouts:
        own = []
        for count in pieces:
            own.append(refs[:count])
            refs = refs[count:]
        sides.append((own, cut(refs[:len(layout)], layout, half)))
        refs = refs[len(layout):]
    gate_ref, up_ref, down_ref = refs[:3]
    da_ref, db_ref, ma_ref, mb_ref, hidden_ref, dgu_ref, x_scr, c_scr, gu_scr, down_scr, sem, w_sem = refs[3:]
    i = pl.program_id(0)
    half = x_scr.shape[1] // 2

    def copies(t):
        slot = t % 2
        found = []
        for (own, others), scratch, which in ((sides[0], x_scr, 0), (sides[1], c_scr, 1)):
            size = half // len(own[t])
            for n, piece in enumerate(own[t]):
                found.append(
                    pltpu.make_async_copy(piece, scratch.at[slot, pl.ds(n * size, size)], sem.at[slot, which, n])
                )
            row = half
            for n, (other, start, size) in enumerate(others[t]):
                found.append(
                    pltpu.make_async_copy(
                        other.at[pl.ds(start, size)],
                        scratch.at[slot, pl.ds(row, size)],
                        sem.at[slot, which, n + 2],
                    )
                )
                row += size
        return found

    mine = hidden_ref.shape[1]
    part = mine // weight_count

    def weight_copies(n):
        at = pl.ds(pl.multiple_of(index_ref[n] * part, part), part)
        return [
            pltpu.make_async_copy(gate_ref.at[:, at], gu_scr.at[:, pl.ds(n * part, part)], w_sem.at[n, 0]),
            pltpu.make_async_copy(up_ref.at[:, at], gu_scr.at[:, pl.ds(mine + n * part, part)], w_sem.at[n, 1]),
            pltpu.make_async_copy(down_ref.at[at], down_scr.at[pl.ds(n * part, part)], w_sem.at[n, 2]),
        ]

    for t in range(tiles):
        @pl.when(i == t)
        def _(t=t):
            if t == 0:
                needed = copies(0) + [copy for n in range(weight_count) for copy in weight_copies(n)]
                for copy in needed:
                    copy.start()
            else:
                needed = copies(t)
            if t + 1 < tiles:
                for copy in copies(t + 1):
                    copy.start()
            for copy in needed:
                copy.wait()

    slot = lax.rem(i, 2)
    both = dot(x_scr[slot], gu_scr[...])
    gate, up = both[:, :mine], both[:, mine:]
    d_hidden = dot(c_scr[slot], down_scr[...], NT)
    sigma = 1.0 / (1.0 + jnp.exp(-gate))
    active = gate * sigma
    hidden = (active * up).astype(BF16)
    hidden_ref[...] = hidden
    dgu_ref[:, :mine] = (d_hidden * up * (sigma * (1.0 + gate * (1.0 - sigma)))).astype(BF16)
    dgu_ref[:, mine:] = (d_hidden * active).astype(BF16)
    d_inner = dot(dgu_ref[...], gu_scr[...], NT)
    mlp = dot(hidden, down_scr[...])
    da_ref[0] = d_inner[:half].astype(BF16)
    db_ref[0] = d_inner[half:].astype(BF16)
    ma_ref[0] = mlp[:half].astype(BF16)
    mb_ref[0] = mlp[half:].astype(BF16)


def feed(x_stage, c_stage, index, weights, part):
    (x_own, x_others), (c_own, c_others) = x_stage, c_stage
    tiles = len(x_own)
    half = x_own[0][0].shape[0] * len(x_own[0])
    layouts = tuple(
        (tuple(len(t) for t in own), tuple(o.shape[0] for o in others))
        for own, others in ((x_own, x_others), (c_own, c_others))
    )
    arrays = [a for own, others in ((x_own, x_others), (c_own, c_others)) for a in sum(own, []) + list(others)]
    rows = 2 * half
    gate, up, down = weights
    width = gate.shape[0]
    blocks = index.shape[0]
    mine = blocks * part
    halves = pl.BlockSpec((1, half, width), lambda i, n: (i, 0, 0))
    return pl.pallas_call(
        functools.partial(feed_kernel, layouts, blocks),
        grid_spec=pltpu.PrefetchScalarGridSpec(
            num_scalar_prefetch=1,
            grid=(tiles,),
            in_specs=[pl.BlockSpec(memory_space=pl.ANY)] * (len(arrays) + 3),
            out_specs=[halves] * 4
            + [
                pl.BlockSpec((rows, mine), lambda i, n: (i, 0)),
                pl.BlockSpec((rows, 2 * mine), lambda i, n: (i, 0)),
            ],
            scratch_shapes=[
                pltpu.VMEM((2, rows, width), BF16),
                pltpu.VMEM((2, rows, width), BF16),
                pltpu.VMEM((width, 2 * mine), BF16),
                pltpu.VMEM((mine, width), BF16),
                pltpu.SemaphoreType.DMA((2, 2, 4)),
                pltpu.SemaphoreType.DMA((blocks, 3)),
            ],
        ),
        out_shape=[jax.ShapeDtypeStruct((tiles, half, width), BF16)] * 4
        + [
            jax.ShapeDtypeStruct((tiles * rows, mine), BF16),
            jax.ShapeDtypeStruct((tiles * rows, 2 * mine), BF16),
        ],
        compiler_params=pltpu.CompilerParams(vmem_limit_bytes=VMEM),
        cost_estimate=COST,
        name="feed",
    )(index, *arrays, gate, up, down)


def stage_arrays(stages):
    arrays, layout = [], []
    for own, others in stages:
        half = own[0][0].shape[0] * len(own[0])
        arrays += sum(own, []) + list(others)
        layout.append((half, tuple(len(t) for t in own), tuple(o.shape[0] for o in others)))
    return arrays, tuple(layout)


def stack_rows(refs, layout, scratch):
    at = row = 0
    for half, tiles, others in layout:
        first = at + sum(tiles)
        for pieces, across in zip(tiles, cut(refs[first:first + len(others)], others, half)):
            size = half // pieces
            for n in range(pieces):
                scratch[row:row + size, :] = refs[at + n][...]
                row += size
            at += pieces
            for other, start, size in across:
                scratch[row:row + size, :] = other[start:start + size, :]
                row += size
        at += len(others)


def gate_grad_kernel(array_count, layout, *refs):
    arrays, refs = refs[:array_count], refs[array_count:]
    rights, (out_ref, scratch) = refs[:len(layout)], refs[len(layout):]
    stack_rows(arrays, layout, scratch)
    row = 0
    total = None
    for right in rights:
        size = right.shape[0]
        term = dot(scratch[row:row + size, :], right[...], TN)
        total = term if total is None else total + term
        row += size
    out_ref[...] = total.astype(BF16)


def gate_grad(stages, rights):
    arrays, layout = stage_arrays(stages)
    width = arrays[0].shape[1]
    units = rights[0].shape[1]
    rows = sum(r.shape[0] for r in rights)
    step = min(256, width)
    return pl.pallas_call(
        functools.partial(gate_grad_kernel, len(arrays), layout),
        grid=(width // step,),
        in_specs=[pl.BlockSpec((p.shape[0], step), lambda i: (0, i)) for p in arrays]
        + [pl.BlockSpec(r.shape, lambda i: (0, 0)) for r in rights],
        out_specs=pl.BlockSpec((step, units), lambda i: (i, 0)),
        out_shape=jax.ShapeDtypeStruct((width, units), BF16),
        scratch_shapes=[pltpu.VMEM((rows, step), BF16)],
        compiler_params=pltpu.CompilerParams(vmem_limit_bytes=VMEM),
        cost_estimate=COST,
        name="gate_grad",
    )(*arrays, *rights)


def down_grad_kernel(array_count, layout, *refs):
    arrays, refs = refs[:array_count], refs[array_count:]
    lefts, (out_ref, left_scr, scratch) = refs[:len(layout)], refs[len(layout):]

    @pl.when(pl.program_id(0) == 0)
    def _():
        col = 0
        for left in lefts:
            size = left.shape[0]
            left_scr[:, col:col + size] = left[...].T
            col += size

    stack_rows(arrays, layout, scratch)
    out_ref[...] = dot(left_scr[...], scratch[...]).astype(BF16)


def down_grad(lefts, stages):
    arrays, layout = stage_arrays(stages)
    width = arrays[0].shape[1]
    units = lefts[0].shape[1]
    rows = sum(r.shape[0] for r in lefts)
    step = min(256, width)
    return pl.pallas_call(
        functools.partial(down_grad_kernel, len(arrays), layout),
        grid=(width // step,),
        in_specs=[pl.BlockSpec((p.shape[0], step), lambda i: (0, i)) for p in arrays]
        + [pl.BlockSpec(r.shape, lambda i: (0, 0)) for r in lefts],
        out_specs=pl.BlockSpec((units, step), lambda i: (0, i)),
        out_shape=jax.ShapeDtypeStruct((units, width), BF16),
        scratch_shapes=[pltpu.VMEM((units, rows), BF16), pltpu.VMEM((rows, step), BF16)],
        compiler_params=pltpu.CompilerParams(vmem_limit_bytes=VMEM),
        cost_estimate=COST,
        name="down_grad",
    )(*arrays, *lefts)


def place_kernel(index_ref, *refs):
    parts, outs = refs[:-2], refs[-2:]
    devices = len(parts) // 2
    for d in range(devices):
        @pl.when(pl.program_id(1) == d)
        def _(d=d):
            outs[0][...] = parts[d][...].astype(F32)
            outs[1][...] = parts[devices + d][...].astype(F32)


def place(parts, own, part):
    devices = len(parts)
    rows, mine = parts[0].shape[0], parts[0].shape[1] // 2
    blocks = mine // part
    if part % LANES:
        stack = jnp.stack(parts).reshape(devices, rows, 2, blocks, part)
        stack = jnp.stack([take(stack, own ^ d) for d in range(devices)])
        both = stack.transpose(2, 1, 3, 0, 4).reshape(2, rows, -1).astype(F32)
        return both[0], both[1]
    first = pl.BlockSpec((rows, part), lambda b, d, n: (0, b))
    second = pl.BlockSpec((rows, part), lambda b, d, n: (0, blocks + b))
    return pl.pallas_call(
        place_kernel,
        grid_spec=pltpu.PrefetchScalarGridSpec(
            num_scalar_prefetch=1,
            grid=(blocks, devices),
            in_specs=[first] * devices + [second] * devices,
            out_specs=[pl.BlockSpec((rows, part), lambda b, d, n: (0, b * devices + (n[0] ^ d)))] * 2,
        ),
        out_shape=[jax.ShapeDtypeStruct((rows, devices * mine), F32)] * 2,
        compiler_params=pltpu.CompilerParams(vmem_limit_bytes=VMEM),
        cost_estimate=COST,
        name="place",
    )(own.astype(jnp.int32).reshape(1), *parts, *parts)


X, Y, Z, C = "fo", "si", "zb", "fi"


def swap(values, axis, offset=1):
    size = lax.axis_size(axis)
    return lax.ppermute(values, axis, [(i, i ^ offset) for i in range(size)])


def swap_cube(values, offset):
    if len(offset) == 1:
        return swap(values, offset[0])
    sizes = [lax.axis_size(a) for a in offset]
    total = 1
    for size in sizes:
        total *= size
    pairs = []
    for i in range(total):
        rest, place = i, []
        for size in reversed(sizes):
            place.append(rest % size ^ 1)
            rest //= size
        j = 0
        for size, p in zip(sizes, reversed(place)):
            j = j * size + p
        pairs.append((i, j))
    return lax.ppermute(values, offset, pairs)


def sync(*values):
    leaves, tree = jax.tree.flatten(values)
    return jax.tree.unflatten(tree, lax.optimization_barrier(leaves))


STAGES = (((),), ((X,), (Y,), (Z,)), ((X, Z), (X, Y), (Z, Y), (X, Z, Y)))


def other_core(arrays):
    return swap(arrays[0] if len(arrays) == 1 else jnp.concatenate(arrays, axis=0), C)


def add_low(left, right):
    return (left.astype(F32) + right.astype(F32)).astype(BF16)


def send_home(stage, here, other):
    total = add_low(here, other)
    return [total[n] if not offset else swap_cube(total[n], offset) for n, offset in enumerate(STAGES[stage])]


def take(partial, block):
    return lax.dynamic_index_in_dim(partial, block, 0, keepdims=False)


def send_far(partial, za):
    return [swap(take(partial, za ^ k), "za", k) for k in range(1, lax.axis_size("za"))]


def add_far(partial, got, za):
    total = take(partial, za).astype(F32)
    for g in got:
        total = total + g.astype(F32)
    return total


def per_device(
    tokens, bounds, cotangent, attn_gain, query_weight, key_matrix, value_matrix,
    query_gain, key_gain, out_weight, ffn_gain, gate_weight, up_weight, down_weight,
):
    fsdp = ("fo", "fi")
    seq = ("za", "zb", "si")
    rows, width = tokens.shape
    f_count = lax.axis_size(fsdp)
    s_count = lax.axis_size(seq)
    far = lax.axis_size("za")
    f_index = lax.axis_index(fsdp)
    s_index = lax.axis_index(seq)
    za, zb, si = lax.axis_index("za"), lax.axis_index("zb"), lax.axis_index("si")
    length = rows * s_count
    heads = QUERY_HEADS // s_count
    copies = max(1, s_count // KEY_VALUE_HEADS)
    assert KEY_VALUE_HEADS * copies == s_count
    q_cols = heads * HEAD_SIZE
    cols = q_cols + 2 * HEAD_SIZE
    padded = -(-cols // LANES) * LANES
    all_q, all_kv = QUERY_HEADS * HEAD_SIZE, KEY_VALUE_HEADS * HEAD_SIZE

    pieces = [
        query_weight.reshape(-1, s_count, q_cols),
        jnp.repeat(key_matrix.reshape(-1, KEY_VALUE_HEADS, HEAD_SIZE), copies, axis=1),
        jnp.repeat(value_matrix.reshape(-1, KEY_VALUE_HEADS, HEAD_SIZE), copies, axis=1),
    ]
    kv_start = (s_index // copies) * HEAD_SIZE
    own_cols = [
        lax.dynamic_slice_in_dim(query_weight, s_index * q_cols, q_cols, 1),
        lax.dynamic_slice_in_dim(key_matrix, kv_start, HEAD_SIZE, 1),
        lax.dynamic_slice_in_dim(value_matrix, kv_start, HEAD_SIZE, 1),
    ]
    if padded > cols:
        pieces.append(jnp.zeros(pieces[0].shape[:2] + (padded - cols,), BF16))
        own_cols.append(jnp.zeros((query_weight.shape[0], padded - cols), BF16))
    w_own = lax.all_gather(jnp.concatenate(own_cols, axis=1), fsdp, axis=0, tiled=True)
    out_full = lax.all_gather(out_weight, fsdp, axis=0, tiled=True)
    w_rows = jnp.concatenate(pieces, axis=2).reshape(-1, s_count * padded)
    w_quarter = w_rows.shape[0] // 4
    w_parts = [w_rows[:w_quarter], w_rows[w_quarter:2 * w_quarter], w_rows[2 * w_quarter:]]

    far_list = [(k, swap(tokens, "za", k)) for k in range(1, far)]
    x_y, x_z, c_x = swap(tokens, Y), swap(tokens, Z), swap(cotangent, X)
    ids = jnp.arange(length, dtype=jnp.int32)
    b0, b1 = bounds[0, 0], bounds[0, 1]
    starts = jnp.where(ids >= b1, b1, jnp.where(ids >= b0, b0, 0))
    frequency = ROPE_BASE ** (-(jnp.arange(HEAD_SIZE // 2, dtype=F32) * 2.0 / HEAD_SIZE))
    phases = (ids - starts).astype(F32)[:, None] * frequency[None, :]
    cosine, sine = jnp.cos(phases), jnp.sin(phases)
    cos2 = jnp.concatenate([cosine] * 4, axis=1)
    sin2 = jnp.concatenate([-sine, sine] * 2, axis=1)
    head_gain = jnp.concatenate(
        [query_gain] * heads + [key_gain] + [jnp.ones((padded - cols + HEAD_SIZE,), F32)]
    )[None, :]
    far_list, x_y, x_z, c_x, w_rows, w_parts, cos2, sin2 = sync(
        [b for _, b in far_list], x_y, x_z, c_x, w_rows, w_parts, cos2, sin2
    )

    def some_project(blocks, held):
        index = jnp.stack([((za ^ k) * 2 + (zb ^ dz)) * 2 + (si ^ dy) for (k, dz, dy), _ in blocks])
        return project(
            heads, [b for _, b in blocks], index.astype(jnp.int32), bounds[0], attn_gain[None, :], w_own, head_gain,
            cos2, sin2, length, held,
        )

    far_y = [swap(b, Y) for b in far_list]
    far_z = [swap(b, Z) for b in far_list]
    held = some_project([((0, 0, 0), tokens), ((0, 0, 1), x_y), ((0, 1, 0), x_z)], None)
    far_y, far_z, held, x_y = sync(far_y, far_z, held, x_y)
    x_yz = swap(x_y, Z)
    far_yz = [swap(b, Y) for b in far_z]
    for n, k in enumerate(range(1, far)):
        held = some_project([((k, 0, 0), far_list[n]), ((k, 0, 1), far_y[n]), ((k, 1, 0), far_z[n])], held)
    w_c = swap(w_rows, C)
    c_own_other = other_core([cotangent])
    x_yz, far_yz, held, w_c, c_own_other, cot, c_x, w_parts = sync(
        x_yz, far_yz, held, w_c, c_own_other, cotangent, c_x, w_parts
    )
    c_y, c_z = swap(cot, Y), swap(cot, Z)
    w_x = [swap(w_parts[0], X)]
    mid = rows // 2
    c_xy, c_xz = [swap(c_x[:mid], Y)], [swap(c_x[:mid], Z)]
    held = some_project([((0, 1, 1), x_yz)] + [((k, 1, 1), far_yz[n]) for n, k in enumerate(range(1, far))], held)
    normed, q, k, v, unit, scale = held
    attended_low, attended, q2 = attend(heads, q, k, v)
    c_y, c_z, attended_low, c_x, c_xy, c_xz, w_x = sync(c_y, c_z, attended_low, c_x, c_xy, c_xz, w_x)
    heads_out = lax.all_to_all(attended_low, seq, split_axis=0, concat_axis=1, tiled=True)
    c_xyz = [swap(c_xy[0], Z)]
    c_xy.append(swap(c_y[mid:], X))
    c_xz.append(swap(c_z[mid:], X))
    c_yz = swap(c_z, Y)
    c_one = [c_x, c_y, c_z]
    c_one_other = other_core(c_one)
    heads_out, c_xz, c_xy, c_yz, c_xyz, c_one_other = sync(heads_out, c_xz, c_xy, c_yz, c_xyz, c_one_other)

    inputs = tokens.astype(F32)
    square_one = jnp.mean(inputs * inputs, axis=1, keepdims=True)
    scale_one = lax.rsqrt(square_one + EPSILON)
    residual = inputs + dot(heads_out, out_full)
    square_two = jnp.mean(residual * residual, axis=1, keepdims=True)
    scale_two = lax.rsqrt(square_two + EPSILON)
    inner = (residual * scale_two * ffn_gain).astype(BF16)
    c_xyz.append(swap(c_yz[mid:], X))
    c_two_other = [swap(c, C) for c in c_xz + c_xy]
    inner, c_xyz, c_two_other, c_yz = sync(inner, c_xyz, c_two_other, c_yz)

    units = gate_weight.shape[1]
    part = units // s_count
    mine = far * part
    own_block = zb * 2 + si
    if part % LANES == 0:
        weights = (gate_weight, up_weight, down_weight)
        unit_index = (jnp.arange(far, dtype=jnp.int32) * 4 + own_block).astype(jnp.int32)
        width_of_part = part
    else:
        pick = lambda w: lax.dynamic_index_in_dim(
            w.reshape(width, far, 4, part), own_block, 2, keepdims=False
        ).reshape(width, mine)
        weights = (
            pick(gate_weight),
            pick(up_weight),
            lax.dynamic_index_in_dim(
                down_weight.reshape(far, 4, part, width), own_block, 1, keepdims=False
            ).reshape(mine, width),
        )
        unit_index = jnp.zeros((1,), jnp.int32)
        width_of_part = mine
    run = lambda x_stage, c_stage: feed(x_stage, c_stage, unit_index, weights, width_of_part)
    x, y, z = swap(inner, X), swap(inner, Y), swap(inner, Z)
    c_two_other.append(swap(c_yz, C))
    x_stages = [([[inner]], [other_core([inner])])]
    c_stages = [([[cot]], [c_own_other])]
    fed = [run(x_stages[0], c_stages[0])]
    x, y, z, fed, inner, c_xyz, c_two_other = sync(x, y, z, fed, inner, c_xyz, c_two_other)
    c_two = [c_xz, c_xy, [c_yz], c_xyz]
    xy, xz, yz = swap(x, Y), swap(z, X), swap(y, Z)
    xyz = swap_cube(inner, (X, Z, Y))
    x_stages.append(([[x], [y], [z]], [other_core([x, y, z])]))
    c_stages.append(([[c] for c in c_one], [c_one_other]))
    c_two_other += [swap(c, C) for c in c_xyz]
    fed.append(run(x_stages[1], c_stages[1]))
    xy, xz, yz, xyz, fed, x_stages, w_parts, c_two, c_two_other = sync(
        xy, xz, yz, xyz, fed, x_stages, w_parts, c_two, c_two_other
    )
    x_stages.append(([[xz], [xy], [yz], [xyz]], [other_core([xz, xy, yz, xyz])]))
    c_stages.append((c_two, c_two_other))
    d_home = send_home(0, fed[0][0], swap(fed[0][1], C)) + send_home(1, fed[1][0], swap(fed[1][1], C))
    w_x.append(swap(w_parts[1], X))
    fed.append(run(x_stages[2], c_stages[2]))
    d_home, fed, x_stages, w_x = sync(d_home, fed, x_stages, w_x)
    far_xz, far_xy, far_yz, far_xyz = add_low(fed[2][0], swap(fed[2][1], C))
    hops = [swap(far_xyz, Y), swap(far_xy, X), swap(far_yz, Z)]
    down_part = down_grad([f[4] for f in fed], c_stages)
    far_xz, hops, d_home, down_part, fed = sync(far_xz, hops, d_home, down_part, fed)
    d_home += [swap_cube(add_low(far_xz, hops[0]), (X, Z)), swap(add_low(hops[1], hops[2]), Y)]
    m_other = [swap(f[3], C) for f in fed[:2]]
    gu_part = gate_grad(x_stages, [f[5] for f in fed])
    d_home, down_part, gu_part, fed, m_other, heads_out = sync(
        d_home, down_part, gu_part, fed, m_other, heads_out
    )
    gu_far = lax.psum_scatter(gu_part, "za", scatter_dimension=0, tiled=True)
    down_far = lax.psum_scatter(down_part, "za", scatter_dimension=0, tiled=True)
    quarter = width // far // 4

    def to_owners(values):
        spread = []
        for offset, axes in enumerate(((), (Y,), (Z,), (Z, Y))):
            block = lax.dynamic_slice_in_dim(values, (own_block ^ offset) * quarter, quarter, 0)
            spread.append(swap_cube(block, axes) if axes else block)
        return spread

    m_other.append(swap(fed[2][3], C))
    own_rows = out_weight.shape[0]
    left = []
    for offset in range(f_count):
        block = lax.dynamic_slice_in_dim(heads_out, (f_index ^ offset) * own_rows, own_rows, 1)
        left.append(swap(block, fsdp, offset) if offset else block)
    d_inner = sum(a.astype(F32) for a in d_home)
    ffn_part = jnp.sum(d_inner * residual * scale_two, axis=0)
    weighted = d_inner * ffn_gain
    d_residual = cotangent.astype(F32) + scale_two * (
        weighted - residual * scale_two * scale_two * jnp.mean(weighted * residual, axis=1, keepdims=True)
    )
    d_branch = d_residual.astype(BF16)
    d_heads = dot(d_branch, out_full, NT).astype(BF16)
    d_heads, d_branch, m_other, fed, left = sync(d_heads, d_branch, m_other, fed, left)
    d_attended = lax.all_to_all(d_heads, seq, split_axis=1, concat_axis=0, tiled=True)
    over = swap(d_branch, X)
    right = [d_branch, swap(d_branch, C), over, swap(over, C)]
    m = [add_low(f[2], other) for f, other in zip(fed[:2], m_other)]
    m.append([add_low(fed[2][2][n], m_other[2][n]) for n in range(4)])
    m_far = swap(m[2][3], Y)
    w_xc = [swap(jnp.concatenate(w_x, axis=0), C)]
    d_attended, right, m, m_far, w_parts, w_xc = sync(d_attended, right, m, m_far, w_parts, w_xc)
    w_x.append(swap(w_parts[2], X))
    out_part = dot(jnp.concatenate(left, axis=0), jnp.concatenate(right, axis=0), TN).astype(BF16)
    out_part = out_part.reshape(far, 2, 2, -1, width)
    pick = lambda values, index, axis: lax.dynamic_index_in_dim(values, index, axis, keepdims=False)
    out_y = swap(pick(out_part, 1 - si, 2), Y)
    d_qkv, gain_parts = attend_back(
        heads, q2, k, v, sync(d_attended, out_part)[0], attended, unit, scale, head_gain, cos2, sin2
    )
    d_qkv, gain_parts, m, m_far, w_x, w_xc, out_part, out_y = sync(
        d_qkv, gain_parts, m, m_far, w_x, w_xc, out_part, out_y
    )
    d_tok = lax.all_to_all(d_qkv, seq, split_axis=0, concat_axis=1, tiled=True)
    proj_part = dot(normed, d_qkv, TN).astype(BF16).reshape(2, 2, width // 4, padded)
    fi, fo = lax.axis_index(C), lax.axis_index(X)
    proj_core = add_low(pick(proj_part, fi, 1), swap(pick(proj_part, 1 - fi, 1), C))
    proj_x = swap(take(proj_core, 1 - fo), X)
    w_xc.append(swap(w_x[2], C))
    m_x, m_yz = swap(m[2][1], X), swap(m[2][2], Y)
    out_part = add_low(pick(out_part, si, 2), out_y)
    m_xz = add_low(m[2][0], m_far)
    d_tok, proj_core, proj_x, w_xc, out_part, m, m_x, m_yz, m_xz, gain_parts, gu_far = sync(
        d_tok, proj_core, proj_x, w_xc, out_part, m, m_x, m_yz, m_xz, gain_parts, gu_far
    )
    m_z = [swap(m_xz, X), m_yz]
    spread = to_owners(gu_far)
    blocks = [w_rows, w_c, jnp.concatenate(w_x, axis=0), jnp.concatenate(w_xc, axis=0)]
    by_offset = jnp.stack([dot(d_tok, w, NT) for w in blocks])
    d_normed = jnp.concatenate([take(by_offset, f_index ^ n) for n in range(f_count)], axis=1)
    weighted = d_normed * attn_gain
    input_grad = (
        d_residual
        + scale_one
        * (weighted - inputs * scale_one * scale_one * jnp.mean(weighted * inputs, axis=1, keepdims=True))
    ).astype(BF16)
    proj_rows = add_low(take(proj_core, fo), proj_x)
    gain_row = gain_parts[0]
    pack = jnp.concatenate(
        [
            ffn_part,
            gain_row[:q_cols].reshape(heads, HEAD_SIZE).sum(axis=0),
            gain_row[q_cols:q_cols + HEAD_SIZE],
        ]
    ).reshape(-1, LANES)
    for axis in ("fi", "fo", "si", "zb", "za"):
        offset = 1
        while offset < lax.axis_size(axis):
            pack = pack + swap(pack, axis, offset)
            offset *= 2
    pack = pack.reshape(-1)
    m_one = [m[1][0], add_low(m[1][1], m_x)]
    m_z, spread, input_grad, proj_rows, m, m_one, out_part, pack = sync(
        m_z, spread, input_grad, proj_rows, m, m_one, out_part, pack
    )
    proj = lax.all_to_all(proj_rows, seq, split_axis=0, concat_axis=1, tiled=True)
    m_last = [swap(m_one[0], X), swap(m_one[1], Y)]
    m_last.append(swap((m[1][2].astype(F32) + m_z[0].astype(F32) + m_z[1].astype(F32)).astype(BF16), Z))
    out_z = swap(pick(out_part, 1 - zb, 1), Z)
    gate_mine, up_mine = place(spread, own_block, part)
    proj, gate_mine, up_mine, m, m_last, out_part, out_z, down_far = sync(
        proj, gate_mine, up_mine, m, m_last, out_part, out_z, down_far
    )
    out_part = add_low(pick(out_part, zb, 1), out_z)
    out_got = send_far(out_part, za)
    down_mine = down_far.astype(F32)
    mlp_out = m[0][0].astype(F32) + sum(a.astype(F32) for a in m_last)
    block_output = (residual + mlp_out).astype(BF16)
    out_mine = add_far(out_part, out_got, za)
    proj = proj.astype(F32)
    count = proj.shape[0]
    by_device = proj.reshape(count, s_count, padded)

    def fold(values):
        return values.reshape(count, KEY_VALUE_HEADS, copies, HEAD_SIZE).sum(axis=2).reshape(count, -1)

    query_mine = by_device[:, :, :q_cols].reshape(count, QUERY_HEADS * HEAD_SIZE)
    key_mine = fold(by_device[:, :, q_cols:q_cols + HEAD_SIZE])
    value_mine = fold(by_device[:, :, q_cols + HEAD_SIZE:cols])

    my_w = lax.dynamic_slice_in_dim(w_rows, s_index * count, count, 0).astype(F32)
    my_gain = lax.dynamic_slice_in_dim(attn_gain, (f_index * s_count + s_index) * count, count, 0)
    attn_gain_mine = jnp.sum(my_w * proj, axis=1) / my_gain
    ffn_gain_mine = lax.dynamic_slice_in_dim(pack, (f_index * s_count + s_index) * count, count, 0)
    attn_rms = jnp.sqrt(square_one + EPSILON)[:, 0]
    mlp_rms = jnp.sqrt(square_two + EPSILON)[:, 0]
    return (
        block_output, input_grad, residual, attn_rms, mlp_rms, attn_gain_mine,
        query_mine, key_mine, value_mine, pack[width:width + HEAD_SIZE], pack[width + HEAD_SIZE:],
        out_mine, ffn_gain_mine, gate_mine, up_mine, down_mine,
    )


def solution(mesh):
    f_count, s_count = mesh.shape["fsdp"], mesh.shape["seq"]
    fine = Mesh(
        mesh.devices.reshape(f_count // 2, 2, s_count // 4, 2, 2), ("fo", "fi", "za", "zb", "si")
    )
    f, s = ("fo", "fi"), ("za", "zb", "si")
    every = P(f + s, None)
    vector = P(f + s)
    placed = (
        every, P(f, None), every, P(), P(f, None), P(f, None), P(f, None), P(), P(),
        P(f, None), P(), P(None, f), P(None, f), P(f, None),
    )
    return jax.shard_map(
        per_device,
        mesh=fine,
        in_specs=placed,
        out_specs=(
            every, every, every, vector, vector, vector, every, every, every, P(), P(),
            every, vector, P(s, f), P(s, f), every,
        ),
        check_vma=False,
    )
```

```python
import functools

import jax
import jax.numpy as jnp
from jax import lax
from jax.experimental import pallas as pl
from jax.experimental.pallas import tpu as pltpu
from jax.sharding import Mesh, PartitionSpec as P

HEAD_SIZE = 64
QUERY_HEADS = 32
KEY_VALUE_HEADS = 8
EPSILON = 1e-05
ROPE_BASE = 1000000.0
BIG = 30000.0
LANES = 128
BLOCK = 256
UNROLLED = 2048
VMEM = 60 * 1024 * 1024
COST = pl.CostEstimate(flops=1000, bytes_accessed=1000, transcendentals=0)

F32 = jnp.float32
BF16 = jnp.bfloat16
NT = (((1,), (1,)), ((), ()))
TN = (((0,), (0,)), ((), ()))


def dot(left, right, dims=(((1,), (0,)), ((), ()))):
    return lax.dot_general(left, right, dims, preferred_element_type=F32)


def split_low(values):
    high = values.astype(BF16)
    return high, (values - high.astype(F32)).astype(BF16)


def head_means(values, ones):
    high, low = split_low(values)
    return (dot(high, ones) + dot(low, ones)) * (1.0 / HEAD_SIZE)


def head_ones():
    row = lax.broadcasted_iota(jnp.int32, (LANES, LANES), 0) // HEAD_SIZE
    col = lax.broadcasted_iota(jnp.int32, (LANES, LANES), 1) // HEAD_SIZE
    return jnp.where(row == col, 1.0, 0.0).astype(BF16)


def swap_halves(values):
    lane = lax.broadcasted_iota(jnp.int32, values.shape, 1) % HEAD_SIZE
    half = HEAD_SIZE // 2
    return jnp.where(
        lane < half, pltpu.roll(values, LANES - half, 1), pltpu.roll(values, half, 1)
    )


def project_kernel(heads, count, fresh, index_ref, bounds_ref, *refs):
    x_refs = refs[:count]
    gain_ref, w_ref, head_gain_ref, cos_ref, sin_ref = refs[count:count + 5]
    refs = refs[count + 5 + (0 if fresh else 6):]
    normed_ref, q_ref, k_ref, v_ref, unit_ref, scale_ref, x_scr = refs
    i = pl.program_id(0)
    rows = x_scr.shape[0]
    for r in range(count):
        @pl.when(i == r)
        def _(r=r):
            x_scr[...] = x_refs[r][...]

    x = x_scr[...].astype(F32)
    scale = lax.rsqrt(jnp.mean(x * x, axis=1, keepdims=True) + EPSILON)
    normed = (x * scale * gain_ref[...]).astype(BF16)
    normed_ref[...] = normed
    pre = dot(normed, w_ref[...])
    cosine, sine = cos_ref[...], sin_ref[...]
    shape = (rows, LANES)
    token = index_ref[i] * rows + lax.broadcasted_iota(jnp.int32, shape, 0)
    doc = (token >= bounds_ref[0]).astype(jnp.int32) + (token >= bounds_ref[1]).astype(jnp.int32)
    lane = lax.broadcasted_iota(jnp.int32, shape, 1)
    mark = lane - HEAD_SIZE
    query_marks = jnp.where(mark == doc, 1.0, 0.0)
    key_marks = jnp.where(mark < 3, jnp.where(mark == doc, 0.0, -BIG), jnp.where(mark < 5, 1.0, 0.0))
    value_marks = jnp.where(mark < 2, 1.0, 0.0)
    ones = head_ones()

    def place(values, segment, marks):
        group = values if segment % 2 == 0 else pltpu.roll(values, HEAD_SIZE, 1)
        return jnp.where(lane < HEAD_SIZE, group, marks).astype(BF16)

    for g in range(pre.shape[1] // LANES):
        cols = slice(g * LANES, (g + 1) * LANES)
        u = pre[:, cols]
        r = lax.rsqrt(head_means(u * u, ones) + EPSILON)
        unit = u * r
        unit_ref[:, cols] = unit
        scale_ref[:, cols] = r
        gained = unit * head_gain_ref[0:1, cols]
        rot = (gained * cosine + swap_halves(gained) * sine).astype(BF16).astype(F32)
        for segment in (2 * g, 2 * g + 1):
            if segment < heads:
                q_ref[segment] = place(rot * 0.125, segment, query_marks)
            elif segment == heads:
                k_ref[...] = place(rot, segment, key_marks)
            elif segment == heads + 1:
                v_ref[...] = place(u, segment, value_marks)


def project(heads, blocks, index, bounds, gain, w, head_gain, cosine, sine, length, held=None):
    rows, width = blocks[0].shape
    count = len(blocks)
    cols = w.shape[1]
    row = lambda c: pl.BlockSpec((rows, c), lambda i, n, b: (n[i], 0))
    whole = lambda a: pl.BlockSpec(a.shape, lambda i, n, b: (0, 0))
    fresh = held is None
    held = () if fresh else held
    outs = [
        jax.ShapeDtypeStruct((length, width), BF16),
        jax.ShapeDtypeStruct((heads, length, LANES), BF16),
        jax.ShapeDtypeStruct((length, LANES), BF16),
        jax.ShapeDtypeStruct((length, LANES), BF16),
        jax.ShapeDtypeStruct((length, cols), F32),
        jax.ShapeDtypeStruct((length, cols), F32),
    ]
    tokens = rows * count
    return pl.pallas_call(
        functools.partial(project_kernel, heads, count, fresh),
        grid_spec=pltpu.PrefetchScalarGridSpec(
            num_scalar_prefetch=2,
            grid=(count,),
            in_specs=[whole(b) for b in blocks]
            + [whole(gain), whole(w), whole(head_gain), row(LANES), row(LANES)]
            + [pl.BlockSpec(memory_space=pl.ANY)] * len(held),
            out_specs=[
                row(width),
                pl.BlockSpec((heads, rows, LANES), lambda i, n, b: (0, n[i], 0)),
                row(LANES),
                row(LANES),
                row(cols),
                row(cols),
            ],
            scratch_shapes=[pltpu.VMEM((rows, width), BF16)],
        ),
        out_shape=outs,
        input_output_aliases={2 + count + 5 + n: n for n in range(len(held))},
        compiler_params=pltpu.CompilerParams(vmem_limit_bytes=VMEM),
        cost_estimate=COST,
        name="project",
    )(index, bounds, *blocks, gain, w, head_gain, cosine, sine, *held)


def attend_kernel(heads, q_ref, k_ref, v_ref, low_ref, out_ref, q2_ref):
    i = pl.program_id(0)
    rows = BLOCK
    q = q_ref[...].reshape(heads * rows, LANES)

    def step(j, total):
        start = pl.multiple_of(j * rows, rows)
        p = jnp.exp(dot(q, k_ref[pl.ds(start, rows), :], NT)).astype(BF16)
        return total + dot(p, v_ref[pl.ds(start, rows), :])

    total = lax.fori_loop(0, i, step, jnp.zeros((heads * rows, LANES), F32))
    start = pl.multiple_of(i * rows, rows)
    s = dot(q, k_ref[pl.ds(start, rows), :], NT)
    t_local = lax.broadcasted_iota(jnp.int32, s.shape, 0) % rows
    u_local = lax.broadcasted_iota(jnp.int32, s.shape, 1)
    p = jnp.where(u_local <= t_local, jnp.exp(s), 0.0).astype(BF16)
    total = total + dot(p, v_ref[pl.ds(start, rows), :])
    weight = total[:, HEAD_SIZE:HEAD_SIZE + 1]
    out = total[:, :HEAD_SIZE] / weight
    for h in range(heads):
        part = out[h * rows:(h + 1) * rows, :]
        out_ref[:, h * HEAD_SIZE:(h + 1) * HEAD_SIZE] = part
        low_ref[:, h * HEAD_SIZE:(h + 1) * HEAD_SIZE] = part.astype(BF16)
    high, low = split_low(-jnp.log(weight))
    lane = lax.broadcasted_iota(jnp.int32, q.shape, 1)
    q2 = jnp.where(lane == HEAD_SIZE + 3, high, jnp.where(lane == HEAD_SIZE + 4, low, q))
    q2_ref[...] = q2.reshape(heads, rows, LANES)


def attend_unrolled_kernel(heads, rows, q_ref, k_ref, v_ref, low_ref, out_ref, q2_ref):
    stretch = q_ref.shape[1]

    def block(first, at):
        q = q_ref[:, at:at + rows, :].reshape(heads * rows, LANES)
        s = dot(q, k_ref[first:first + rows, :], NT)
        t_local = lax.broadcasted_iota(jnp.int32, s.shape, 0) % rows
        u_local = lax.broadcasted_iota(jnp.int32, s.shape, 1)
        p = jnp.where(u_local <= t_local, jnp.exp(s), 0.0).astype(BF16)
        total = dot(p, v_ref[first:first + rows, :])
        if first:
            p = jnp.exp(dot(q, k_ref[:first, :], NT)).astype(BF16)
            total = total + dot(p, v_ref[:first, :])
        weight = total[:, HEAD_SIZE:HEAD_SIZE + 1]
        out = total[:, :HEAD_SIZE] / weight
        for h in range(heads):
            part = out[h * rows:(h + 1) * rows, :]
            out_ref[at:at + rows, h * HEAD_SIZE:(h + 1) * HEAD_SIZE] = part
            low_ref[at:at + rows, h * HEAD_SIZE:(h + 1) * HEAD_SIZE] = part.astype(BF16)
        high, low = split_low(-jnp.log(weight))
        lane = lax.broadcasted_iota(jnp.int32, q.shape, 1)
        q2 = jnp.where(lane == HEAD_SIZE + 3, high, jnp.where(lane == HEAD_SIZE + 4, low, q))
        q2_ref[:, at:at + rows, :] = q2.reshape(heads, rows, LANES)

    for step in range(k_ref.shape[0] // stretch):
        @pl.when(pl.program_id(0) == step)
        def _(step=step):
            for at in range(0, stretch, rows):
                block(step * stretch + at, at)


def attend(heads, q, k, v):
    tokens = k.shape[0]
    if tokens <= UNROLLED and tokens % (2 * BLOCK) == 0:
        kernel, rows = functools.partial(attend_unrolled_kernel, heads, BLOCK // 2), 2 * BLOCK
    else:
        kernel, rows = functools.partial(attend_kernel, heads), BLOCK
    return pl.pallas_call(
        kernel,
        grid=(tokens // rows,),
        in_specs=[
            pl.BlockSpec((heads, rows, LANES), lambda i: (0, i, 0)),
            pl.BlockSpec((tokens, LANES), lambda i: (0, 0)),
            pl.BlockSpec((tokens, LANES), lambda i: (0, 0)),
        ],
        out_specs=[
            pl.BlockSpec((rows, heads * HEAD_SIZE), lambda i: (i, 0)),
            pl.BlockSpec((rows, heads * HEAD_SIZE), lambda i: (i, 0)),
            pl.BlockSpec((heads, rows, LANES), lambda i: (0, i, 0)),
        ],
        out_shape=[
            jax.ShapeDtypeStruct((tokens, heads * HEAD_SIZE), BF16),
            jax.ShapeDtypeStruct((tokens, heads * HEAD_SIZE), F32),
            jax.ShapeDtypeStruct((heads, tokens, LANES), BF16),
        ],
        compiler_params=pltpu.CompilerParams(vmem_limit_bytes=VMEM),
        cost_estimate=COST,
        name="attend",
    )(q, k, v)


def attend_back_kernel(heads, q_ref, k_ref, v_ref, grad_ref, out_ref, unit_hbm, scale_hbm, head_gain_ref,
                       cos_hbm, sin_hbm, dqkv_ref, gains_ref, g_scr, dq_scr, dk_scr, dv_scr,
                       unit_ref, scale_ref, cos_ref, sin_ref, sems):
    rows = BLOCK
    tokens = k_ref.shape[0]
    blocks = tokens // rows
    wide = heads * rows
    late = [
        pltpu.make_async_copy(source, target, sems.at[n])
        for n, (source, target) in enumerate(
            ((unit_hbm, unit_ref), (scale_hbm, scale_ref), (cos_hbm, cos_ref), (sin_hbm, sin_ref))
        )
    ]
    for copy in late:
        copy.start()

    def prepare(i, carry):
        at = pl.ds(pl.multiple_of(i * rows, rows), rows)
        lane = lax.broadcasted_iota(jnp.int32, (rows, HEAD_SIZE), 1)
        for h in range(heads):
            cols = slice(h * HEAD_SIZE, (h + 1) * HEAD_SIZE)
            grad = grad_ref[at, cols]
            delta = jnp.sum(grad.astype(F32) * out_ref[at, cols], axis=1, keepdims=True)
            high, low = split_low(-delta)
            g_scr[h, at, :HEAD_SIZE] = grad
            g_scr[h, at, HEAD_SIZE:] = jnp.where(lane == 0, high, jnp.where(lane == 1, low, jnp.zeros_like(low)))
        dq_scr[:, at, :] = jnp.zeros((heads, rows, LANES), F32)
        return carry

    lax.fori_loop(0, blocks, prepare, 0)

    def pair(j, i, diagonal):
        at = pl.ds(i * rows, rows)
        k = k_ref[pl.ds(j * rows, rows), :]
        q = q_ref[:, at, :].reshape(wide, LANES)
        g = g_scr[:, at, :].reshape(wide, LANES)
        p = jnp.exp(dot(k, q, NT))
        if diagonal:
            u_local = lax.broadcasted_iota(jnp.int32, p.shape, 0)
            t_local = lax.broadcasted_iota(jnp.int32, p.shape, 1) % rows
            p = jnp.where(u_local <= t_local, p, 0.0)
        dv = dot(p.astype(BF16), g)
        ds = (p * dot(v_ref[pl.ds(j * rows, rows), :], g, NT)).astype(BF16)
        dk = dot(ds, q)
        dq_scr[:, at, :] += dot(ds, k, TN).reshape(heads, rows, LANES)
        return dk, dv

    def key_step(j, carry):
        def query_step(i, state):
            dk, dv = pair(j, i, False)
            return state[0] + dk, state[1] + dv

        state = pair(j, j, True)
        if tokens <= UNROLLED:
            for i in range(j + 1, blocks):
                state = query_step(i, state)
        else:
            state = lax.fori_loop(j + 1, blocks, query_step, state)
        dk_scr[pl.ds(j * rows, rows), :] = state[0]
        dv_scr[pl.ds(j * rows, rows), :] = state[1]
        return carry

    if tokens <= UNROLLED:
        for j in range(blocks):
            key_step(j, 0)
    else:
        lax.fori_loop(0, blocks, key_step, 0)
    for copy in late:
        copy.wait()
    groups = unit_ref.shape[1] // LANES
    ones = head_ones()

    def finish(i, carry):
        at = pl.ds(pl.multiple_of(i * rows, rows), rows)
        cosine, sine = cos_ref[at, :], sin_ref[at, :]
        lane = lax.broadcasted_iota(jnp.int32, (rows, LANES), 1)

        def segment_of(s):
            if s < heads:
                return dq_scr[s, at, :] * 0.125
            return (dk_scr if s == heads else dv_scr)[at, :]

        sums = list(carry)
        for g in range(groups):
            cols = slice(g * LANES, (g + 1) * LANES)
            first = segment_of(2 * g)
            last = segment_of(2 * g + 1) if 2 * g + 1 < heads + 2 else first
            d = jnp.where(lane < HEAD_SIZE, first, pltpu.roll(last, HEAD_SIZE, 1))
            e = d * cosine - swap_halves(d) * sine
            unit = unit_ref[at, cols]
            sums[g] = sums[g] + jnp.sum(e * unit, axis=0, keepdims=True)
            w = e * head_gain_ref[0:1, cols]
            normal = scale_ref[at, cols] * (w - unit * head_means(w * unit, ones))
            is_value = lane + g * LANES >= (heads + 1) * HEAD_SIZE
            dqkv_ref[at, cols] = jnp.where(is_value, d, normal).astype(BF16)
        return tuple(sums)

    zero = jnp.zeros((1, LANES), F32)
    sums = lax.fori_loop(0, blocks, finish, (zero,) * groups)
    gains_ref[...] = jnp.zeros(gains_ref.shape, F32)
    for g in range(groups):
        gains_ref[0:1, g * LANES:(g + 1) * LANES] = sums[g]


def attend_back(heads, q, k, v, grad, out, unit, scale, head_gain, cosine, sine):
    tokens = k.shape[0]
    cols = unit.shape[1]
    vmem, late = pl.BlockSpec(memory_space=pltpu.VMEM), pl.BlockSpec(memory_space=pl.ANY)
    return pl.pallas_call(
        functools.partial(attend_back_kernel, heads),
        in_specs=[vmem] * 5 + [late] * 2 + [vmem] + [late] * 2,
        out_specs=[vmem] * 2,
        out_shape=[
            jax.ShapeDtypeStruct((tokens, cols), BF16),
            jax.ShapeDtypeStruct((8, cols), F32),
        ],
        scratch_shapes=[
            pltpu.VMEM((heads, tokens, LANES), BF16),
            pltpu.VMEM((heads, tokens, LANES), F32),
            pltpu.VMEM((tokens, LANES), F32),
            pltpu.VMEM((tokens, LANES), F32),
            pltpu.VMEM((tokens, cols), F32),
            pltpu.VMEM((tokens, cols), F32),
            pltpu.VMEM((tokens, LANES), F32),
            pltpu.VMEM((tokens, LANES), F32),
            pltpu.SemaphoreType.DMA((4,)),
        ],
        compiler_params=pltpu.CompilerParams(vmem_limit_bytes=VMEM),
        cost_estimate=COST,
        name="attend_back",
    )(q, k, v, grad, out, unit, scale, head_gain, cosine, sine)


def cut(arrays, sizes, half):
    tiles = [[] for _ in range(sum(sizes) // half)]
    row = 0
    for array, size in zip(arrays, sizes):
        start = 0
        while start < size:
            count = min(size - start, half - row % half)
            tiles[row // half].append((array, start, count))
            start += count
            row += count
    return tiles


def feed_kernel(layouts, weight_count, index_ref, *refs):
    tiles = len(layouts[0][0])
    half = refs[-6].shape[1] // 2
    sides = []
    for pieces, layout in layouts:
        own = []
        for count in pieces:
            own.append(refs[:count])
            refs = refs[count:]
        sides.append((own, cut(refs[:len(layout)], layout, half)))
        refs = refs[len(layout):]
    gate_ref, up_ref, down_ref = refs[:3]
    da_ref, db_ref, ma_ref, mb_ref, hidden_ref, dgu_ref, x_scr, c_scr, gu_scr, down_scr, sem, w_sem = refs[3:]
    i = pl.program_id(0)
    half = x_scr.shape[1] // 2

    def copies(t):
        slot = t % 2
        found = []
        for (own, others), scratch, which in ((sides[0], x_scr, 0), (sides[1], c_scr, 1)):
            size = half // len(own[t])
            for n, piece in enumerate(own[t]):
                found.append(
                    pltpu.make_async_copy(piece, scratch.at[slot, pl.ds(n * size, size)], sem.at[slot, which, n])
                )
            row = half
            for n, (other, start, size) in enumerate(others[t]):
                found.append(
                    pltpu.make_async_copy(
                        other.at[pl.ds(start, size)],
                        scratch.at[slot, pl.ds(row, size)],
                        sem.at[slot, which, n + 2],
                    )
                )
                row += size
        return found

    mine = hidden_ref.shape[1]
    part = mine // weight_count

    def weight_copies(n):
        at = pl.ds(pl.multiple_of(index_ref[n] * part, part), part)
        return [
            pltpu.make_async_copy(gate_ref.at[:, at], gu_scr.at[:, pl.ds(n * part, part)], w_sem.at[n, 0]),
            pltpu.make_async_copy(up_ref.at[:, at], gu_scr.at[:, pl.ds(mine + n * part, part)], w_sem.at[n, 1]),
            pltpu.make_async_copy(down_ref.at[at], down_scr.at[pl.ds(n * part, part)], w_sem.at[n, 2]),
        ]

    for t in range(tiles):
        @pl.when(i == t)
        def _(t=t):
            if t == 0:
                needed = copies(0) + [copy for n in range(weight_count) for copy in weight_copies(n)]
                for copy in needed:
                    copy.start()
            else:
                needed = copies(t)
            if t + 1 < tiles:
                for copy in copies(t + 1):
                    copy.start()
            for copy in needed:
                copy.wait()

    slot = lax.rem(i, 2)
    both = dot(x_scr[slot], gu_scr[...])
    gate, up = both[:, :mine], both[:, mine:]
    d_hidden = dot(c_scr[slot], down_scr[...], NT)
    sigma = 1.0 / (1.0 + jnp.exp(-gate))
    active = gate * sigma
    hidden = (active * up).astype(BF16)
    hidden_ref[...] = hidden
    dgu_ref[:, :mine] = (d_hidden * up * (sigma * (1.0 + gate * (1.0 - sigma)))).astype(BF16)
    dgu_ref[:, mine:] = (d_hidden * active).astype(BF16)
    d_inner = dot(dgu_ref[...], gu_scr[...], NT)
    mlp = dot(hidden, down_scr[...])
    da_ref[0] = d_inner[:half].astype(BF16)
    db_ref[0] = d_inner[half:].astype(BF16)
    ma_ref[0] = mlp[:half].astype(BF16)
    mb_ref[0] = mlp[half:].astype(BF16)


def feed(x_stage, c_stage, index, weights, part):
    (x_own, x_others), (c_own, c_others) = x_stage, c_stage
    tiles = len(x_own)
    half = x_own[0][0].shape[0] * len(x_own[0])
    layouts = tuple(
        (tuple(len(t) for t in own), tuple(o.shape[0] for o in others))
        for own, others in ((x_own, x_others), (c_own, c_others))
    )
    arrays = [a for own, others in ((x_own, x_others), (c_own, c_others)) for a in sum(own, []) + list(others)]
    rows = 2 * half
    gate, up, down = weights
    width = gate.shape[0]
    blocks = index.shape[0]
    mine = blocks * part
    halves = pl.BlockSpec((1, half, width), lambda i, n: (i, 0, 0))
    return pl.pallas_call(
        functools.partial(feed_kernel, layouts, blocks),
        grid_spec=pltpu.PrefetchScalarGridSpec(
            num_scalar_prefetch=1,
            grid=(tiles,),
            in_specs=[pl.BlockSpec(memory_space=pl.ANY)] * (len(arrays) + 3),
            out_specs=[halves] * 4
            + [
                pl.BlockSpec((rows, mine), lambda i, n: (i, 0)),
                pl.BlockSpec((rows, 2 * mine), lambda i, n: (i, 0)),
            ],
            scratch_shapes=[
                pltpu.VMEM((2, rows, width), BF16),
                pltpu.VMEM((2, rows, width), BF16),
                pltpu.VMEM((width, 2 * mine), BF16),
                pltpu.VMEM((mine, width), BF16),
                pltpu.SemaphoreType.DMA((2, 2, 4)),
                pltpu.SemaphoreType.DMA((blocks, 3)),
            ],
        ),
        out_shape=[jax.ShapeDtypeStruct((tiles, half, width), BF16)] * 4
        + [
            jax.ShapeDtypeStruct((tiles * rows, mine), BF16),
            jax.ShapeDtypeStruct((tiles * rows, 2 * mine), BF16),
        ],
        compiler_params=pltpu.CompilerParams(vmem_limit_bytes=VMEM),
        cost_estimate=COST,
        name="feed",
    )(index, *arrays, gate, up, down)


def stage_arrays(stages):
    arrays, layout = [], []
    for own, others in stages:
        half = own[0][0].shape[0] * len(own[0])
        arrays += sum(own, []) + list(others)
        layout.append((half, tuple(len(t) for t in own), tuple(o.shape[0] for o in others)))
    return arrays, tuple(layout)


def stack_rows(refs, layout, scratch):
    at = row = 0
    for half, tiles, others in layout:
        first = at + sum(tiles)
        for pieces, across in zip(tiles, cut(refs[first:first + len(others)], others, half)):
            size = half // pieces
            for n in range(pieces):
                scratch[row:row + size, :] = refs[at + n][...]
                row += size
            at += pieces
            for other, start, size in across:
                scratch[row:row + size, :] = other[start:start + size, :]
                row += size
        at += len(others)


def gate_grad_kernel(array_count, layout, *refs):
    arrays, refs = refs[:array_count], refs[array_count:]
    rights, (out_ref, scratch) = refs[:len(layout)], refs[len(layout):]
    stack_rows(arrays, layout, scratch)
    row = 0
    total = None
    for right in rights:
        size = right.shape[0]
        term = dot(scratch[row:row + size, :], right[...], TN)
        total = term if total is None else total + term
        row += size
    out_ref[...] = total.astype(BF16)


def gate_grad(stages, rights):
    arrays, layout = stage_arrays(stages)
    width = arrays[0].shape[1]
    units = rights[0].shape[1]
    rows = sum(r.shape[0] for r in rights)
    step = min(256, width)
    return pl.pallas_call(
        functools.partial(gate_grad_kernel, len(arrays), layout),
        grid=(width // step,),
        in_specs=[pl.BlockSpec((p.shape[0], step), lambda i: (0, i)) for p in arrays]
        + [pl.BlockSpec(r.shape, lambda i: (0, 0)) for r in rights],
        out_specs=pl.BlockSpec((step, units), lambda i: (i, 0)),
        out_shape=jax.ShapeDtypeStruct((width, units), BF16),
        scratch_shapes=[pltpu.VMEM((rows, step), BF16)],
        compiler_params=pltpu.CompilerParams(vmem_limit_bytes=VMEM),
        cost_estimate=COST,
        name="gate_grad",
    )(*arrays, *rights)


def down_grad_kernel(array_count, layout, *refs):
    arrays, refs = refs[:array_count], refs[array_count:]
    lefts, (out_ref, left_scr, scratch) = refs[:len(layout)], refs[len(layout):]

    @pl.when(pl.program_id(0) == 0)
    def _():
        col = 0
        for left in lefts:
            size = left.shape[0]
            left_scr[:, col:col + size] = left[...].T
            col += size

    stack_rows(arrays, layout, scratch)
    out_ref[...] = dot(left_scr[...], scratch[...]).astype(BF16)


def down_grad(lefts, stages):
    arrays, layout = stage_arrays(stages)
    width = arrays[0].shape[1]
    units = lefts[0].shape[1]
    rows = sum(r.shape[0] for r in lefts)
    step = min(256, width)
    return pl.pallas_call(
        functools.partial(down_grad_kernel, len(arrays), layout),
        grid=(width // step,),
        in_specs=[pl.BlockSpec((p.shape[0], step), lambda i: (0, i)) for p in arrays]
        + [pl.BlockSpec(r.shape, lambda i: (0, 0)) for r in lefts],
        out_specs=pl.BlockSpec((units, step), lambda i: (0, i)),
        out_shape=jax.ShapeDtypeStruct((units, width), BF16),
        scratch_shapes=[pltpu.VMEM((units, rows), BF16), pltpu.VMEM((rows, step), BF16)],
        compiler_params=pltpu.CompilerParams(vmem_limit_bytes=VMEM),
        cost_estimate=COST,
        name="down_grad",
    )(*arrays, *lefts)


def place_kernel(index_ref, *refs):
    parts, outs = refs[:-2], refs[-2:]
    devices = len(parts) // 2
    for d in range(devices):
        @pl.when(pl.program_id(1) == d)
        def _(d=d):
            outs[0][...] = parts[d][...].astype(F32)
            outs[1][...] = parts[devices + d][...].astype(F32)


def place(parts, own, part):
    devices = len(parts)
    rows, mine = parts[0].shape[0], parts[0].shape[1] // 2
    blocks = mine // part
    if part % LANES:
        stack = jnp.stack(parts).reshape(devices, rows, 2, blocks, part)
        stack = jnp.stack([take(stack, own ^ d) for d in range(devices)])
        both = stack.transpose(2, 1, 3, 0, 4).reshape(2, rows, -1).astype(F32)
        return both[0], both[1]
    first = pl.BlockSpec((rows, part), lambda b, d, n: (0, b))
    second = pl.BlockSpec((rows, part), lambda b, d, n: (0, blocks + b))
    return pl.pallas_call(
        place_kernel,
        grid_spec=pltpu.PrefetchScalarGridSpec(
            num_scalar_prefetch=1,
            grid=(blocks, devices),
            in_specs=[first] * devices + [second] * devices,
            out_specs=[pl.BlockSpec((rows, part), lambda b, d, n: (0, b * devices + (n[0] ^ d)))] * 2,
        ),
        out_shape=[jax.ShapeDtypeStruct((rows, devices * mine), F32)] * 2,
        compiler_params=pltpu.CompilerParams(vmem_limit_bytes=VMEM),
        cost_estimate=COST,
        name="place",
    )(own.astype(jnp.int32).reshape(1), *parts, *parts)


X, Y, Z, C = "fo", "si", "zb", "fi"


def swap(values, axis, offset=1):
    size = lax.axis_size(axis)
    return lax.ppermute(values, axis, [(i, i ^ offset) for i in range(size)])


def swap_cube(values, offset):
    if len(offset) == 1:
        return swap(values, offset[0])
    sizes = [lax.axis_size(a) for a in offset]
    total = 1
    for size in sizes:
        total *= size
    pairs = []
    for i in range(total):
        rest, place = i, []
        for size in reversed(sizes):
            place.append(rest % size ^ 1)
            rest //= size
        j = 0
        for size, p in zip(sizes, reversed(place)):
            j = j * size + p
        pairs.append((i, j))
    return lax.ppermute(values, offset, pairs)


def sync(*values):
    leaves, tree = jax.tree.flatten(values)
    return jax.tree.unflatten(tree, lax.optimization_barrier(leaves))


STAGES = (((),), ((X,), (Y,), (Z,)), ((X, Z), (X, Y), (Z, Y), (X, Z, Y)))


def other_core(arrays):
    return swap(arrays[0] if len(arrays) == 1 else jnp.concatenate(arrays, axis=0), C)


def add_low(left, right):
    return (left.astype(F32) + right.astype(F32)).astype(BF16)


def send_home(stage, here, other):
    total = add_low(here, other)
    return [total[n] if not offset else swap_cube(total[n], offset) for n, offset in enumerate(STAGES[stage])]


def take(partial, block):
    return lax.dynamic_index_in_dim(partial, block, 0, keepdims=False)


def send_far(partial, za):
    return [swap(take(partial, za ^ k), "za", k) for k in range(1, lax.axis_size("za"))]


def add_far(partial, got, za):
    total = take(partial, za).astype(F32)
    for g in got:
        total = total + g.astype(F32)
    return total


def per_device(
    tokens, bounds, cotangent, attn_gain, query_weight, key_matrix, value_matrix,
    query_gain, key_gain, out_weight, ffn_gain, gate_weight, up_weight, down_weight,
):
    fsdp = ("fo", "fi")
    seq = ("za", "zb", "si")
    rows, width = tokens.shape
    f_count = lax.axis_size(fsdp)
    s_count = lax.axis_size(seq)
    far = lax.axis_size("za")
    f_index = lax.axis_index(fsdp)
    s_index = lax.axis_index(seq)
    za, zb, si = lax.axis_index("za"), lax.axis_index("zb"), lax.axis_index("si")
    length = rows * s_count
    heads = QUERY_HEADS // s_count
    copies = max(1, s_count // KEY_VALUE_HEADS)
    assert KEY_VALUE_HEADS * copies == s_count
    q_cols = heads * HEAD_SIZE
    cols = q_cols + 2 * HEAD_SIZE
    padded = -(-cols // LANES) * LANES
    all_q, all_kv = QUERY_HEADS * HEAD_SIZE, KEY_VALUE_HEADS * HEAD_SIZE

    pieces = [
        query_weight.reshape(-1, s_count, q_cols),
        jnp.repeat(key_matrix.reshape(-1, KEY_VALUE_HEADS, HEAD_SIZE), copies, axis=1),
        jnp.repeat(value_matrix.reshape(-1, KEY_VALUE_HEADS, HEAD_SIZE), copies, axis=1),
    ]
    kv_start = (s_index // copies) * HEAD_SIZE
    own_cols = [
        lax.dynamic_slice_in_dim(query_weight, s_index * q_cols, q_cols, 1),
        lax.dynamic_slice_in_dim(key_matrix, kv_start, HEAD_SIZE, 1),
        lax.dynamic_slice_in_dim(value_matrix, kv_start, HEAD_SIZE, 1),
    ]
    if padded > cols:
        pieces.append(jnp.zeros(pieces[0].shape[:2] + (padded - cols,), BF16))
        own_cols.append(jnp.zeros((query_weight.shape[0], padded - cols), BF16))
    w_own = lax.all_gather(jnp.concatenate(own_cols, axis=1), fsdp, axis=0, tiled=True)
    out_full = lax.all_gather(out_weight, fsdp, axis=0, tiled=True)
    w_rows = jnp.concatenate(pieces, axis=2).reshape(-1, s_count * padded)
    w_quarter = w_rows.shape[0] // 4
    w_parts = [w_rows[:w_quarter], w_rows[w_quarter:2 * w_quarter], w_rows[2 * w_quarter:]]

    far_list = [(k, swap(tokens, "za", k)) for k in range(1, far)]
    x_y, x_z, c_x = swap(tokens, Y), swap(tokens, Z), swap(cotangent, X)
    ids = jnp.arange(length, dtype=jnp.int32)
    b0, b1 = bounds[0, 0], bounds[0, 1]
    starts = jnp.where(ids >= b1, b1, jnp.where(ids >= b0, b0, 0))
    frequency = ROPE_BASE ** (-(jnp.arange(HEAD_SIZE // 2, dtype=F32) * 2.0 / HEAD_SIZE))
    phases = (ids - starts).astype(F32)[:, None] * frequency[None, :]
    cosine, sine = jnp.cos(phases), jnp.sin(phases)
    cos2 = jnp.concatenate([cosine] * 4, axis=1)
    sin2 = jnp.concatenate([-sine, sine] * 2, axis=1)
    head_gain = jnp.concatenate(
        [query_gain] * heads + [key_gain] + [jnp.ones((padded - cols + HEAD_SIZE,), F32)]
    )[None, :]
    far_list, x_y, x_z, c_x, w_rows, w_parts, cos2, sin2 = sync(
        [b for _, b in far_list], x_y, x_z, c_x, w_rows, w_parts, cos2, sin2
    )

    def some_project(blocks, held):
        index = jnp.stack([((za ^ k) * 2 + (zb ^ dz)) * 2 + (si ^ dy) for (k, dz, dy), _ in blocks])
        return project(
            heads, [b for _, b in blocks], index.astype(jnp.int32), bounds[0], attn_gain[None, :], w_own, head_gain,
            cos2, sin2, length, held,
        )

    far_y = [swap(b, Y) for b in far_list]
    far_z = [swap(b, Z) for b in far_list]
    held = some_project([((0, 0, 0), tokens), ((0, 0, 1), x_y), ((0, 1, 0), x_z)], None)
    far_y, far_z, held, x_y = sync(far_y, far_z, held, x_y)
    x_yz = swap(x_y, Z)
    far_yz = [swap(b, Y) for b in far_z]
    for n, k in enumerate(range(1, far)):
        held = some_project([((k, 0, 0), far_list[n]), ((k, 0, 1), far_y[n]), ((k, 1, 0), far_z[n])], held)
    w_c = swap(w_rows, C)
    c_own_other, c_x_other = swap(cotangent, C), swap(c_x, C)
    x_yz, far_yz, held, w_c, c_own_other, c_x_other, cot, c_x, w_parts = sync(
        x_yz, far_yz, held, w_c, c_own_other, c_x_other, cotangent, c_x, w_parts
    )
    c_y, c_z = swap(cot, Y), swap(cot, Z)
    w_x = [swap(w_parts[0], X)]
    mid = rows // 2
    c_xy, c_xz = [swap(c_x[:mid], Y)], [swap(c_x[:mid], Z)]
    held = some_project([((0, 1, 1), x_yz)] + [((k, 1, 1), far_yz[n]) for n, k in enumerate(range(1, far))], held)
    normed, q, k, v, unit, scale = held
    attended_low, attended, q2 = attend(heads, q, k, v)
    c_y, c_z, attended_low, c_x, c_xy, c_xz, w_x = sync(c_y, c_z, attended_low, c_x, c_xy, c_xz, w_x)
    heads_out = lax.all_to_all(attended_low, seq, split_axis=0, concat_axis=1, tiled=True)
    c_xyz = [swap(c_xy[0], Z)]
    c_xy.append(swap(c_y[mid:], X))
    c_xz.append(swap(c_z[mid:], X))
    c_yz = swap(c_z, Y)
    c_one = [c_x, c_y, c_z]
    c_one_other = [c_x_other, swap(c_y, C), swap(c_z, C)]
    heads_out, c_xz, c_xy, c_yz, c_xyz, c_one_other = sync(heads_out, c_xz, c_xy, c_yz, c_xyz, c_one_other)

    inputs = tokens.astype(F32)
    square_one = jnp.mean(inputs * inputs, axis=1, keepdims=True)
    scale_one = lax.rsqrt(square_one + EPSILON)
    residual = inputs + dot(heads_out, out_full)
    square_two = jnp.mean(residual * residual, axis=1, keepdims=True)
    scale_two = lax.rsqrt(square_two + EPSILON)
    inner = (residual * scale_two * ffn_gain).astype(BF16)
    c_xyz.append(swap(c_yz[mid:], X))
    c_two_other = [swap(c, C) for c in c_xz + c_xy]
    inner, c_xyz, c_two_other, c_yz = sync(inner, c_xyz, c_two_other, c_yz)

    units = gate_weight.shape[1]
    part = units // s_count
    mine = far * part
    own_block = zb * 2 + si
    if part % LANES == 0:
        weights = (gate_weight, up_weight, down_weight)
        unit_index = (jnp.arange(far, dtype=jnp.int32) * 4 + own_block).astype(jnp.int32)
        width_of_part = part
    else:
        pick = lambda w: lax.dynamic_index_in_dim(
            w.reshape(width, far, 4, part), own_block, 2, keepdims=False
        ).reshape(width, mine)
        weights = (
            pick(gate_weight),
            pick(up_weight),
            lax.dynamic_index_in_dim(
                down_weight.reshape(far, 4, part, width), own_block, 1, keepdims=False
            ).reshape(mine, width),
        )
        unit_index = jnp.zeros((1,), jnp.int32)
        width_of_part = mine
    run = lambda x_stage, c_stage: feed(x_stage, c_stage, unit_index, weights, width_of_part)
    x, y, z = swap(inner, X), swap(inner, Y), swap(inner, Z)
    c_two_other.append(swap(c_yz, C))
    x_stages = [([[inner]], [other_core([inner])])]
    c_stages = [([[cot]], [c_own_other])]
    fed = [run(x_stages[0], c_stages[0])]
    x, y, z, fed, inner, c_xyz, c_two_other = sync(x, y, z, fed, inner, c_xyz, c_two_other)
    c_two = [c_xz, c_xy, [c_yz], c_xyz]
    xy, xz, yz = swap(x, Y), swap(z, X), swap(y, Z)
    xyz = swap_cube(inner, (X, Z, Y))
    x_stages.append(([[x], [y], [z]], [other_core([x, y, z])]))
    c_stages.append(([[c] for c in c_one], c_one_other))
    c_two_other += [swap(c, C) for c in c_xyz]
    fed.append(run(x_stages[1], c_stages[1]))
    xy, xz, yz, xyz, fed, x_stages, w_parts, c_two, c_two_other = sync(
        xy, xz, yz, xyz, fed, x_stages, w_parts, c_two, c_two_other
    )
    x_stages.append(([[xz], [xy], [yz], [xyz]], [other_core([xz, xy, yz, xyz])]))
    c_stages.append((c_two, c_two_other))
    d_home = send_home(0, fed[0][0], swap(fed[0][1], C)) + send_home(1, fed[1][0], swap(fed[1][1], C))
    w_x.append(swap(w_parts[1], X))
    fed.append(run(x_stages[2], c_stages[2]))
    d_home, fed, x_stages, w_x = sync(d_home, fed, x_stages, w_x)
    far_xz, far_xy, far_yz, far_xyz = add_low(fed[2][0], swap(fed[2][1], C))
    hops = [swap(far_xyz, Y), swap(far_xy, X), swap(far_yz, Z)]
    down_part = down_grad([f[4] for f in fed], c_stages)
    far_xz, hops, d_home, down_part, fed = sync(far_xz, hops, d_home, down_part, fed)
    d_home += [swap_cube(add_low(far_xz, hops[0]), (X, Z)), swap(add_low(hops[1], hops[2]), Y)]
    m_other = [swap(f[3], C) for f in fed[:2]]
    gu_part = gate_grad(x_stages, [f[5] for f in fed])
    d_home, down_part, gu_part, fed, m_other, heads_out = sync(
        d_home, down_part, gu_part, fed, m_other, heads_out
    )
    gu_far = lax.psum_scatter(gu_part, "za", scatter_dimension=0, tiled=True)
    down_far = lax.psum_scatter(down_part, "za", scatter_dimension=0, tiled=True)
    quarter = width // far // 4

    def to_owners(values):
        spread = []
        for offset, axes in enumerate(((), (Y,), (Z,), (Z, Y))):
            block = lax.dynamic_slice_in_dim(values, (own_block ^ offset) * quarter, quarter, 0)
            spread.append(swap_cube(block, axes) if axes else block)
        return spread

    m_other.append(swap(fed[2][3], C))
    own_rows = out_weight.shape[0]
    left = []
    for offset in range(f_count):
        block = lax.dynamic_slice_in_dim(heads_out, (f_index ^ offset) * own_rows, own_rows, 1)
        left.append(swap(block, fsdp, offset) if offset else block)
    d_inner = sum(a.astype(F32) for a in d_home)
    ffn_part = jnp.sum(d_inner * residual * scale_two, axis=0)
    weighted = d_inner * ffn_gain
    d_residual = cotangent.astype(F32) + scale_two * (
        weighted - residual * scale_two * scale_two * jnp.mean(weighted * residual, axis=1, keepdims=True)
    )
    d_branch = d_residual.astype(BF16)
    d_heads = dot(d_branch, out_full, NT).astype(BF16)
    d_heads, d_branch, m_other, fed, left = sync(d_heads, d_branch, m_other, fed, left)
    d_attended = lax.all_to_all(d_heads, seq, split_axis=1, concat_axis=0, tiled=True)
    over = swap(d_branch, X)
    right = [d_branch, swap(d_branch, C), over, swap(over, C)]
    m = [add_low(f[2], other) for f, other in zip(fed[:2], m_other)]
    m.append([add_low(fed[2][2][n], m_other[2][n]) for n in range(4)])
    m_far = swap(m[2][3], Y)
    w_xc = [swap(jnp.concatenate(w_x, axis=0), C)]
    d_attended, right, m, m_far, w_parts, w_xc = sync(d_attended, right, m, m_far, w_parts, w_xc)
    w_x.append(swap(w_parts[2], X))
    out_part = dot(jnp.concatenate(left, axis=0), jnp.concatenate(right, axis=0), TN).astype(BF16)
    out_part = out_part.reshape(far, 2, 2, -1, width)
    pick = lambda values, index, axis: lax.dynamic_index_in_dim(values, index, axis, keepdims=False)
    out_y = swap(pick(out_part, 1 - si, 2), Y)
    d_qkv, gain_parts = attend_back(
        heads, q2, k, v, sync(d_attended, out_part)[0], attended, unit, scale, head_gain, cos2, sin2
    )
    d_qkv, gain_parts, m, m_far, w_x, w_xc, out_part, out_y = sync(
        d_qkv, gain_parts, m, m_far, w_x, w_xc, out_part, out_y
    )
    d_tok = lax.all_to_all(d_qkv, seq, split_axis=0, concat_axis=1, tiled=True)
    proj_part = dot(normed, d_qkv, TN).astype(BF16).reshape(2, 2, width // 4, padded)
    fi, fo = lax.axis_index(C), lax.axis_index(X)
    proj_core = add_low(pick(proj_part, fi, 1), swap(pick(proj_part, 1 - fi, 1), C))
    proj_x = swap(take(proj_core, 1 - fo), X)
    w_xc.append(swap(w_x[2], C))
    m_x, m_yz = swap(m[2][1], X), swap(m[2][2], Y)
    out_part = add_low(pick(out_part, si, 2), out_y)
    m_xz = add_low(m[2][0], m_far)
    d_tok, proj_core, proj_x, w_xc, out_part, m, m_x, m_yz, m_xz, gain_parts, gu_far = sync(
        d_tok, proj_core, proj_x, w_xc, out_part, m, m_x, m_yz, m_xz, gain_parts, gu_far
    )
    m_z = [swap(m_xz, X), m_yz]
    spread = to_owners(gu_far)
    blocks = [w_rows, w_c, jnp.concatenate(w_x, axis=0), jnp.concatenate(w_xc, axis=0)]
    by_offset = jnp.stack([dot(d_tok, w, NT) for w in blocks])
    d_normed = jnp.concatenate([take(by_offset, f_index ^ n) for n in range(f_count)], axis=1)
    weighted = d_normed * attn_gain
    input_grad = (
        d_residual
        + scale_one
        * (weighted - inputs * scale_one * scale_one * jnp.mean(weighted * inputs, axis=1, keepdims=True))
    ).astype(BF16)
    proj_rows = add_low(take(proj_core, fo), proj_x)
    gain_row = gain_parts[0]
    pack = jnp.concatenate(
        [
            ffn_part,
            gain_row[:q_cols].reshape(heads, HEAD_SIZE).sum(axis=0),
            gain_row[q_cols:q_cols + HEAD_SIZE],
        ]
    ).reshape(-1, LANES)
    for axis in ("fi", "fo", "si", "zb", "za"):
        offset = 1
        while offset < lax.axis_size(axis):
            pack = pack + swap(pack, axis, offset)
            offset *= 2
    pack = pack.reshape(-1)
    m_one = [m[1][0], add_low(m[1][1], m_x)]
    m_z, spread, input_grad, proj_rows, m, m_one, out_part, pack = sync(
        m_z, spread, input_grad, proj_rows, m, m_one, out_part, pack
    )
    proj = lax.all_to_all(proj_rows, seq, split_axis=0, concat_axis=1, tiled=True)
    m_last = [swap(m_one[0], X), swap(m_one[1], Y)]
    m_last.append(swap((m[1][2].astype(F32) + m_z[0].astype(F32) + m_z[1].astype(F32)).astype(BF16), Z))
    out_z = swap(pick(out_part, 1 - zb, 1), Z)
    gate_mine, up_mine = place(spread, own_block, part)
    proj, gate_mine, up_mine, m, m_last, out_part, out_z, down_far = sync(
        proj, gate_mine, up_mine, m, m_last, out_part, out_z, down_far
    )
    out_part = add_low(pick(out_part, zb, 1), out_z)
    out_got = send_far(out_part, za)
    down_mine = down_far.astype(F32)
    mlp_out = m[0][0].astype(F32) + sum(a.astype(F32) for a in m_last)
    block_output = (residual + mlp_out).astype(BF16)
    out_mine = add_far(out_part, out_got, za)
    proj = proj.astype(F32)
    count = proj.shape[0]
    by_device = proj.reshape(count, s_count, padded)

    def fold(values):
        return values.reshape(count, KEY_VALUE_HEADS, copies, HEAD_SIZE).sum(axis=2).reshape(count, -1)

    query_mine = by_device[:, :, :q_cols].reshape(count, QUERY_HEADS * HEAD_SIZE)
    key_mine = fold(by_device[:, :, q_cols:q_cols + HEAD_SIZE])
    value_mine = fold(by_device[:, :, q_cols + HEAD_SIZE:cols])

    my_w = lax.dynamic_slice_in_dim(w_rows, s_index * count, count, 0).astype(F32)
    my_gain = lax.dynamic_slice_in_dim(attn_gain, (f_index * s_count + s_index) * count, count, 0)
    attn_gain_mine = jnp.sum(my_w * proj, axis=1) / my_gain
    ffn_gain_mine = lax.dynamic_slice_in_dim(pack, (f_index * s_count + s_index) * count, count, 0)
    attn_rms = jnp.sqrt(square_one + EPSILON)[:, 0]
    mlp_rms = jnp.sqrt(square_two + EPSILON)[:, 0]
    return (
        block_output, input_grad, residual, attn_rms, mlp_rms, attn_gain_mine,
        query_mine, key_mine, value_mine, pack[width:width + HEAD_SIZE], pack[width + HEAD_SIZE:],
        out_mine, ffn_gain_mine, gate_mine, up_mine, down_mine,
    )


def solution(mesh):
    f_count, s_count = mesh.shape["fsdp"], mesh.shape["seq"]
    fine = Mesh(
        mesh.devices.reshape(f_count // 2, 2, s_count // 4, 2, 2), ("fo", "fi", "za", "zb", "si")
    )
    f, s = ("fo", "fi"), ("za", "zb", "si")
    every = P(f + s, None)
    vector = P(f + s)
    placed = (
        every, P(f, None), every, P(), P(f, None), P(f, None), P(f, None), P(), P(),
        P(f, None), P(), P(None, f), P(None, f), P(f, None),
    )
    return jax.shard_map(
        per_device,
        mesh=fine,
        in_specs=placed,
        out_specs=(
            every, every, every, vector, vector, vector, every, every, every, P(), P(),
            every, vector, P(s, f), P(s, f), every,
        ),
        check_vma=False,
    )
```
